32 devices in a mesh: tm: 2 (over y), chan: 16 (over z, x, core).
Axes of the slice: x: 2, y: 2, z: 4, core: 2. Of those that a mesh axis runs over, the one named last changes fastest.
Arguments:
- signal: bfloat16 [2048, 512], P('tm', 'chan'), may hold values from -6 to 6
- mel_frames: bfloat16 [2048, 80], P('tm'), may hold values from -6 to 6
- speaker_ids: int32 [16], P('tm'), may hold values from 0 to 943
- owners: int32 [320], replicated, may hold values from 0 to 15, as said below
- master: float32 [640, 8, 1024], P('chan'), may hold values from -0.25 to 0.25
- first_moment: float32 [640, 8, 1024], P('chan'), may hold values from -96 to 96
- second_moment: float32 [640, 8, 1024], P('chan'), may hold values from 122.88 to 2048
- res_cot: bfloat16 [2048, 512], P('tm', 'chan'), may hold values from -6 to 6
- skip_cot: bfloat16 [2048, 512], P('tm', 'chan'), may hold values from -6 to 6
Outputs:
- residual: float32 [2048, 512], P('tm', 'chan')
- skipped: float32 [2048, 512], P('tm', 'chan')
- grad_input: float32 [2048, 512], P('tm', 'chan')
- new_first: float32 [640, 8, 1024], P('chan')
- new_second: float32 [640, 8, 1024], P('chan')
- new_master: float32 [640, 8, 1024], P('chan')
The draws below stay inside these ranges and needn't reach their ends.
Inputs may be any that keep to these rules, and one draw needn't show every extreme that they name: Device d of chan owns the blocks b with owners[b] = d; no device owns more than 40 blocks, and one device owns exactly 40.
All inputs are finite; a program needn't handle non-finite values.
Results may differ from the reference program's by a relative error of at most 0.0055.
Values may be sent and summed in bfloat16 or wider, within the bound.
No kernel may reach another device: no remote copies, remote signals or barrier semaphores. Data moves between devices by JAX's collectives and lax.ppermute only.
A program may use at most 64 MiB of HBM per device.

```python
import math
import jax
import jax.numpy as jnp
import numpy as np
from jax import lax

RESID = 512
HIDDEN_SIZE = 512
MELS = 80
SPEAKERS = 944
DILATION = 8
SEG = 128
BLOCK = 8
STEP = 5
TOKENS = 2048
NSEG = 16
GATES = 1024
ROWS = 2560
NBLK = 320
MAXOWN = 40
SLOTS = 640
N_CHAN = 16


def draw_owners(key, part):
    key = jax.random.fold_in(key, 7)
    heavy_key, block_key, device_key = jax.random.split(key, 3)
    heavy = jax.random.randint(heavy_key, (), 0, N_CHAN)
    order = jax.random.permutation(block_key, NBLK)
    others = (heavy + 1 + jax.random.permutation(device_key, N_CHAN - 1)) % N_CHAN
    position = jnp.arange(NBLK)
    spread = others[jnp.maximum(position - MAXOWN, 0) % (N_CHAN - 1)]
    chosen = jnp.where(position < MAXOWN, heavy, spread).astype(jnp.int32)
    return jnp.zeros((NBLK,), jnp.int32).at[order].set(chosen)


def plant(entries, key, low, high):
    index_at = [jax.random.randint(jax.random.fold_in(key, axis), (), 0, length) for axis, length in enumerate(entries.shape)]
    longest = entries.shape.index(max(entries.shape))
    neighbour = index_at[:longest] + [(index_at[longest] + 1) % entries.shape[longest]] + index_at[longest + 1:]
    return entries.at[tuple(index_at)].set(low).at[tuple(neighbour)].set(high)


def block_levels(stream_key, extent, shards, least, high):
    def one(dim, shards_of):
        steps = jax.random.uniform(jax.random.fold_in(jax.random.fold_in(stream_key, 6), dim), (shards_of,), jnp.float32, least / len(shards), high / len(shards))
        return jnp.repeat(jnp.exp(steps), extent[dim] // shards_of).reshape((-1,) + (1,) * (len(extent) - dim - 1))

    gain = one(*shards[0])
    for cut in shards[1:]:
        gain = gain * one(*cut)
    return gain


def rank_table(number_of, lean):
    loads = [(1 << 20) // math.isqrt(standing ** lean) + 1 for standing in range(1, number_of + 1)]
    deviation = 1 + sum(loads) // (1 << 30)
    return np.cumsum(np.array([max(1, weight // deviation) for weight in loads]))


def ranked(stream_key, extent, number_of, skew):
    grid = rank_table(number_of, skew)
    pick = jax.random.randint(jax.random.fold_in(stream_key, 1), extent, 0, int(grid[number_of - 1]))
    rank = jnp.searchsorted(jnp.asarray(grid, jnp.int32), pick, side="right")
    return jax.random.permutation(jax.random.fold_in(stream_key, 2), number_of)[rank].astype(jnp.int32)


def centred(stream_key, extent, width, most, cuts=(), kind=jnp.bfloat16):
    result = width * jax.random.normal(stream_key, extent, jnp.float32)
    if cuts:
        result = result * block_levels(stream_key, extent, cuts, -0.22, 0.18)
    return jnp.clip(result, -most, most).astype(kind)


def setup_inputs(seed: int = 0) -> dict:
    splits = jax.random.split(jax.random.key(seed), 10)
    signal = centred(splits[0], (TOKENS, RESID), 1.0, 6.0, ((0, 2), (1, 16)))
    mel_frames = centred(splits[1], (TOKENS, MELS), 1.0, 6.0, ((0, 2),))
    speaker_ids = plant(ranked(splits[2], (NSEG,), SPEAKERS, 2), jax.random.fold_in(splits[2], 3), 0, SPEAKERS - 1).astype(jnp.int32)
    owners = draw_owners(jax.random.fold_in(splits[9], 71), 0)
    master = centred(splits[4], (SLOTS, BLOCK, GATES), RESID ** -0.5, 0.25, ((0, 16),), jnp.float32)
    first_moment = centred(splits[5], (SLOTS, BLOCK, GATES), (0.35 * TOKENS ** 0.5), 96.0, ((0, 16),), jnp.float32)
    second_moment = jnp.clip(jnp.exp(math.log(2048.0) - 2.8134107 * jax.random.uniform(splits[6], (SLOTS, BLOCK, GATES), jnp.float32) ** block_levels(splits[6], (SLOTS, BLOCK, GATES), ((0, 16),), -0.2, 0.2)), 122.88, 2048.0)
    res_cot = centred(splits[7], (TOKENS, RESID), 1.0, 6.0, ((0, 2), (1, 16)))
    skip_cot = centred(splits[8], (TOKENS, RESID), 1.0, 6.0, ((0, 2), (1, 16)))
    return {"signal": signal, "mel_frames": mel_frames, "speaker_ids": speaker_ids, "owners": owners, "master": master, "first_moment": first_moment, "second_moment": second_moment, "res_cot": res_cot, "skip_cot": skip_cot}


@jax.custom_vjp
def low(v):
    return lax.optimization_barrier(v.astype(jnp.bfloat16)).astype(jnp.float32)

@jax.custom_vjp
def low_back(v):
    return v

def low_keep(v):
    return (low(v), None)

def low_pass(kept, grad):
    return (grad,)

def back_keep(v):
    return (v, None)

def back_low(kept, grad):
    return (low(grad),)
low.defvjp(low_keep, low_pass)
low_back.defvjp(back_keep, back_low)
MOMENT_DECAY = 0.5
STEP_RATE = 0.03
WEIGHT_DECAY = 0.01
EPSILON = 1e-08

def place_index(owners):
    count = owners.shape[0]
    matches = owners[:, None] == owners[None, :]
    before = jnp.arange(count)[None, :] < jnp.arange(count)[:, None]
    ranks = lax.optimization_barrier(jnp.sum((matches & before).astype(jnp.int32), axis=1))
    return (owners * MAXOWN + ranks).astype(jnp.int32)

def matmul(left, right):
    return jnp.dot(left, right, preferred_element_type=jnp.float32, precision=lax.Precision.HIGHEST)

def layer_forward(params, inputs, mels, speaker_ids):
    weights = low(params)
    tap_prev = weights[:RESID]
    tap_now = weights[RESID:2 * RESID]
    mel_proj = weights[2 * RESID:2 * RESID + MELS]
    speaker_table = weights[2 * RESID + MELS:2 * RESID + MELS + SPEAKERS]
    out_weight = weights[2 * RESID + MELS + SPEAKERS:]
    shifted = jnp.concatenate([jnp.zeros((DILATION, RESID), jnp.float32), inputs[:-DILATION]], 0)
    pre_act = matmul(shifted, tap_prev) + matmul(inputs, tap_now) + matmul(mels, mel_proj)
    one_hot = (speaker_ids[:, None] == jnp.arange(SPEAKERS)[None, :]).astype(jnp.float32)
    embedded = matmul(one_hot, speaker_table)
    pre_act = (pre_act.reshape(NSEG, SEG, GATES) + embedded[:, None, :]).reshape(TOKENS, GATES)
    pre_act = low_back(pre_act)
    hidden = low(jnp.tanh(pre_act[:, 0::2]) * jax.nn.sigmoid(pre_act[:, 1::2]))
    paired = out_weight.reshape(RESID, HIDDEN_SIZE, 2)
    resid_part = matmul(hidden, paired[:, :, 0].T)
    skip_part = matmul(hidden, paired[:, :, 1].T)
    return (inputs + resid_part, skip_part)

def adamw(weights, first_old, second_old, grads, used):
    first_new = MOMENT_DECAY * first_old + (1.0 - MOMENT_DECAY) * grads
    second_new = MOMENT_DECAY * second_old + (1.0 - MOMENT_DECAY) * grads * grads
    first_hat = first_new / (1.0 - MOMENT_DECAY ** STEP)
    second_hat = second_new / (1.0 - MOMENT_DECAY ** STEP)
    stepped = weights - STEP_RATE * (first_hat / (jnp.sqrt(second_hat) + EPSILON) + WEIGHT_DECAY * weights)
    keep = used > 0.5
    return (jnp.where(keep, first_new, first_old), jnp.where(keep, second_new, second_old), jnp.where(keep, stepped, weights))

def reference(signal, mel_frames, speaker_ids, owners, master, first_moment, second_moment, res_cot, skip_cot):
    places = place_index(owners)
    params = master[places].reshape(ROWS, GATES)
    inputs = signal.astype(jnp.float32)
    mels = mel_frames.astype(jnp.float32)

    def forward(params_in, inputs_in):
        return layer_forward(params_in, inputs_in, mels, speaker_ids)
    (residual, skipped), pullback = jax.vjp(forward, params, inputs)
    grad_params, grad_input = pullback((res_cot.astype(jnp.float32), skip_cot.astype(jnp.float32)))
    grad_slots = jnp.zeros_like(master).at[places].set(grad_params.reshape(NBLK, BLOCK, GATES))
    used = jnp.zeros((SLOTS,), jnp.float32).at[places].set(1.0)[:, None, None]
    new_first, new_second, new_master = adamw(master, first_moment, second_moment, grad_slots, used)
    return (residual, skipped, grad_input, new_first, new_second, new_master)
```

```python
import functools

import jax
import jax.numpy as jnp
from jax import lax
from jax.experimental import pallas as pl
from jax.experimental.pallas import tpu as pltpu
from jax.sharding import PartitionSpec as P

RESID = 512
HIDDEN_SIZE = 512
MELS = 80
SPEAKERS = 944
DILATION = 8
SEG = 128
BLOCK = 8
STEP = 5
GATES = 1024
ROWS = 2560
NBLK = 320

MOMENT_DECAY = 0.5
STEP_RATE = 0.03
WEIGHT_DECAY = 0.01
EPSILON = 1e-08

F32 = jnp.float32
BF16 = jnp.bfloat16
NN = (((1,), (0,)), ((), ()))
NT = (((1,), (1,)), ((), ()))
TN = (((0,), (0,)), ((), ()))

TAPS = 2 * RESID // BLOCK
MEL_AT = TAPS
MEL_BLOCKS = MELS // BLOCK
SEG_AT = 144
OUT_AT = 160
PACKED = 224
SPK_BLOCK = TAPS + MEL_BLOCKS
OUT_BLOCK = SPK_BLOCK + SPEAKERS // BLOCK
PIECE = 112


def dot(a, b, dims=NN):
    return lax.dot_general(a, b, dims, preferred_element_type=F32)


def iota(shape, dim):
    return lax.broadcasted_iota(jnp.int32, shape, dim)


def onehot(cond):
    return jnp.where(cond, 1.0, 0.0).astype(BF16)


def call(kernel, out, n_smem, n_in, flops=0, mbytes=1, scratch=()):
    return pl.pallas_call(
        kernel,
        out_shape=out,
        in_specs=[pl.BlockSpec(memory_space=pltpu.SMEM)] * n_smem
        + [pl.BlockSpec(memory_space=pltpu.VMEM)] * n_in,
        out_specs=jax.tree.map(lambda _: pl.BlockSpec(memory_space=pltpu.VMEM), out),
        scratch_shapes=list(scratch),
        compiler_params=pltpu.CompilerParams(vmem_limit_bytes=48 * 2**20),
        cost_estimate=pl.CostEstimate(
            flops=flops, bytes_accessed=int(mbytes * 2**20), transcendentals=0
        ),
    )


def gate_order(dim):
    natural, split = iota((256, 256), dim), iota((256, 256), 1 - dim)
    return onehot(natural == 2 * (split & 127) + (split >> 7))


def pack_weights(ids, master, out):
    half = ids[0]
    slots = master.shape[0]
    rows = 4 * slots
    here = iota((rows, 8 * slots), 0)
    there = iota((rows, 8 * slots), 1)
    row, slot = jnp.zeros_like(here), here
    for step in range(1, 4):
        past = here >= step * slots
        row = jnp.where(past, step, row)
        slot = jnp.where(past, here - step * slots, slot)
    pick = onehot(there == 8 * slot + 4 * half + row)
    flat = master[...].reshape(8 * slots, GATES).astype(BF16)
    got = dot(pick, flat)
    for z in range(4):
        for j in range(4):
            out[4 * z + j] = got[j * slots : (j + 1) * slots, 256 * z : 256 * (z + 1)].astype(BF16)


def pack_tokens(ids, sig, res, skp, halo, o0, o1, o2, o3):
    j = ids[1] & 3
    ends = []
    outs = (o0, o1, o2, o3)
    for k in range(4):
        to = j ^ k
        cut = pl.ds(pl.multiple_of(to * 256, 256), 256)
        for n, part in enumerate((sig, res, skp)):
            outs[k][32 * n : 32 * n + 32, :] = part[:, cut]
        before = sig[:, pl.ds(pl.multiple_of(jnp.maximum(to * 256 - 128, 0), 128), 128)]
        ends.append(jnp.where(to == 0, halo[...].astype(F32), before.astype(F32)))
    tails = jnp.concatenate(ends, 0).astype(BF16)
    last = onehot(iota((16, 128), 1) == iota((16, 128), 0) + 112)
    rows = dot(last, tails, NT)
    lane = iota((16, 128), 1)
    for k in range(4):
        outs[k][96:112, 0:128] = jnp.where((lane >> 5) == k, rows, 0.0).astype(BF16)
        outs[k][96:112, 128:256] = jnp.zeros((16, 128), BF16)


def place_blocks(sid, owners, pick, put, *, slots_dev):
    own_row = owners[...]
    down, across = iota((NBLK, NBLK), 0), iota((NBLK, NBLK), 1)
    row_all = jnp.broadcast_to(own_row, (NBLK, NBLK))
    own_col = jnp.sum(jnp.where(down == across, row_all, 0), axis=1, keepdims=True)
    before = (own_col == row_all) & (down < across)
    rank = jnp.sum(jnp.where(before, 1, 0), axis=0, keepdims=True)
    place = own_row * slots_dev + rank
    n = iota((PACKED, 1), 0)
    spk = jnp.zeros((PACKED, 1), jnp.int32)
    for s in range(16):
        spk = jnp.where(n == SEG_AT + s, sid[s] >> 3, spk)
    blk = jnp.where(
        n < SPK_BLOCK,
        n,
        jnp.where(n < SEG_AT, -1, jnp.where(n < OUT_AT, SPK_BLOCK + spk, n + (OUT_BLOCK - OUT_AT))),
    )
    match = jnp.broadcast_to(blk, (PACKED, NBLK)) == iota((PACKED, NBLK), 1)
    at = jnp.sum(jnp.where(match, jnp.broadcast_to(place, (PACKED, NBLK)), 0), axis=1, keepdims=True)
    at = jnp.where(blk < 0, -1, at)
    slots = pick.shape[1]
    pick[...] = onehot(jnp.broadcast_to(at, (PACKED, slots)) == iota((PACKED, slots), 1))
    same = iota((PACKED, PACKED), 0) == iota((PACKED, PACKED), 1)
    at_row = jnp.sum(jnp.where(same, jnp.broadcast_to(at, (PACKED, PACKED)), 0), axis=0, keepdims=True)
    put[...] = onehot(jnp.broadcast_to(at_row, (slots, PACKED)) == iota((slots, PACKED), 0))


def gather_blocks(pick, slots, out):
    got = dot(pick[...], slots[...]).astype(BF16)
    got = dot(got, gate_order(0)).astype(BF16)
    for n in range(8):
        out[n] = got


def scatter_blocks(put, parts, out):
    total = parts[0].astype(F32)
    for n in range(1, 8):
        total = total + parts[n].astype(F32)
    natural = dot(total.astype(BF16), gate_order(1)).astype(BF16)
    spread = dot(put[...], natural).astype(BF16)
    out[0] = spread
    out[1] = spread


def channel_of(pos, ch):
    return ((pos >> 5) ^ ch) * 32 + (pos & 31)


def layer(ids, packed, p0, p1, p2, p3, mel, grads, z0, z1, z2, z3, feat):
    half, ch = ids[0], ids[1]
    j = ch & 3
    got = (p0, p1, p2, p3)
    sq = (RESID, RESID)

    def order(dim):
        major = iota(sq, dim)
        return onehot(channel_of(iota(sq, 1 - dim), ch) == 8 * (major & 63) + (major >> 6))

    to_major = order(0)
    to_place = order(1)
    tokens = 256

    def stacked(n):
        return jnp.concatenate(
            [got[k][i, 32 * n : 32 * n + 32, :] for k in range(4) for i in range(4)], 0
        )

    sig = dot(to_major, stacked(0))
    res = dot(to_major, stacked(1)).astype(BF16)
    skp = dot(to_major, stacked(2)).astype(BF16)
    ends = []
    for k in range(4):
        end = got[k][0, 96:112, 0:128].astype(F32)
        for i in range(1, 4):
            end = end + got[k][i, 96:112, 0:128].astype(F32)
        ends.append(end)
    halo = jnp.concatenate([jnp.zeros((112, RESID), F32), jnp.concatenate(ends, 1)], 0).astype(BF16)
    halo = pltpu.roll(dot(to_major, halo, NT), DILATION, 1)
    moved = pltpu.roll(sig, DILATION, 1)
    first = iota((RESID, 128), 1) < DILATION
    shifted = jnp.concatenate([jnp.where(first, halo, moved[:, :128]), moved[:, 128:]], 1).astype(BF16)
    sig = sig.astype(BF16)
    m = iota((128, MELS), 0)
    mel_pick = onehot(((m & 15) < MEL_BLOCKS) & (iota((128, MELS), 1) == 8 * (m & 15) + (m >> 4)))
    mels = dot(mel_pick, mel[:, pl.ds(pl.multiple_of(j * tokens, tokens), tokens)]).astype(BF16)
    seg_row = iota((16, tokens), 0)
    seg_of = 8 * half + 2 * j + (iota((16, tokens), 1) >> 7)
    sub = jnp.where(iota((16, tokens), 1) < SEG, ids[2 + 2 * j] & 7, ids[3 + 2 * j] & 7)
    for r in range(8):
        feat[r, 0:64] = shifted[64 * r : 64 * r + 64]
        feat[r, 64:128] = sig[64 * r : 64 * r + 64]
        feat[r, 128:144] = mels[16 * r : 16 * r + 16]
        feat[r, 144:160] = onehot((seg_row == seg_of) & (sub == r))
    features = feat[...].reshape(8 * OUT_AT, tokens)
    conv = packed[:, 0:OUT_AT, :].reshape(8 * OUT_AT, 256)
    pre = dot(conv, features, TN)
    filt = jnp.tanh(pre[:128])
    gate = jax.nn.sigmoid(pre[128:])
    hidden = (filt * gate).astype(BF16)
    out_res = packed[:, OUT_AT:PACKED, 0:128].reshape(RESID, 128)
    out_skp = packed[:, OUT_AT:PACKED, 128:256].reshape(RESID, 128)
    res_part = dot(out_res, hidden).astype(BF16)
    skp_part = dot(out_skp, hidden).astype(BF16)
    grad_hidden = dot(out_res, res, TN) + dot(out_skp, skp, TN)
    grad_pre = jnp.concatenate(
        [
            grad_hidden * gate * (1.0 - filt * filt),
            grad_hidden * filt * gate * (1.0 - gate),
        ],
        0,
    ).astype(BF16)
    prev = packed[:, 0:64, :].reshape(RESID, 256)
    now = packed[:, 64:128, :].reshape(RESID, 256)
    later = dot(prev, grad_pre)
    kept = iota((RESID, tokens), 1) < tokens - DILATION
    in_part = dot(now, grad_pre) + jnp.where(kept, pltpu.roll(later, tokens - DILATION, 1), 0.0)
    conv_grad = dot(features, grad_pre, NT).astype(BF16)
    res_grad = dot(res, hidden, NT).astype(BF16)
    skp_grad = dot(skp, hidden, NT).astype(BF16)
    grads[:, 0:OUT_AT, :] = conv_grad.reshape(8, OUT_AT, 256)
    grads[:, OUT_AT:PACKED, 0:128] = res_grad.reshape(8, 64, 128)
    grads[:, OUT_AT:PACKED, 128:256] = skp_grad.reshape(8, 64, 128)
    res_part = dot(to_place, res_part).astype(BF16)
    skp_part = dot(to_place, skp_part).astype(BF16)
    in_part = dot(to_place, in_part.astype(BF16)).astype(BF16)
    early = dot(to_place, later[:, :128].astype(BF16)).astype(BF16)
    head = onehot(iota((16, 128), 0) == iota((16, 128), 1))
    early = dot(head, early, NT).astype(BF16)
    outs = (z0, z1, z2, z3)
    for k in range(4):
        for i in range(4):
            at = 128 * k + 32 * i
            outs[k][i, 0:32] = res_part[at : at + 32]
            outs[k][i, 32:64] = skp_part[at : at + 32]
            outs[k][i, 64:96] = in_part[at : at + 32]
            outs[k][i, 96:112, 0:128] = early[:, 128 * k : 128 * k + 128]
            outs[k][i, 96:112, 128:256] = jnp.zeros((16, 128), BF16)


def sum_units(z0, z1, z2, z3, o0, o1, o2, o3):
    for i, out in enumerate((o0, o1, o2, o3)):
        out[...] = (
            z0[i].astype(F32) + z1[i].astype(F32) + z2[i].astype(F32) + z3[i].astype(F32)
        ).astype(BF16)


def late_tail(rows, k):
    lane = onehot(iota((32, 128), 1) == 32 * k + iota((32, 128), 0))
    chans = dot(lane, rows, NT).astype(BF16)
    t = iota((16, 128), 0)
    return dot(chans, onehot((t < DILATION) & (iota((16, 128), 1) == 120 + t)))


def edge(ids, o0, o1, o2, o3, out):
    j = ids[1] & 3
    total = jnp.zeros((32, 128), F32)
    for k, piece in enumerate((o0, o1, o2, o3)):
        total = total + jnp.where(j == k, late_tail(piece[96:112, 0:128], k), 0.0)
    out[...] = total.astype(BF16)


def finish_tokens(ids, o0, o1, o2, o3, ahead, sig, res, residual, skipped, grad_in):
    j = ids[1] & 3
    pieces = (o0, o1, o2, o3)
    for k, piece in enumerate(pieces):
        cut = pl.ds(pl.multiple_of((j ^ k) * 256, 256), 256)
        residual[:, cut] = sig[:, cut].astype(F32) + piece[0:32, :].astype(F32)
        skipped[:, cut] = piece[32:64, :].astype(F32)
        grad_in[:, cut] = res[:, cut].astype(F32) + piece[64:96, :].astype(F32)
    for k, piece in enumerate(pieces):
        tail = late_tail(piece[96:112, 0:128], k)
        start = (j ^ k) * 256 - 128

        @pl.when(start >= 0)
        def _():
            cut = pl.ds(pl.multiple_of(start, 128), 128)
            grad_in[:, cut] = grad_in[:, cut] + tail

    grad_in[:, 896:1024] = grad_in[:, 896:1024] + ahead[...].astype(F32)


def update(ids, owners, grads, master, first, second, new_first, new_second, new_master):
    slots = grads.shape[1]
    owned = jnp.sum(jnp.where(owners[...] == ids[1], 1, 0))
    keep = iota((8 * slots, 1), 0) < 8 * owned
    spread = []
    for r in range(8):
        spread.append(onehot(iota((8 * slots, slots), 0) == 8 * iota((8 * slots, slots), 1) + r))
    for z in range(4):
        cut = slice(256 * z, 256 * z + 256)
        grad = dot(spread[0], grads[4 * z])
        for r in range(1, 8):
            grad = grad + dot(spread[r], grads[16 * (r // 4) + 4 * z + r % 4])
        old_m = master[:, cut]
        old_f = first[:, cut]
        old_s = second[:, cut]
        first_new = MOMENT_DECAY * old_f + (1.0 - MOMENT_DECAY) * grad
        second_new = MOMENT_DECAY * old_s + (1.0 - MOMENT_DECAY) * grad * grad
        first_hat = first_new / (1.0 - MOMENT_DECAY**STEP)
        second_hat = second_new / (1.0 - MOMENT_DECAY**STEP)
        stepped = old_m - STEP_RATE * (
            first_hat / (jnp.sqrt(second_hat) + EPSILON) + WEIGHT_DECAY * old_m
        )
        new_first[:, cut] = jnp.where(keep, first_new, old_f)
        new_second[:, cut] = jnp.where(keep, second_new, old_s)
        new_master[:, cut] = jnp.where(keep, stepped, old_m)


BOTH = ("tm", "chan")


def swap(x, k):
    n = lax.axis_size("chan")
    return lax.ppermute(x, "chan", [(i, i ^ k) for i in range(n)])


def local(
    signal, mel_frames, speaker_ids, owners, master, first_moment, second_moment, res_cot, skip_cot
):
    slots_dev = master.shape[0]
    slots = 16 * slots_dev
    half = lax.axis_index("tm")
    ids = jnp.concatenate([jnp.stack([half, lax.axis_index("chan")]).astype(jnp.int32), speaker_ids])
    sig, res, skp, mel = signal.T, res_cot.T, skip_cot.T, mel_frames.T
    own_row = owners.reshape(1, NBLK)
    share = [[16 * y + 4 * z + j for y in range(2) for j in range(4)] for z in range(4)]
    sds = jax.ShapeDtypeStruct

    halo = lax.ppermute(sig[:, -128:], "tm", [(0, 1)])
    other_ids = lax.ppermute(speaker_ids, "tm", [(0, 1), (1, 0)])
    sids = jnp.where(
        half == 0,
        jnp.concatenate([speaker_ids, other_ids]),
        jnp.concatenate([other_ids, speaker_ids]),
    )

    sent = call(pack_weights, sds((16, slots_dev, 256), BF16), 1, 1)(ids, master)
    arrived = lax.all_to_all(sent, "chan", 0, 0, tiled=True)
    piece = sds((PIECE, 256), BF16)
    o = call(pack_tokens, (piece,) * 4, 1, 4)(ids, sig, res, skp, halo)
    mine = jnp.stack([o[0], swap(o[1], 1), swap(o[2], 2), swap(o[3], 3)])
    p1, p2, p3 = (swap(mine, 4 * k) for k in (1, 2, 3))

    pick, put = call(
        functools.partial(place_blocks, slots_dev=slots_dev),
        (sds((PACKED, slots), BF16), sds((slots, PACKED), BF16)),
        1,
        1,
    )(sids, own_row)
    gathered = call(gather_blocks, sds((8, PACKED, 256), BF16), 0, 2)(
        pick, arrived.reshape(slots, 256)
    )
    packed = lax.all_to_all(gathered, BOTH, 0, 0, axis_index_groups=share)

    quad = sds((4, PIECE, 256), BF16)
    grads, z0, z1, z2, z3 = call(
        layer,
        (sds((8, PACKED, 256), BF16), quad, quad, quad, quad),
        1,
        6,
        scratch=(pltpu.VMEM((8, OUT_AT, 256), BF16),),
    )(ids, packed, mine, p1, p2, p3, mel)

    parts = lax.all_to_all(grads, BOTH, 0, 0, axis_index_groups=share)
    t1, t2, t3 = (swap(z, 4 * k) for k, z in ((1, z1), (2, z2), (3, z3)))
    o = call(sum_units, (piece,) * 4, 0, 4)(z0, t1, t2, t3)
    o = (o[0], swap(o[1], 1), swap(o[2], 2), swap(o[3], 3))
    spread = call(scatter_blocks, sds((2, slots, 256), BF16), 0, 2)(put, parts)
    returned = lax.all_to_all(spread.reshape(32, slots_dev, 256), BOTH, 0, 0)
    tail = call(edge, sds((32, 128), BF16), 1, 4)(ids, *o)
    ahead = lax.ppermute(tail, "tm", [(1, 0)])
    narrow = sds(sig.shape, F32)
    residual, skipped, grad_in = call(finish_tokens, (narrow,) * 3, 1, 7)(
        ids, *o, ahead, sig, res
    )
    flat = (8 * slots_dev, GATES)
    new = call(update, (sds(flat, F32),) * 3, 1, 5)(
        ids,
        own_row,
        returned,
        master.reshape(flat),
        first_moment.reshape(flat),
        second_moment.reshape(flat),
    )
    return (residual.T, skipped.T, grad_in.T, *(x.reshape(master.shape) for x in new))


def place_index(owners, slots_dev):
    count = owners.shape[0]
    matches = owners[:, None] == owners[None, :]
    before = jnp.arange(count)[None, :] < jnp.arange(count)[:, None]
    ranks = jnp.sum((matches & before).astype(jnp.int32), axis=1)
    return owners * slots_dev + ranks


def local_plain(
    signal, mel_frames, speaker_ids, owners, master, first_moment, second_moment, res_cot, skip_cot
):
    chans = lax.axis_size("chan")
    slots_dev = master.shape[0]
    tok_count = signal.shape[0]
    hid_local = HIDDEN_SIZE // chans
    col_count = GATES // chans
    seg_count = speaker_ids.shape[0]
    spk_start = 2 * RESID + MELS
    out_start = spk_start + SPEAKERS
    places = place_index(owners, slots_dev)
    table = places[:, None] == jnp.arange(chans * slots_dev)[None, :]
    received = lax.all_to_all(
        master.astype(BF16), "chan", split_axis=2, concat_axis=0, tiled=True
    ).reshape(chans * slots_dev, BLOCK * col_count)
    params = jnp.dot(table.astype(BF16), received, preferred_element_type=F32)
    params = params.astype(BF16).reshape(ROWS, col_count)
    tap_prev, tap_now = params[:RESID], params[RESID : 2 * RESID]
    mel_proj = params[2 * RESID : spk_start]
    speaker_table = params[spk_start:out_start]
    out_cols = params[out_start:].reshape(RESID, hid_local, 2)
    n_tm = lax.axis_size("tm")
    tail_prev = lax.ppermute(signal[-DILATION:], "tm", [(i, i + 1) for i in range(n_tm - 1)])
    inputs = lax.all_gather(signal, "chan", axis=1, tiled=True)
    tail_full = lax.all_gather(tail_prev, "chan", axis=1, tiled=True)
    shifted = jnp.concatenate([tail_full, inputs[:-DILATION]], 0)
    pre_act = jnp.dot(shifted, tap_prev, preferred_element_type=F32)
    pre_act = pre_act + jnp.dot(inputs, tap_now, preferred_element_type=F32)
    pre_act = pre_act + jnp.dot(mel_frames, mel_proj, preferred_element_type=F32)
    one_hot = (speaker_ids[:, None] == jnp.arange(SPEAKERS)[None, :]).astype(BF16)
    embedded = jnp.dot(one_hot, speaker_table, preferred_element_type=F32)
    pre_act = (pre_act.reshape(seg_count, SEG, col_count) + embedded[:, None, :]).reshape(
        tok_count, col_count
    )
    filt = jnp.tanh(pre_act[:, 0::2])
    gates = jax.nn.sigmoid(pre_act[:, 1::2])
    hidden = (filt * gates).astype(BF16)
    summed = lax.psum_scatter(
        jnp.einsum("cuw,tu->cwt", out_cols, hidden, preferred_element_type=F32),
        "chan",
        scatter_dimension=0,
        tiled=True,
    )
    cots = lax.all_gather(
        jnp.stack([res_cot.T, skip_cot.T], axis=1), "chan", axis=0, tiled=True
    )
    grad_hid = jnp.einsum("cwt,cuw->tu", cots, out_cols, preferred_element_type=F32)
    term = jnp.einsum("cwt,tu->cuw", cots, hidden, preferred_element_type=F32)
    grad_filt = grad_hid * gates * (1.0 - filt * filt)
    grad_gate = grad_hid * filt * gates * (1.0 - gates)
    grad_pre = (
        jnp.stack([grad_filt, grad_gate], axis=2).reshape(tok_count, col_count).astype(BF16)
    )
    ahead = lax.ppermute(grad_pre[:DILATION], "tm", [(i + 1, i) for i in range(n_tm - 1)])
    later = jnp.concatenate([grad_pre[DILATION:], ahead], 0)
    input_part = lax.psum_scatter(
        dot(tap_now, grad_pre, NT) + dot(tap_prev, later, NT),
        "chan",
        scatter_dimension=0,
        tiled=True,
    )
    seg_sums = jnp.sum(grad_pre.astype(F32).reshape(seg_count, SEG, col_count), axis=1)
    grad_spk = lax.dot_general(
        one_hot.astype(F32),
        seg_sums,
        TN,
        precision=lax.Precision.HIGHEST,
        preferred_element_type=F32,
    )
    grad_params = jnp.concatenate(
        [
            dot(shifted, grad_pre, TN),
            dot(inputs, grad_pre, TN),
            dot(mel_frames, grad_pre, TN),
            grad_spk,
            term.reshape(RESID, col_count),
        ],
        0,
    )
    grad_params = lax.psum(grad_params, "tm").reshape(NBLK, BLOCK * col_count)
    outgoing = lax.dot_general(
        table.astype(F32), grad_params, TN, precision=lax.Precision.HIGHEST
    ).reshape(chans * slots_dev, BLOCK, col_count)
    grad_slots = lax.all_to_all(outgoing, "chan", split_axis=0, concat_axis=2, tiled=True)
    owned = jnp.sum((owners == lax.axis_index("chan")).astype(jnp.int32))
    keep = (jnp.arange(slots_dev) < owned)[:, None, None]
    first_new = MOMENT_DECAY * first_moment + (1.0 - MOMENT_DECAY) * grad_slots
    second_new = MOMENT_DECAY * second_moment + (1.0 - MOMENT_DECAY) * grad_slots * grad_slots
    first_hat = first_new / (1.0 - MOMENT_DECAY**STEP)
    second_hat = second_new / (1.0 - MOMENT_DECAY**STEP)
    stepped = master - STEP_RATE * (
        first_hat / (jnp.sqrt(second_hat) + EPSILON) + WEIGHT_DECAY * master
    )
    return (
        signal.astype(F32) + summed[:, 0, :].T,
        summed[:, 1, :].T,
        res_cot.astype(F32) + input_part.T,
        jnp.where(keep, first_new, first_moment),
        jnp.where(keep, second_new, second_moment),
        jnp.where(keep, stepped, master),
    )


def solution(mesh):
    wide = P("tm", "chan")
    slots = P("chan", None, None)
    packed_mesh = mesh.shape["tm"] == 2 and mesh.shape["chan"] == 16
    return jax.shard_map(
        local if packed_mesh else local_plain,
        mesh=mesh,
        in_specs=(wide, P("tm", None), P("tm"), P(), slots, slots, slots, wide, wide),
        out_specs=(wide, wide, wide, slots, slots, slots),
        check_vma=False,
    )
```

```python
import functools

import jax
import jax.numpy as jnp
from jax import lax
from jax.experimental import pallas as pl
from jax.experimental.pallas import tpu as pltpu
from jax.sharding import PartitionSpec as P

RESID = 512
HIDDEN_SIZE = 512
MELS = 80
SPEAKERS = 944
DILATION = 8
SEG = 128
BLOCK = 8
STEP = 5
GATES = 1024
ROWS = 2560
NBLK = 320

MOMENT_DECAY = 0.5
STEP_RATE = 0.03
WEIGHT_DECAY = 0.01
EPSILON = 1e-08

F32 = jnp.float32
BF16 = jnp.bfloat16
NN = (((1,), (0,)), ((), ()))
NT = (((1,), (1,)), ((), ()))
TN = (((0,), (0,)), ((), ()))

TAPS = 2 * RESID // BLOCK
MEL_AT = TAPS
MEL_BLOCKS = MELS // BLOCK
SEG_AT = 144
OUT_AT = 160
PACKED = 224
SPK_BLOCK = TAPS + MEL_BLOCKS
OUT_BLOCK = SPK_BLOCK + SPEAKERS // BLOCK
PIECE = 112


def dot(a, b, dims=NN):
    return lax.dot_general(a, b, dims, preferred_element_type=F32)


def iota(shape, dim):
    return lax.broadcasted_iota(jnp.int32, shape, dim)


def onehot(cond):
    return jnp.where(cond, 1.0, 0.0).astype(BF16)


def call(kernel, out, n_smem, n_in, flops=0, mbytes=1, scratch=()):
    return pl.pallas_call(
        kernel,
        out_shape=out,
        in_specs=[pl.BlockSpec(memory_space=pltpu.SMEM)] * n_smem
        + [pl.BlockSpec(memory_space=pltpu.VMEM)] * n_in,
        out_specs=jax.tree.map(lambda _: pl.BlockSpec(memory_space=pltpu.VMEM), out),
        scratch_shapes=list(scratch),
        compiler_params=pltpu.CompilerParams(vmem_limit_bytes=24 * 2**20),
        cost_estimate=pl.CostEstimate(
            flops=flops, bytes_accessed=int(mbytes * 2**20), transcendentals=0
        ),
    )


def gate_order(dim):
    natural, split = iota((256, 256), dim), iota((256, 256), 1 - dim)
    return onehot(natural == 2 * (split & 127) + (split >> 7))


def pack_weights(ids, master, out):
    half = ids[0]
    slots = master.shape[0]
    rows = 4 * slots
    here = iota((rows, 8 * slots), 0)
    there = iota((rows, 8 * slots), 1)
    row, slot = jnp.zeros_like(here), here
    for step in range(1, 4):
        past = here >= step * slots
        row = jnp.where(past, step, row)
        slot = jnp.where(past, here - step * slots, slot)
    pick = onehot(there == 8 * slot + 4 * half + row)
    flat = master[...].reshape(8 * slots, GATES).astype(BF16)
    got = dot(pick, flat)
    for z in range(4):
        for j in range(4):
            out[4 * z + j] = got[j * slots : (j + 1) * slots, 256 * z : 256 * (z + 1)].astype(BF16)


def pack_tokens(ids, sig, res, skp, halo, o0, o1, o2, o3):
    j = ids[1] & 3
    ends = []
    outs = (o0, o1, o2, o3)
    for k in range(4):
        to = j ^ k
        cut = pl.ds(pl.multiple_of(to * 256, 256), 256)
        for n, part in enumerate((sig, res, skp)):
            outs[k][32 * n : 32 * n + 32, :] = part[:, cut]
        before = sig[:, pl.ds(pl.multiple_of(jnp.maximum(to * 256 - 128, 0), 128), 128)]
        ends.append(jnp.where(to == 0, halo[...].astype(F32), before.astype(F32)))
    tails = jnp.concatenate(ends, 0).astype(BF16)
    last = onehot(iota((16, 128), 1) == iota((16, 128), 0) + 112)
    rows = dot(last, tails, NT)
    lane = iota((16, 128), 1)
    for k in range(4):
        outs[k][96:112, 0:128] = jnp.where((lane >> 5) == k, rows, 0.0).astype(BF16)
        outs[k][96:112, 128:256] = jnp.zeros((16, 128), BF16)


def place_blocks(sid, owners, pick, put, *, slots_dev):
    own_row = owners[...]
    down, across = iota((NBLK, NBLK), 0), iota((NBLK, NBLK), 1)
    row_all = jnp.broadcast_to(own_row, (NBLK, NBLK))
    own_col = jnp.sum(jnp.where(down == across, row_all, 0), axis=1, keepdims=True)
    before = (own_col == row_all) & (down < across)
    rank = jnp.sum(jnp.where(before, 1, 0), axis=0, keepdims=True)
    place = own_row * slots_dev + rank
    n = iota((PACKED, 1), 0)
    spk = jnp.zeros((PACKED, 1), jnp.int32)
    for s in range(16):
        spk = jnp.where(n == SEG_AT + s, sid[s] >> 3, spk)
    blk = jnp.where(
        n < SPK_BLOCK,
        n,
        jnp.where(n < SEG_AT, -1, jnp.where(n < OUT_AT, SPK_BLOCK + spk, n + (OUT_BLOCK - OUT_AT))),
    )
    match = jnp.broadcast_to(blk, (PACKED, NBLK)) == iota((PACKED, NBLK), 1)
    at = jnp.sum(jnp.where(match, jnp.broadcast_to(place, (PACKED, NBLK)), 0), axis=1, keepdims=True)
    at = jnp.where(blk < 0, -1, at)
    slots = pick.shape[1]
    pick[...] = onehot(jnp.broadcast_to(at, (PACKED, slots)) == iota((PACKED, slots), 1))
    same = iota((PACKED, PACKED), 0) == iota((PACKED, PACKED), 1)
    at_row = jnp.sum(jnp.where(same, jnp.broadcast_to(at, (PACKED, PACKED)), 0), axis=0, keepdims=True)
    put[...] = onehot(jnp.broadcast_to(at_row, (slots, PACKED)) == iota((slots, PACKED), 0))


def gather_blocks(pick, slots, out):
    got = dot(pick[...], slots[...]).astype(BF16)
    got = dot(got, gate_order(0)).astype(BF16)
    for n in range(8):
        out[n] = got


def scatter_blocks(put, parts, out):
    total = parts[0].astype(F32)
    for n in range(1, 8):
        total = total + parts[n].astype(F32)
    natural = dot(total.astype(BF16), gate_order(1)).astype(BF16)
    spread = dot(put[...], natural).astype(BF16)
    out[0] = spread
    out[1] = spread


def channel_of(pos, ch):
    return ((pos >> 5) ^ ch) * 32 + (pos & 31)


def layer(ids, packed, p0, p1, p2, p3, mel, grads, z0, z1, z2, z3, feat):
    half, ch = ids[0], ids[1]
    j = ch & 3
    got = (p0, p1, p2, p3)
    sq = (RESID, RESID)

    def order(dim):
        major = iota(sq, dim)
        return onehot(channel_of(iota(sq, 1 - dim), ch) == 8 * (major & 63) + (major >> 6))

    to_major = order(0)
    to_place = order(1)
    tokens = 256

    def stacked(n):
        return jnp.concatenate(
            [got[k][i, 32 * n : 32 * n + 32, :] for k in range(4) for i in range(4)], 0
        )

    sig = dot(to_major, stacked(0))
    res = dot(to_major, stacked(1)).astype(BF16)
    skp = dot(to_major, stacked(2)).astype(BF16)
    ends = []
    for k in range(4):
        end = got[k][0, 96:112, 0:128].astype(F32)
        for i in range(1, 4):
            end = end + got[k][i, 96:112, 0:128].astype(F32)
        ends.append(end)
    halo = jnp.concatenate([jnp.zeros((112, RESID), F32), jnp.concatenate(ends, 1)], 0).astype(BF16)
    halo = pltpu.roll(dot(to_major, halo, NT), DILATION, 1)
    moved = pltpu.roll(sig, DILATION, 1)
    first = iota((RESID, 128), 1) < DILATION
    shifted = jnp.concatenate([jnp.where(first, halo, moved[:, :128]), moved[:, 128:]], 1).astype(BF16)
    sig = sig.astype(BF16)
    m = iota((128, MELS), 0)
    mel_pick = onehot(((m & 15) < MEL_BLOCKS) & (iota((128, MELS), 1) == 8 * (m & 15) + (m >> 4)))
    mels = dot(mel_pick, mel[:, pl.ds(pl.multiple_of(j * tokens, tokens), tokens)]).astype(BF16)
    seg_row = iota((16, tokens), 0)
    seg_of = 8 * half + 2 * j + (iota((16, tokens), 1) >> 7)
    sub = jnp.where(iota((16, tokens), 1) < SEG, ids[2 + 2 * j] & 7, ids[3 + 2 * j] & 7)
    for r in range(8):
        feat[r, 0:64] = shifted[64 * r : 64 * r + 64]
        feat[r, 64:128] = sig[64 * r : 64 * r + 64]
        feat[r, 128:144] = mels[16 * r : 16 * r + 16]
        feat[r, 144:160] = onehot((seg_row == seg_of) & (sub == r))
    features = feat[...].reshape(8 * OUT_AT, tokens)
    conv = packed[:, 0:OUT_AT, :].reshape(8 * OUT_AT, 256)
    pre = dot(conv, features, TN)
    filt = jnp.tanh(pre[:128])
    gate = jax.nn.sigmoid(pre[128:])
    hidden = (filt * gate).astype(BF16)
    out_res = packed[:, OUT_AT:PACKED, 0:128].reshape(RESID, 128)
    out_skp = packed[:, OUT_AT:PACKED, 128:256].reshape(RESID, 128)
    res_part = dot(out_res, hidden).astype(BF16)
    skp_part = dot(out_skp, hidden).astype(BF16)
    grad_hidden = dot(out_res, res, TN) + dot(out_skp, skp, TN)
    grad_pre = jnp.concatenate(
        [
            grad_hidden * gate * (1.0 - filt * filt),
            grad_hidden * filt * gate * (1.0 - gate),
        ],
        0,
    ).astype(BF16)
    prev = packed[:, 0:64, :].reshape(RESID, 256)
    now = packed[:, 64:128, :].reshape(RESID, 256)
    later = dot(prev, grad_pre)
    kept = iota((RESID, tokens), 1) < tokens - DILATION
    in_part = dot(now, grad_pre) + jnp.where(kept, pltpu.roll(later, tokens - DILATION, 1), 0.0)
    conv_grad = dot(features, grad_pre, NT).astype(BF16)
    res_grad = dot(res, hidden, NT).astype(BF16)
    skp_grad = dot(skp, hidden, NT).astype(BF16)
    grads[:, 0:OUT_AT, :] = conv_grad.reshape(8, OUT_AT, 256)
    grads[:, OUT_AT:PACKED, 0:128] = res_grad.reshape(8, 64, 128)
    grads[:, OUT_AT:PACKED, 128:256] = skp_grad.reshape(8, 64, 128)
    res_part = dot(to_place, res_part).astype(BF16)
    skp_part = dot(to_place, skp_part).astype(BF16)
    in_part = dot(to_place, in_part.astype(BF16)).astype(BF16)
    early = dot(to_place, later[:, :128].astype(BF16)).astype(BF16)
    head = onehot(iota((16, 128), 0) == iota((16, 128), 1))
    early = dot(head, early, NT).astype(BF16)
    outs = (z0, z1, z2, z3)
    for k in range(4):
        for i in range(4):
            at = 128 * k + 32 * i
            outs[k][i, 0:32] = res_part[at : at + 32]
            outs[k][i, 32:64] = skp_part[at : at + 32]
            outs[k][i, 64:96] = in_part[at : at + 32]
            outs[k][i, 96:112, 0:128] = early[:, 128 * k : 128 * k + 128]
            outs[k][i, 96:112, 128:256] = jnp.zeros((16, 128), BF16)


def sum_units(z0, z1, z2, z3, o0, o1, o2, o3):
    for i, out in enumerate((o0, o1, o2, o3)):
        out[...] = (
            z0[i].astype(F32) + z1[i].astype(F32) + z2[i].astype(F32) + z3[i].astype(F32)
        ).astype(BF16)


def late_tail(rows, k):
    lane = onehot(iota((32, 128), 1) == 32 * k + iota((32, 128), 0))
    chans = dot(lane, rows, NT).astype(BF16)
    t = iota((16, 128), 0)
    return dot(chans, onehot((t < DILATION) & (iota((16, 128), 1) == 120 + t)))


def edge(ids, o0, o1, o2, o3, out):
    j = ids[1] & 3
    total = jnp.zeros((32, 128), F32)
    for k, piece in enumerate((o0, o1, o2, o3)):
        total = total + jnp.where(j == k, late_tail(piece[96:112, 0:128], k), 0.0)
    out[...] = total.astype(BF16)


def finish_tokens(ids, o0, o1, o2, o3, ahead, sig, res, residual, skipped, grad_in):
    j = ids[1] & 3
    pieces = (o0, o1, o2, o3)
    for k, piece in enumerate(pieces):
        cut = pl.ds(pl.multiple_of((j ^ k) * 256, 256), 256)
        residual[:, cut] = sig[:, cut].astype(F32) + piece[0:32, :].astype(F32)
        skipped[:, cut] = piece[32:64, :].astype(F32)
        grad_in[:, cut] = res[:, cut].astype(F32) + piece[64:96, :].astype(F32)
    for k, piece in enumerate(pieces):
        tail = late_tail(piece[96:112, 0:128], k)
        start = (j ^ k) * 256 - 128

        @pl.when(start >= 0)
        def _():
            cut = pl.ds(pl.multiple_of(start, 128), 128)
            grad_in[:, cut] = grad_in[:, cut] + tail

    grad_in[:, 896:1024] = grad_in[:, 896:1024] + ahead[...].astype(F32)


def update(ids, owners, grads, master, first, second, new_first, new_second, new_master):
    slots = grads.shape[1]
    owned = jnp.sum(jnp.where(owners[...] == ids[1], 1, 0))
    keep = iota((8 * slots, 1), 0) < 8 * owned
    spread = []
    for r in range(8):
        spread.append(onehot(iota((8 * slots, slots), 0) == 8 * iota((8 * slots, slots), 1) + r))
    for z in range(4):
        cut = slice(256 * z, 256 * z + 256)
        grad = dot(spread[0], grads[4 * z])
        for r in range(1, 8):
            grad = grad + dot(spread[r], grads[16 * (r // 4) + 4 * z + r % 4])
        old_m = master[:, cut]
        old_f = first[:, cut]
        old_s = second[:, cut]
        first_new = MOMENT_DECAY * old_f + (1.0 - MOMENT_DECAY) * grad
        second_new = MOMENT_DECAY * old_s + (1.0 - MOMENT_DECAY) * grad * grad
        first_hat = first_new / (1.0 - MOMENT_DECAY**STEP)
        second_hat = second_new / (1.0 - MOMENT_DECAY**STEP)
        stepped = old_m - STEP_RATE * (
            first_hat / (jnp.sqrt(second_hat) + EPSILON) + WEIGHT_DECAY * old_m
        )
        new_first[:, cut] = jnp.where(keep, first_new, old_f)
        new_second[:, cut] = jnp.where(keep, second_new, old_s)
        new_master[:, cut] = jnp.where(keep, stepped, old_m)


BOTH = ("tm", "chan")


def swap(x, k):
    n = lax.axis_size("chan")
    return lax.ppermute(x, "chan", [(i, i ^ k) for i in range(n)])


def local(
    signal, mel_frames, speaker_ids, owners, master, first_moment, second_moment, res_cot, skip_cot
):
    slots_dev = master.shape[0]
    slots = 16 * slots_dev
    half = lax.axis_index("tm")
    ids = jnp.concatenate([jnp.stack([half, lax.axis_index("chan")]).astype(jnp.int32), speaker_ids])
    sig, res, skp, mel = signal.T, res_cot.T, skip_cot.T, mel_frames.T
    own_row = owners.reshape(1, NBLK)
    share = [[16 * y + 4 * z + j for y in range(2) for j in range(4)] for z in range(4)]
    sds = jax.ShapeDtypeStruct

    halo = lax.ppermute(sig[:, -128:], "tm", [(0, 1)])
    other_ids = lax.ppermute(speaker_ids, "tm", [(0, 1), (1, 0)])
    sids = jnp.where(
        half == 0,
        jnp.concatenate([speaker_ids, other_ids]),
        jnp.concatenate([other_ids, speaker_ids]),
    )

    sent = call(pack_weights, sds((16, slots_dev, 256), BF16), 1, 1)(ids, master)
    arrived = lax.all_to_all(sent, "chan", 0, 0, tiled=True)
    piece = sds((PIECE, 256), BF16)
    o = call(pack_tokens, (piece,) * 4, 1, 4)(ids, sig, res, skp, halo)
    mine = jnp.stack([o[0], swap(o[1], 1), swap(o[2], 2), swap(o[3], 3)])
    p1, p2, p3 = (swap(mine, 4 * k) for k in (1, 2, 3))

    pick, put = call(
        functools.partial(place_blocks, slots_dev=slots_dev),
        (sds((PACKED, slots), BF16), sds((slots, PACKED), BF16)),
        1,
        1,
    )(sids, own_row)
    arrived, _ = lax.optimization_barrier((arrived, mine))
    gathered = call(gather_blocks, sds((8, PACKED, 256), BF16), 0, 2)(
        pick, arrived.reshape(slots, 256)
    )
    packed = lax.all_to_all(gathered, BOTH, 0, 0, axis_index_groups=share)

    quad = sds((4, PIECE, 256), BF16)
    grads, z0, z1, z2, z3 = call(
        layer,
        (sds((8, PACKED, 256), BF16), quad, quad, quad, quad),
        1,
        6,
        scratch=(pltpu.VMEM((8, OUT_AT, 256), BF16),),
    )(ids, packed, mine, p1, p2, p3, mel)

    parts = lax.all_to_all(grads, BOTH, 0, 0, axis_index_groups=share)
    t1, t2, t3 = (swap(z, 4 * k) for k, z in ((1, z1), (2, z2), (3, z3)))
    o = call(sum_units, (piece,) * 4, 0, 4)(z0, t1, t2, t3)
    parts, _ = lax.optimization_barrier((parts, o[0]))
    o = (o[0], swap(o[1], 1), swap(o[2], 2), swap(o[3], 3))
    spread = call(scatter_blocks, sds((2, slots, 256), BF16), 0, 2)(put, parts)
    returned = lax.all_to_all(spread.reshape(32, slots_dev, 256), BOTH, 0, 0)
    tail = call(edge, sds((32, 128), BF16), 1, 4)(ids, *o)
    ahead = lax.ppermute(tail, "tm", [(1, 0)])
    narrow = sds(sig.shape, F32)
    residual, skipped, grad_in = call(finish_tokens, (narrow,) * 3, 1, 7)(
        ids, *o, ahead, sig, res
    )
    flat = (8 * slots_dev, GATES)
    new = call(update, (sds(flat, F32),) * 3, 1, 5)(
        ids,
        own_row,
        returned,
        master.reshape(flat),
        first_moment.reshape(flat),
        second_moment.reshape(flat),
    )
    return (residual.T, skipped.T, grad_in.T, *(x.reshape(master.shape) for x in new))


def place_index(owners, slots_dev):
    count = owners.shape[0]
    matches = owners[:, None] == owners[None, :]
    before = jnp.arange(count)[None, :] < jnp.arange(count)[:, None]
    ranks = jnp.sum((matches & before).astype(jnp.int32), axis=1)
    return owners * slots_dev + ranks


def local_plain(
    signal, mel_frames, speaker_ids, owners, master, first_moment, second_moment, res_cot, skip_cot
):
    chans = lax.axis_size("chan")
    slots_dev = master.shape[0]
    tok_count = signal.shape[0]
    hid_local = HIDDEN_SIZE // chans
    col_count = GATES // chans
    seg_count = speaker_ids.shape[0]
    spk_start = 2 * RESID + MELS
    out_start = spk_start + SPEAKERS
    places = place_index(owners, slots_dev)
    table = places[:, None] == jnp.arange(chans * slots_dev)[None, :]
    received = lax.all_to_all(
        master.astype(BF16), "chan", split_axis=2, concat_axis=0, tiled=True
    ).reshape(chans * slots_dev, BLOCK * col_count)
    params = jnp.dot(table.astype(BF16), received, preferred_element_type=F32)
    params = params.astype(BF16).reshape(ROWS, col_count)
    tap_prev, tap_now = params[:RESID], params[RESID : 2 * RESID]
    mel_proj = params[2 * RESID : spk_start]
    speaker_table = params[spk_start:out_start]
    out_cols = params[out_start:].reshape(RESID, hid_local, 2)
    n_tm = lax.axis_size("tm")
    tail_prev = lax.ppermute(signal[-DILATION:], "tm", [(i, i + 1) for i in range(n_tm - 1)])
    inputs = lax.all_gather(signal, "chan", axis=1, tiled=True)
    tail_full = lax.all_gather(tail_prev, "chan", axis=1, tiled=True)
    shifted = jnp.concatenate([tail_full, inputs[:-DILATION]], 0)
    pre_act = jnp.dot(shifted, tap_prev, preferred_element_type=F32)
    pre_act = pre_act + jnp.dot(inputs, tap_now, preferred_element_type=F32)
    pre_act = pre_act + jnp.dot(mel_frames, mel_proj, preferred_element_type=F32)
    one_hot = (speaker_ids[:, None] == jnp.arange(SPEAKERS)[None, :]).astype(BF16)
    embedded = jnp.dot(one_hot, speaker_table, preferred_element_type=F32)
    pre_act = (pre_act.reshape(seg_count, SEG, col_count) + embedded[:, None, :]).reshape(
        tok_count, col_count
    )
    filt = jnp.tanh(pre_act[:, 0::2])
    gates = jax.nn.sigmoid(pre_act[:, 1::2])
    hidden = (filt * gates).astype(BF16)
    summed = lax.psum_scatter(
        jnp.einsum("cuw,tu->cwt", out_cols, hidden, preferred_element_type=F32),
        "chan",
        scatter_dimension=0,
        tiled=True,
    )
    cots = lax.all_gather(
        jnp.stack([res_cot.T, skip_cot.T], axis=1), "chan", axis=0, tiled=True
    )
    grad_hid = jnp.einsum("cwt,cuw->tu", cots, out_cols, preferred_element_type=F32)
    term = jnp.einsum("cwt,tu->cuw", cots, hidden, preferred_element_type=F32)
    grad_filt = grad_hid * gates * (1.0 - filt * filt)
    grad_gate = grad_hid * filt * gates * (1.0 - gates)
    grad_pre = (
        jnp.stack([grad_filt, grad_gate], axis=2).reshape(tok_count, col_count).astype(BF16)
    )
    ahead = lax.ppermute(grad_pre[:DILATION], "tm", [(i + 1, i) for i in range(n_tm - 1)])
    later = jnp.concatenate([grad_pre[DILATION:], ahead], 0)
    input_part = lax.psum_scatter(
        dot(tap_now, grad_pre, NT) + dot(tap_prev, later, NT),
        "chan",
        scatter_dimension=0,
        tiled=True,
    )
    seg_sums = jnp.sum(grad_pre.astype(F32).reshape(seg_count, SEG, col_count), axis=1)
    grad_spk = lax.dot_general(
        one_hot.astype(F32),
        seg_sums,
        TN,
        precision=lax.Precision.HIGHEST,
        preferred_element_type=F32,
    )
    grad_params = jnp.concatenate(
        [
            dot(shifted, grad_pre, TN),
            dot(inputs, grad_pre, TN),
            dot(mel_frames, grad_pre, TN),
            grad_spk,
            term.reshape(RESID, col_count),
        ],
        0,
    )
    grad_params = lax.psum(grad_params, "tm").reshape(NBLK, BLOCK * col_count)
    outgoing = lax.dot_general(
        table.astype(F32), grad_params, TN, precision=lax.Precision.HIGHEST
    ).reshape(chans * slots_dev, BLOCK, col_count)
    grad_slots = lax.all_to_all(outgoing, "chan", split_axis=0, concat_axis=2, tiled=True)
    owned = jnp.sum((owners == lax.axis_index("chan")).astype(jnp.int32))
    keep = (jnp.arange(slots_dev) < owned)[:, None, None]
    first_new = MOMENT_DECAY * first_moment + (1.0 - MOMENT_DECAY) * grad_slots
    second_new = MOMENT_DECAY * second_moment + (1.0 - MOMENT_DECAY) * grad_slots * grad_slots
    first_hat = first_new / (1.0 - MOMENT_DECAY**STEP)
    second_hat = second_new / (1.0 - MOMENT_DECAY**STEP)
    stepped = master - STEP_RATE * (
        first_hat / (jnp.sqrt(second_hat) + EPSILON) + WEIGHT_DECAY * master
    )
    return (
        signal.astype(F32) + summed[:, 0, :].T,
        summed[:, 1, :].T,
        res_cot.astype(F32) + input_part.T,
        jnp.where(keep, first_new, first_moment),
        jnp.where(keep, second_new, second_moment),
        jnp.where(keep, stepped, master),
    )


def solution(mesh):
    wide = P("tm", "chan")
    slots = P("chan", None, None)
    packed_mesh = mesh.shape["tm"] == 2 and mesh.shape["chan"] == 16
    return jax.shard_map(
        local if packed_mesh else local_plain,
        mesh=mesh,
        in_specs=(wide, P("tm", None), P("tm"), P(), slots, slots, slots, wide, wide),
        out_specs=(wide, wide, wide, slots, slots, slots),
        check_vma=False,
    )
```

```python
import functools

import jax
import jax.numpy as jnp
from jax import lax
from jax.experimental import pallas as pl
from jax.experimental.pallas import tpu as pltpu
from jax.sharding import PartitionSpec as P

RESID = 512
HIDDEN_SIZE = 512
MELS = 80
SPEAKERS = 944
DILATION = 8
SEG = 128
BLOCK = 8
STEP = 5
GATES = 1024
ROWS = 2560
NBLK = 320

MOMENT_DECAY = 0.5
STEP_RATE = 0.03
WEIGHT_DECAY = 0.01
EPSILON = 1e-08

F32 = jnp.float32
BF16 = jnp.bfloat16
NN = (((1,), (0,)), ((), ()))
NT = (((1,), (1,)), ((), ()))
TN = (((0,), (0,)), ((), ()))

TAPS = 2 * RESID // BLOCK
MEL_AT = TAPS
MEL_BLOCKS = MELS // BLOCK
SEG_AT = 144
OUT_AT = 160
PACKED = 224
SPK_BLOCK = TAPS + MEL_BLOCKS
OUT_BLOCK = SPK_BLOCK + SPEAKERS // BLOCK
PIECE = 112


def dot(a, b, dims=NN):
    return lax.dot_general(a, b, dims, preferred_element_type=F32)


def iota(shape, dim):
    return lax.broadcasted_iota(jnp.int32, shape, dim)


def onehot(cond):
    return jnp.where(cond, 1.0, 0.0).astype(BF16)


def call(kernel, out, n_smem, n_in, flops=0, mbytes=1, scratch=(), out_space=pltpu.VMEM):
    return pl.pallas_call(
        kernel,
        out_shape=out,
        in_specs=[pl.BlockSpec(memory_space=pltpu.SMEM)] * n_smem
        + [pl.BlockSpec(memory_space=pltpu.VMEM)] * n_in,
        out_specs=jax.tree.map(lambda _: pl.BlockSpec(memory_space=out_space), out),
        scratch_shapes=list(scratch),
        compiler_params=pltpu.CompilerParams(vmem_limit_bytes=24 * 2**20),
        cost_estimate=pl.CostEstimate(
            flops=flops, bytes_accessed=int(mbytes * 2**20), transcendentals=0
        ),
    )


def gate_order(dim):
    natural, split = iota((256, 256), dim), iota((256, 256), 1 - dim)
    return onehot(natural == 2 * (split & 127) + (split >> 7))


def pack_weights(ids, master, out):
    half = ids[0]
    slots = master.shape[0]
    rows = 4 * slots
    here = iota((rows, 8 * slots), 0)
    there = iota((rows, 8 * slots), 1)
    row, slot = jnp.zeros_like(here), here
    for step in range(1, 4):
        past = here >= step * slots
        row = jnp.where(past, step, row)
        slot = jnp.where(past, here - step * slots, slot)
    pick = onehot(there == 8 * slot + 4 * half + row)
    flat = master[...].reshape(8 * slots, GATES).astype(BF16)
    got = dot(pick, flat)
    for z in range(4):
        for j in range(4):
            out[4 * z + j] = got[j * slots : (j + 1) * slots, 256 * z : 256 * (z + 1)].astype(BF16)


def edge_tiles(ids, sig, res, skp, mel, out):
    cut = pl.ds(pl.multiple_of((1 - ids[0]) * 896, 128), 128)
    for n, part in enumerate((sig, res, skp)):
        out[32 * n : 32 * n + 32, :] = part[:, cut]
    out[96:176, :] = mel[:, cut]


def pack_tokens(ids, sig, res, skp, other, o0, o1, o2, o3):
    half, j = ids[0], ids[1] & 3
    outs = (o0, o1, o2, o3)
    parts = (sig, res, skp)
    befores, nexts = [], ([], [], [])
    for k in range(4):
        to = j ^ k
        cut = pl.ds(pl.multiple_of(to * 256, 256), 256)
        for n, part in enumerate(parts):
            outs[k][32 * n : 32 * n + 32, :] = part[:, cut]
        cut = pl.ds(pl.multiple_of(jnp.maximum(to * 256 - 128, 0), 128), 128)
        edge = jnp.where(half == 1, other[0:32, :].astype(F32), 0.0)
        befores.append(jnp.where(to == 0, edge, sig[:, cut].astype(F32)))
        cut = pl.ds(pl.multiple_of(jnp.minimum(to * 256 + 256, 896), 128), 128)
        for n, part in enumerate(parts):
            edge = jnp.where(half == 0, other[32 * n : 32 * n + 32, :].astype(F32), 0.0)
            nexts[n].append(jnp.where(to == 3, edge, part[:, cut].astype(F32)))
    tall = [jnp.concatenate(x, 0).astype(BF16) for x in (befores, *nexts)]
    t, lane = iota((16, 128), 0), iota((16, 128), 1)
    top, low = t < DILATION, t >= DILATION
    head_top = onehot(top & (lane == t))
    head_low = onehot(low & (lane == t - DILATION))
    last_top = onehot(top & (lane == t + 120))
    rows = (
        dot(last_top, tall[0], NT) + dot(head_low, tall[1], NT),
        dot(head_top, tall[2], NT) + dot(head_low, tall[3], NT),
    )
    for k in range(4):
        for n in range(2):
            outs[k][96:112, 128 * n : 128 * n + 128] = jnp.where(
                (lane >> 5) == k, rows[n], 0.0
            ).astype(BF16)


def place_blocks(sid, owners, pick, put, *, slots_dev):
    own_row = owners[...]
    down, across = iota((NBLK, NBLK), 0), iota((NBLK, NBLK), 1)
    row_all = jnp.broadcast_to(own_row, (NBLK, NBLK))
    own_col = jnp.sum(jnp.where(down == across, row_all, 0), axis=1, keepdims=True)
    before = (own_col == row_all) & (down < across)
    rank = jnp.sum(jnp.where(before, 1, 0), axis=0, keepdims=True)
    place = own_row * slots_dev + rank
    n = iota((PACKED, 1), 0)
    spk = jnp.zeros((PACKED, 1), jnp.int32)
    for s in range(16):
        spk = jnp.where(n == SEG_AT + s, sid[2 + s] >> 3, spk)
    blk = jnp.where(
        n < SPK_BLOCK,
        n,
        jnp.where(n < SEG_AT, -1, jnp.where(n < OUT_AT, SPK_BLOCK + spk, n + (OUT_BLOCK - OUT_AT))),
    )
    match = jnp.broadcast_to(blk, (PACKED, NBLK)) == iota((PACKED, NBLK), 1)
    at = jnp.sum(jnp.where(match, jnp.broadcast_to(place, (PACKED, NBLK)), 0), axis=1, keepdims=True)
    at = jnp.where(blk < 0, -1, at)
    slots = pick.shape[1]
    pick[...] = onehot(jnp.broadcast_to(at, (PACKED, slots)) == iota((PACKED, slots), 1))
    same = iota((PACKED, PACKED), 0) == iota((PACKED, PACKED), 1)
    at_row = jnp.sum(jnp.where(same, jnp.broadcast_to(at, (PACKED, PACKED)), 0), axis=0, keepdims=True)
    put[...] = onehot(jnp.broadcast_to(at_row, (slots, PACKED)) == iota((slots, PACKED), 0))


def gather_blocks(pick, slots, out):
    got = dot(pick[...], slots[...]).astype(BF16)
    got = dot(got, gate_order(0)).astype(BF16)
    for n in range(8):
        out[n] = got


def scatter_blocks(put, parts, out):
    total = parts[0].astype(F32)
    for n in range(1, 8):
        total = total + parts[n].astype(F32)
    natural = dot(total.astype(BF16), gate_order(1)).astype(BF16)
    spread = dot(put[...], natural).astype(BF16)
    out[0] = spread
    out[1] = spread


def channel_of(pos, ch):
    return ((pos >> 5) ^ ch) * 32 + (pos & 31)


def layer(ids, packed, p0, p1, p2, p3, mel, other, grads, z0, z1, z2, z3, feat):
    half, ch = ids[0], ids[1]
    j = ch & 3
    got = (p0, p1, p2, p3)
    sq = (RESID, RESID)
    tokens, wide = 256, 384

    def order(dim):
        major = iota(sq, dim)
        return onehot(channel_of(iota(sq, 1 - dim), ch) == 8 * (major & 63) + (major >> 6))

    to_major = order(0)
    to_place = order(1)

    def stacked(n):
        return jnp.concatenate(
            [got[k][i, 32 * n : 32 * n + 32, :] for k in range(4) for i in range(4)], 0
        )

    ends = []
    for k in range(4):
        end = got[k][0, 96:112, :].astype(F32)
        for i in range(1, 4):
            end = end + got[k][i, 96:112, :].astype(F32)
        ends.append(end)
    ends = [jnp.concatenate([e[:, 128 * n : 128 * n + 128] for e in ends], 1) for n in range(2)]
    gap = jnp.zeros((120, RESID), F32)
    ends = jnp.concatenate(
        [ends[0][8:16], gap[:112], ends[0][0:8], ends[1][0:8], gap, ends[1][8:16], gap], 0
    ).astype(BF16)
    ends = dot(to_major, ends, NT)
    sig = jnp.concatenate([dot(to_major, stacked(0)), ends[:, 0:128]], 1)
    res = jnp.concatenate([dot(to_major, stacked(1)), ends[:, 128:256]], 1).astype(BF16)
    skp = jnp.concatenate([dot(to_major, stacked(2)), ends[:, 256:384]], 1).astype(BF16)
    shifted = pltpu.roll(sig, DILATION, 1).astype(BF16)
    sig = sig.astype(BF16)
    m = iota((128, MELS), 0)
    mel_pick = onehot(((m & 15) < MEL_BLOCKS) & (iota((128, MELS), 1) == 8 * (m & 15) + (m >> 4)))
    cut = pl.ds(pl.multiple_of(j * tokens, tokens), tokens)
    far = pl.ds(pl.multiple_of(jnp.minimum(j * tokens + tokens, 896), 128), 128)
    ahead = jnp.where(j == 3, other[96:176, :].astype(F32), mel[:, far].astype(F32)).astype(BF16)
    mels = jnp.concatenate([dot(mel_pick, mel[:, cut]), dot(mel_pick, ahead)], 1).astype(BF16)
    seg = 8 * half + 2 * j
    row, lane = iota((16, wide), 0), iota((16, wide), 1)
    sub = jnp.where(
        lane < SEG,
        ids[2 + seg] & 7,
        jnp.where(lane < 2 * SEG, ids[3 + seg] & 7, ids[2 + jnp.minimum(seg + 2, 15)] & 7),
    )
    for r in range(8):
        feat[r, 0:64] = shifted[64 * r : 64 * r + 64]
        feat[r, 64:128] = sig[64 * r : 64 * r + 64]
        feat[r, 128:144] = mels[16 * r : 16 * r + 16]
        feat[r, 144:160] = onehot((row == seg + (lane >> 7)) & (sub == r))
    features = feat[...].reshape(8 * OUT_AT, wide)
    conv = packed[:, 0:OUT_AT, :].reshape(8 * OUT_AT, 256)
    pre = dot(conv, features, TN)
    filt = jnp.tanh(pre[:128])
    gate = jax.nn.sigmoid(pre[128:])
    hidden = (filt[:, :tokens] * gate[:, :tokens]).astype(BF16)
    out_res = packed[:, OUT_AT:PACKED, 0:128].reshape(RESID, 128)
    out_skp = packed[:, OUT_AT:PACKED, 128:256].reshape(RESID, 128)
    res_part = dot(out_res, hidden).astype(BF16)
    skp_part = dot(out_skp, hidden).astype(BF16)
    grad_hidden = dot(out_res, res, TN) + dot(out_skp, skp, TN)
    grad_pre = jnp.concatenate(
        [
            grad_hidden * gate * (1.0 - filt * filt),
            grad_hidden * filt * gate * (1.0 - gate),
        ],
        0,
    ).astype(BF16)
    prev = packed[:, 0:64, :].reshape(RESID, 256)
    now = packed[:, 64:128, :].reshape(RESID, 256)
    later = pltpu.roll(dot(prev, grad_pre), wide - DILATION, 1)[:, :tokens]
    grad_pre = grad_pre[:, :tokens]
    in_part = (dot(now, grad_pre) + later).astype(BF16)
    conv_grad = dot(features[:, :tokens], grad_pre, NT).astype(BF16)
    res_grad = dot(res[:, :tokens], hidden, NT).astype(BF16)
    skp_grad = dot(skp[:, :tokens], hidden, NT).astype(BF16)
    grads[:, 0:OUT_AT, :] = conv_grad.reshape(8, OUT_AT, 256)
    grads[:, OUT_AT:PACKED, 0:128] = res_grad.reshape(8, 64, 128)
    grads[:, OUT_AT:PACKED, 128:256] = skp_grad.reshape(8, 64, 128)
    parts = [dot(to_place, part).astype(BF16) for part in (res_part, skp_part, in_part)]
    for k, out in enumerate((z0, z1, z2, z3)):
        for i in range(4):
            at = 128 * k + 32 * i
            for n in range(3):
                out[i, 32 * n : 32 * n + 32] = parts[n][at : at + 32]


def sum_units(z0, z1, z2, z3, o0, o1, o2, o3):
    for i, out in enumerate((o0, o1, o2, o3)):
        out[...] = (
            z0[i].astype(F32) + z1[i].astype(F32) + z2[i].astype(F32) + z3[i].astype(F32)
        ).astype(BF16)


def finish_tokens(ids, o0, o1, o2, o3, sig, res, residual, skipped, grad_in):
    j = ids[1] & 3
    for k, piece in enumerate((o0, o1, o2, o3)):
        cut = pl.ds(pl.multiple_of((j ^ k) * 256, 256), 256)
        residual[:, cut] = sig[:, cut].astype(F32) + piece[0:32, :].astype(F32)
        skipped[:, cut] = piece[32:64, :].astype(F32)
        grad_in[:, cut] = res[:, cut].astype(F32) + piece[64:96, :].astype(F32)


def update(ids, owners, grads, master, first, second, *refs):
    outs, held, sems = refs[:3], refs[3:6], refs[6]
    slots = grads.shape[1]
    rows = 8 * slots
    owned = jnp.sum(jnp.where(owners[...] == ids[1], 1, 0))
    keep = iota((rows, 1), 0) < 8 * owned
    to, of = iota((rows, rows), 0), iota((rows, rows), 1)
    spread = jnp.zeros((rows, rows), jnp.bool_)
    for r in range(8):
        inside = (of >= r * slots) & (of < (r + 1) * slots)
        spread = spread | (inside & (to == 8 * (of - r * slots) + r))
    spread = onehot(spread)
    copies = []
    for z in range(4):
        cut = slice(256 * z, 256 * z + 256)
        grad = jnp.concatenate(
            [grads[16 * (r // 4) + 4 * z + r % 4].astype(F32) for r in range(8)], 0
        )
        grad = dot(spread, grad.astype(BF16))
        old_m = master[:, cut]
        old_f = first[:, cut]
        old_s = second[:, cut]
        first_new = MOMENT_DECAY * old_f + (1.0 - MOMENT_DECAY) * grad
        second_new = MOMENT_DECAY * old_s + (1.0 - MOMENT_DECAY) * grad * grad
        first_hat = first_new / (1.0 - MOMENT_DECAY**STEP)
        second_hat = second_new / (1.0 - MOMENT_DECAY**STEP)
        stepped = old_m - STEP_RATE * (
            first_hat / (jnp.sqrt(second_hat) + EPSILON) + WEIGHT_DECAY * old_m
        )
        held[0][:, cut] = jnp.where(keep, first_new, old_f)
        held[1][:, cut] = jnp.where(keep, second_new, old_s)
        held[2][:, cut] = jnp.where(keep, stepped, old_m)
        for n in range(3):
            copy = pltpu.make_async_copy(
                held[n].at[:, cut], outs[n].at[:, cut], sems.at[3 * z + n]
            )
            copy.start()
            copies.append(copy)
    for copy in copies:
        copy.wait()


BOTH = ("tm", "chan")


def swap(x, k):
    n = lax.axis_size("chan")
    return lax.ppermute(x, "chan", [(i, i ^ k) for i in range(n)])


def local(
    signal, mel_frames, speaker_ids, owners, master, first_moment, second_moment, res_cot, skip_cot
):
    slots_dev = master.shape[0]
    slots = 16 * slots_dev
    half = lax.axis_index("tm")
    ids = jnp.stack([half, lax.axis_index("chan")]).astype(jnp.int32)
    sig, res, skp, mel = signal.T, res_cot.T, skip_cot.T, mel_frames.T
    own_row = owners.reshape(1, NBLK)
    share = [[16 * y + 4 * z + j for y in range(2) for j in range(4)] for z in range(4)]
    sds = jax.ShapeDtypeStruct
    turn = [(0, 1), (1, 0)]

    edges = call(edge_tiles, sds((176, 128), BF16), 1, 4)(ids, sig, res, skp, mel)
    other = lax.ppermute(edges, "tm", turn)
    other_ids = lax.ppermute(speaker_ids, "tm", turn)
    sids = jnp.where(
        half == 0,
        jnp.concatenate([speaker_ids, other_ids]),
        jnp.concatenate([other_ids, speaker_ids]),
    )
    info = jnp.concatenate([ids, sids])

    sent = call(pack_weights, sds((16, slots_dev, 256), BF16), 1, 1)(ids, master)
    piece = sds((PIECE, 256), BF16)
    o = call(pack_tokens, (piece,) * 4, 1, 4)(ids, sig, res, skp, other)
    sent, _ = lax.optimization_barrier((sent, other))
    arrived = lax.all_to_all(sent, "chan", 0, 0, tiled=True)
    mine = jnp.stack([o[0], swap(o[1], 1), swap(o[2], 2), swap(o[3], 3)])
    p1, p2, p3 = (swap(mine, 4 * k) for k in (1, 2, 3))

    pick, put = call(
        functools.partial(place_blocks, slots_dev=slots_dev),
        (sds((PACKED, slots), BF16), sds((slots, PACKED), BF16)),
        1,
        1,
    )(info, own_row)
    arrived, _ = lax.optimization_barrier((arrived, mine))
    gathered = call(gather_blocks, sds((8, PACKED, 256), BF16), 0, 2)(
        pick, arrived.reshape(slots, 256)
    )
    packed = lax.all_to_all(gathered, BOTH, 0, 0, axis_index_groups=share)

    quad = sds((4, 96, 256), BF16)
    grads, z0, z1, z2, z3 = call(
        layer,
        (sds((8, PACKED, 256), BF16), quad, quad, quad, quad),
        1,
        7,
        scratch=(pltpu.VMEM((8, OUT_AT, 384), BF16),),
    )(info, packed, mine, p1, p2, p3, mel, other)

    parts = lax.all_to_all(grads, BOTH, 0, 0, axis_index_groups=share)
    t1, t2, t3 = (swap(z, 4 * k) for k, z in ((1, z1), (2, z2), (3, z3)))
    o = call(sum_units, (sds((96, 256), BF16),) * 4, 0, 4)(z0, t1, t2, t3)
    parts, _ = lax.optimization_barrier((parts, o[0]))
    spread = call(scatter_blocks, sds((2, slots, 256), BF16), 0, 2)(put, parts)
    returned = lax.all_to_all(spread.reshape(32, slots_dev, 256), BOTH, 0, 0)
    o = (o[0], swap(o[1], 1), swap(o[2], 2), swap(o[3], 3))
    narrow = sds(sig.shape, F32)
    residual, skipped, grad_in = call(finish_tokens, (narrow,) * 3, 1, 6)(ids, *o, sig, res)
    flat = (8 * slots_dev, GATES)
    new = call(
        update,
        (sds(flat, F32),) * 3,
        1,
        5,
        scratch=(pltpu.VMEM(flat, F32),) * 3 + (pltpu.SemaphoreType.DMA((12,)),),
        out_space=pl.ANY,
    )(
        ids,
        own_row,
        returned,
        master.reshape(flat),
        first_moment.reshape(flat),
        second_moment.reshape(flat),
    )
    return (residual.T, skipped.T, grad_in.T, *(x.reshape(master.shape) for x in new))


def place_index(owners, slots_dev):
    count = owners.shape[0]
    matches = owners[:, None] == owners[None, :]
    before = jnp.arange(count)[None, :] < jnp.arange(count)[:, None]
    ranks = jnp.sum((matches & before).astype(jnp.int32), axis=1)
    return owners * slots_dev + ranks


def local_plain(
    signal, mel_frames, speaker_ids, owners, master, first_moment, second_moment, res_cot, skip_cot
):
    chans = lax.axis_size("chan")
    slots_dev = master.shape[0]
    tok_count = signal.shape[0]
    hid_local = HIDDEN_SIZE // chans
    col_count = GATES // chans
    seg_count = speaker_ids.shape[0]
    spk_start = 2 * RESID + MELS
    out_start = spk_start + SPEAKERS
    places = place_index(owners, slots_dev)
    table = places[:, None] == jnp.arange(chans * slots_dev)[None, :]
    received = lax.all_to_all(
        master.astype(BF16), "chan", split_axis=2, concat_axis=0, tiled=True
    ).reshape(chans * slots_dev, BLOCK * col_count)
    params = jnp.dot(table.astype(BF16), received, preferred_element_type=F32)
    params = params.astype(BF16).reshape(ROWS, col_count)
    tap_prev, tap_now = params[:RESID], params[RESID : 2 * RESID]
    mel_proj = params[2 * RESID : spk_start]
    speaker_table = params[spk_start:out_start]
    out_cols = params[out_start:].reshape(RESID, hid_local, 2)
    n_tm = lax.axis_size("tm")
    tail_prev = lax.ppermute(signal[-DILATION:], "tm", [(i, i + 1) for i in range(n_tm - 1)])
    inputs = lax.all_gather(signal, "chan", axis=1, tiled=True)
    tail_full = lax.all_gather(tail_prev, "chan", axis=1, tiled=True)
    shifted = jnp.concatenate([tail_full, inputs[:-DILATION]], 0)
    pre_act = jnp.dot(shifted, tap_prev, preferred_element_type=F32)
    pre_act = pre_act + jnp.dot(inputs, tap_now, preferred_element_type=F32)
    pre_act = pre_act + jnp.dot(mel_frames, mel_proj, preferred_element_type=F32)
    one_hot = (speaker_ids[:, None] == jnp.arange(SPEAKERS)[None, :]).astype(BF16)
    embedded = jnp.dot(one_hot, speaker_table, preferred_element_type=F32)
    pre_act = (pre_act.reshape(seg_count, SEG, col_count) + embedded[:, None, :]).reshape(
        tok_count, col_count
    )
    filt = jnp.tanh(pre_act[:, 0::2])
    gates = jax.nn.sigmoid(pre_act[:, 1::2])
    hidden = (filt * gates).astype(BF16)
    summed = lax.psum_scatter(
        jnp.einsum("cuw,tu->cwt", out_cols, hidden, preferred_element_type=F32),
        "chan",
        scatter_dimension=0,
        tiled=True,
    )
    cots = lax.all_gather(
        jnp.stack([res_cot.T, skip_cot.T], axis=1), "chan", axis=0, tiled=True
    )
    grad_hid = jnp.einsum("cwt,cuw->tu", cots, out_cols, preferred_element_type=F32)
    term = jnp.einsum("cwt,tu->cuw", cots, hidden, preferred_element_type=F32)
    grad_filt = grad_hid * gates * (1.0 - filt * filt)
    grad_gate = grad_hid * filt * gates * (1.0 - gates)
    grad_pre = (
        jnp.stack([grad_filt, grad_gate], axis=2).reshape(tok_count, col_count).astype(BF16)
    )
    ahead = lax.ppermute(grad_pre[:DILATION], "tm", [(i + 1, i) for i in range(n_tm - 1)])
    later = jnp.concatenate([grad_pre[DILATION:], ahead], 0)
    input_part = lax.psum_scatter(
        dot(tap_now, grad_pre, NT) + dot(tap_prev, later, NT),
        "chan",
        scatter_dimension=0,
        tiled=True,
    )
    seg_sums = jnp.sum(grad_pre.astype(F32).reshape(seg_count, SEG, col_count), axis=1)
    grad_spk = lax.dot_general(
        one_hot.astype(F32),
        seg_sums,
        TN,
        precision=lax.Precision.HIGHEST,
        preferred_element_type=F32,
    )
    grad_params = jnp.concatenate(
        [
            dot(shifted, grad_pre, TN),
            dot(inputs, grad_pre, TN),
            dot(mel_frames, grad_pre, TN),
            grad_spk,
            term.reshape(RESID, col_count),
        ],
        0,
    )
    grad_params = lax.psum(grad_params, "tm").reshape(NBLK, BLOCK * col_count)
    outgoing = lax.dot_general(
        table.astype(F32), grad_params, TN, precision=lax.Precision.HIGHEST
    ).reshape(chans * slots_dev, BLOCK, col_count)
    grad_slots = lax.all_to_all(outgoing, "chan", split_axis=0, concat_axis=2, tiled=True)
    owned = jnp.sum((owners == lax.axis_index("chan")).astype(jnp.int32))
    keep = (jnp.arange(slots_dev) < owned)[:, None, None]
    first_new = MOMENT_DECAY * first_moment + (1.0 - MOMENT_DECAY) * grad_slots
    second_new = MOMENT_DECAY * second_moment + (1.0 - MOMENT_DECAY) * grad_slots * grad_slots
    first_hat = first_new / (1.0 - MOMENT_DECAY**STEP)
    second_hat = second_new / (1.0 - MOMENT_DECAY**STEP)
    stepped = master - STEP_RATE * (
        first_hat / (jnp.sqrt(second_hat) + EPSILON) + WEIGHT_DECAY * master
    )
    return (
        signal.astype(F32) + summed[:, 0, :].T,
        summed[:, 1, :].T,
        res_cot.astype(F32) + input_part.T,
        jnp.where(keep, first_new, first_moment),
        jnp.where(keep, second_new, second_moment),
        jnp.where(keep, stepped, master),
    )


def solution(mesh):
    wide = P("tm", "chan")
    slots = P("chan", None, None)
    packed_mesh = mesh.shape["tm"] == 2 and mesh.shape["chan"] == 16
    return jax.shard_map(
        local if packed_mesh else local_plain,
        mesh=mesh,
        in_specs=(wide, P("tm", None), P("tm"), P(), slots, slots, slots, wide, wide),
        out_specs=(wide, wide, wide, slots, slots, slots),
        check_vma=False,
    )
```

```python
import functools

import jax
import jax.numpy as jnp
from jax import lax
from jax.experimental import pallas as pl
from jax.experimental.pallas import tpu as pltpu
from jax.sharding import PartitionSpec as P

RESID = 512
HIDDEN_SIZE = 512
MELS = 80
SPEAKERS = 944
DILATION = 8
SEG = 128
BLOCK = 8
STEP = 5
GATES = 1024
ROWS = 2560
NBLK = 320

MOMENT_DECAY = 0.5
STEP_RATE = 0.03
WEIGHT_DECAY = 0.01
EPSILON = 1e-08

F32 = jnp.float32
BF16 = jnp.bfloat16
NN = (((1,), (0,)), ((), ()))
NT = (((1,), (1,)), ((), ()))
TN = (((0,), (0,)), ((), ()))

TAPS = 2 * RESID // BLOCK
MEL_AT = TAPS
MEL_BLOCKS = MELS // BLOCK
SEG_AT = 144
OUT_AT = 160
PACKED = 224
SPK_BLOCK = TAPS + MEL_BLOCKS
OUT_BLOCK = SPK_BLOCK + SPEAKERS // BLOCK
PIECE = 112


def dot(a, b, dims=NN):
    return lax.dot_general(a, b, dims, preferred_element_type=F32)


def iota(shape, dim):
    return lax.broadcasted_iota(jnp.int32, shape, dim)


def onehot(cond):
    return jnp.where(cond, 1.0, 0.0).astype(BF16)


MIB = 2**20
VMEM, SMEM, HBM = pltpu.VMEM, pltpu.SMEM, pltpu.HBM


def call(kernel, out, spaces, gflops=0, scratch=(), out_space=VMEM, room=40 * MIB):
    return pl.pallas_call(
        kernel,
        out_shape=out,
        in_specs=[pl.BlockSpec(memory_space=space) for space in spaces],
        out_specs=jax.tree.map(lambda _: pl.BlockSpec(memory_space=out_space), out),
        scratch_shapes=list(scratch),
        compiler_params=pltpu.CompilerParams(vmem_limit_bytes=64 * MIB - room),
        cost_estimate=pl.CostEstimate(
            flops=gflops * 10**9, bytes_accessed=MIB, transcendentals=0
        ),
    )


def gate_order(dim):
    natural, split = iota((256, 256), dim), iota((256, 256), 1 - dim)
    return onehot(natural == 2 * (split & 127) + (split >> 7))


def begin(spk, master, sig, res, skp, mel, sent, edges, strips, sems):
    half = lax.axis_index("tm")
    slots = master.shape[0]
    rows = 4 * slots
    cut = pl.ds(pl.multiple_of((1 - half) * 896, 128), 128)
    tiles = []
    for n, part in enumerate((sig, res, skp, mel)):
        to = edges.at[32 * n : 32 * n + part.shape[0], :]
        tiles.append(pltpu.make_async_copy(part.at[:, cut], to, sems.at[4 + n]))
    copies = []
    for z in range(4):
        part = master.at[:, :, 256 * z : 256 * z + 256]
        copies.append(pltpu.make_async_copy(part, strips.at[z], sems.at[z]))
    for copy in copies + tiles:
        copy.start()
    row, lane = iota((16, 128), 0), iota((16, 128), 1)
    table = jnp.zeros((16, 128), jnp.int32)
    for s in range(8):
        code = jnp.where(row == 0, spk[s] >> 3, spk[s] & 7)
        table = jnp.where((lane == s) & (row < 2), code, table)
    edges[176:192, :] = table.astype(F32).astype(BF16)
    here = iota((rows, 8 * slots), 0)
    there = iota((rows, 8 * slots), 1)
    row, slot = jnp.zeros_like(here), here
    for step in range(1, 4):
        past = here >= step * slots
        row = jnp.where(past, step, row)
        slot = jnp.where(past, here - step * slots, slot)
    pick = onehot(there == 8 * slot + 4 * half + row)
    for z in range(4):
        copies[z].wait()
        got = dot(pick, strips[z].reshape(8 * slots, 256).astype(BF16))
        for j in range(4):
            sent[4 * z + j] = got[j * slots : (j + 1) * slots].astype(BF16)
    for tile in tiles:
        tile.wait()


def pack_tokens(sig, res, skp, other, o0, o1, o2, o3):
    half, j = lax.axis_index("tm"), lax.axis_index("chan") & 3
    outs = (o0, o1, o2, o3)
    parts = (sig, res, skp)
    befores, nexts = [], ([], [], [])
    for k in range(4):
        to = j ^ k
        cut = pl.ds(pl.multiple_of(to * 256, 256), 256)
        for n, part in enumerate(parts):
            outs[k][32 * n : 32 * n + 32, :] = part[:, cut]
        cut = pl.ds(pl.multiple_of(jnp.maximum(to * 256 - 128, 0), 128), 128)
        edge = jnp.where(half == 1, other[0:32, :].astype(F32), 0.0)
        befores.append(jnp.where(to == 0, edge, sig[:, cut].astype(F32)))
        cut = pl.ds(pl.multiple_of(jnp.minimum(to * 256 + 256, 896), 128), 128)
        for n, part in enumerate(parts):
            edge = jnp.where(half == 0, other[32 * n : 32 * n + 32, :].astype(F32), 0.0)
            nexts[n].append(jnp.where(to == 3, edge, part[:, cut].astype(F32)))
    tall = [jnp.concatenate(x, 0).astype(BF16) for x in (befores, *nexts)]
    t, lane = iota((16, 128), 0), iota((16, 128), 1)
    top, low = t < DILATION, t >= DILATION
    head_top = onehot(top & (lane == t))
    head_low = onehot(low & (lane == t - DILATION))
    last_top = onehot(top & (lane == t + 120))
    rows = (
        dot(last_top, tall[0], NT) + dot(head_low, tall[1], NT),
        dot(head_top, tall[2], NT) + dot(head_low, tall[3], NT),
    )
    for k in range(4):
        for n in range(2):
            outs[k][96:112, 128 * n : 128 * n + 128] = jnp.where(
                (lane >> 5) == k, rows[n], 0.0
            ).astype(BF16)


def place_blocks(spk_ids, owners, other, at_col, at_row, *, slots_dev):
    half = lax.axis_index("tm")
    own_row = owners[...]
    down, across = iota((NBLK, NBLK), 0), iota((NBLK, NBLK), 1)
    row_all = jnp.broadcast_to(own_row, (NBLK, NBLK))
    own_col = jnp.sum(jnp.where(down == across, row_all, 0), axis=1, keepdims=True)
    before = (own_col == row_all) & (down < across)
    rank = jnp.sum(jnp.where(before, 1, 0), axis=0, keepdims=True)
    place = own_row * slots_dev + rank
    n = iota((PACKED, 128), 0)
    far = n - SEG_AT - 8 * (1 - half) == iota((PACKED, 128), 1)
    blocks = jnp.broadcast_to(other[176:192, :].astype(F32)[0:1], (PACKED, 128))
    spk = jnp.sum(jnp.where(far, blocks, 0.0), axis=1, keepdims=True).astype(jnp.int32)
    n = iota((PACKED, 1), 0)
    for s in range(8):
        spk = jnp.where(n == SEG_AT + 8 * half + s, spk_ids[s] >> 3, spk)
    blk = jnp.where(
        n < SPK_BLOCK,
        n,
        jnp.where(n < SEG_AT, -1, jnp.where(n < OUT_AT, SPK_BLOCK + spk, n + (OUT_BLOCK - OUT_AT))),
    )
    match = jnp.broadcast_to(blk, (PACKED, NBLK)) == iota((PACKED, NBLK), 1)
    at = jnp.sum(jnp.where(match, jnp.broadcast_to(place, (PACKED, NBLK)), 0), axis=1, keepdims=True)
    at = jnp.where(blk < 0, -1, at)
    at_col[...] = jnp.broadcast_to(at, (PACKED, 128))
    same = iota((PACKED, PACKED), 0) == iota((PACKED, PACKED), 1)
    row = jnp.sum(jnp.where(same, jnp.broadcast_to(at, (PACKED, PACKED)), 0), axis=0, keepdims=True)
    at_row[...] = jnp.broadcast_to(row, (8, PACKED))


def gather_blocks(at_col, slots, out):
    shape = (PACKED, slots.shape[0])
    pick = onehot(jnp.broadcast_to(at_col[:, 0:1], shape) == iota(shape, 1))
    got = dot(pick, slots[...]).astype(BF16)
    got = dot(got, gate_order(0)).astype(BF16)
    for n in range(8):
        out[n] = got


def scatter_blocks(at_row, parts, out):
    total = parts[0].astype(F32)
    for n in range(1, 8):
        total = total + parts[n].astype(F32)
    natural = dot(total.astype(BF16), gate_order(1)).astype(BF16)
    shape = (out.shape[1], PACKED)
    put = onehot(jnp.broadcast_to(at_row[0:1, :], shape) == iota(shape, 0))
    spread = dot(put, natural).astype(BF16)
    out[0] = spread
    out[1] = spread


def sum_units(z0, z1, z2, z3, o0, o1, o2, o3):
    for i, out in enumerate((o0, o1, o2, o3)):
        out[...] = (
            z0[i].astype(F32) + z1[i].astype(F32) + z2[i].astype(F32) + z3[i].astype(F32)
        ).astype(BF16)


def channel_of(pos, ch):
    return ((pos >> 5) ^ ch) * 32 + (pos & 31)


def to_major(ch, dim):
    shape = (RESID, RESID)
    major = iota(shape, dim)
    return onehot(channel_of(iota(shape, 1 - dim), ch) == 8 * (major & 63) + (major >> 6))


def prepare(spk, p0, p1, p2, p3, mel, other, features, res, skp):
    half, ch = lax.axis_index("tm"), lax.axis_index("chan")
    j = ch & 3
    got = (p0, p1, p2, p3)
    tokens, wide = 256, 384
    order = to_major(ch, 0)

    def stacked(n):
        return jnp.concatenate(
            [got[k][i, 32 * n : 32 * n + 32, :] for k in range(4) for i in range(4)], 0
        )

    ends = []
    for k in range(4):
        end = got[k][0, 96:112, :].astype(F32)
        for i in range(1, 4):
            end = end + got[k][i, 96:112, :].astype(F32)
        ends.append(end)
    ends = [jnp.concatenate([e[:, 128 * n : 128 * n + 128] for e in ends], 1) for n in range(2)]
    gap = jnp.zeros((120, RESID), F32)
    ends = jnp.concatenate(
        [ends[0][8:16], gap[:112], ends[0][0:8], ends[1][0:8], gap, ends[1][8:16], gap], 0
    ).astype(BF16)
    ends = dot(order, ends, NT)
    sig = jnp.concatenate([dot(order, stacked(0)), ends[:, 0:128]], 1)
    res[...] = jnp.concatenate([dot(order, stacked(1)), ends[:, 128:256]], 1).astype(BF16)
    skp[...] = jnp.concatenate([dot(order, stacked(2)), ends[:, 256:384]], 1).astype(BF16)
    shifted = pltpu.roll(sig, DILATION, 1).astype(BF16)
    sig = sig.astype(BF16)
    m = iota((128, MELS), 0)
    mel_pick = onehot(((m & 15) < MEL_BLOCKS) & (iota((128, MELS), 1) == 8 * (m & 15) + (m >> 4)))
    cut = pl.ds(pl.multiple_of(j * tokens, tokens), tokens)
    far = pl.ds(pl.multiple_of(jnp.minimum(j * tokens + tokens, 896), 128), 128)
    ahead = jnp.where(j == 3, other[96:176, :].astype(F32), mel[:, far].astype(F32)).astype(BF16)
    mels = jnp.concatenate([dot(mel_pick, mel[:, cut]), dot(mel_pick, ahead)], 1).astype(BF16)
    seg = 8 * half + 2 * j
    row, lane = iota((16, wide), 0), iota((16, wide), 1)
    beyond = other[176:192, :].astype(F32)[1:2, 0:1].astype(jnp.int32)
    beyond = jnp.where(j == 3, beyond, spk[jnp.minimum(2 * j + 2, 7)] & 7)
    sub = jnp.where(
        lane < SEG,
        spk[2 * j] & 7,
        jnp.where(lane < 2 * SEG, spk[2 * j + 1] & 7, jnp.broadcast_to(beyond, (16, wide))),
    )
    for r in range(8):
        features[r, 0:64] = shifted[64 * r : 64 * r + 64]
        features[r, 64:128] = sig[64 * r : 64 * r + 64]
        features[r, 128:144] = mels[16 * r : 16 * r + 16]
        features[r, 144:160] = onehot((row == seg + (lane >> 7)) & (sub == r))


def layer(packed, feat, res, skp, grads, z0, z1, z2, z3):
    tokens, wide = 256, 384
    to_place = to_major(lax.axis_index("chan"), 1)
    features = feat[...].reshape(8 * OUT_AT, wide)
    conv = packed[:, 0:OUT_AT, :].reshape(8 * OUT_AT, 256)
    pre = dot(conv, features, TN)
    filt = jnp.tanh(pre[:128])
    gate = jax.nn.sigmoid(pre[128:])
    hidden = (filt[:, :tokens] * gate[:, :tokens]).astype(BF16)
    out_res = packed[:, OUT_AT:PACKED, 0:128].reshape(RESID, 128)
    out_skp = packed[:, OUT_AT:PACKED, 128:256].reshape(RESID, 128)
    res_part = dot(out_res, hidden).astype(BF16)
    skp_part = dot(out_skp, hidden).astype(BF16)
    grad_hidden = dot(out_res, res[...], TN) + dot(out_skp, skp[...], TN)
    grad_pre = jnp.concatenate(
        [
            grad_hidden * gate * (1.0 - filt * filt),
            grad_hidden * filt * gate * (1.0 - gate),
        ],
        0,
    ).astype(BF16)
    prev = packed[:, 0:64, :].reshape(RESID, 256)
    now = packed[:, 64:128, :].reshape(RESID, 256)
    later = pltpu.roll(dot(prev, grad_pre), wide - DILATION, 1)[:, :tokens]
    grad_pre = grad_pre[:, :tokens]
    in_part = (dot(now, grad_pre) + later).astype(BF16)
    conv_grad = dot(features[:, :tokens], grad_pre, NT).astype(BF16)
    res_grad = dot(res[:, :tokens], hidden, NT).astype(BF16)
    skp_grad = dot(skp[:, :tokens], hidden, NT).astype(BF16)
    grads[:, 0:OUT_AT, :] = conv_grad.reshape(8, OUT_AT, 256)
    grads[:, OUT_AT:PACKED, 0:128] = res_grad.reshape(8, 64, 128)
    grads[:, OUT_AT:PACKED, 128:256] = skp_grad.reshape(8, 64, 128)
    parts = [dot(to_place, part).astype(BF16) for part in (res_part, skp_part, in_part)]
    for k, out in enumerate((z0, z1, z2, z3)):
        for i in range(4):
            at = 128 * k + 32 * i
            for n in range(3):
                out[i, 32 * n : 32 * n + 32] = parts[n][at : at + 32]


def finish_tokens(o0, o1, o2, o3, sig, res, residual, skipped, grad_in):
    j = lax.axis_index("chan") & 3
    for k, piece in enumerate((o0, o1, o2, o3)):
        cut = pl.ds(pl.multiple_of((j ^ k) * 256, 256), 256)
        residual[:, cut] = sig[:, cut].astype(F32) + piece[0:32, :].astype(F32)
        skipped[:, cut] = piece[32:64, :].astype(F32)
        grad_in[:, cut] = res[:, cut].astype(F32) + piece[64:96, :].astype(F32)


def update(owners, grads, master, first, second, *refs):
    outs, held, old, grad, sems = refs[:3], refs[3:6], refs[6:9], refs[9], refs[10]
    slots = grads.shape[1]
    rows = 8 * slots
    parts = [slice(n * rows // 4, (n + 1) * rows // 4) for n in range(4)]
    fetches = []
    for n, part in enumerate(parts):
        for m, source in enumerate((first, second, master)):
            fetch = pltpu.make_async_copy(
                source.at[part, :], old[m].at[part, :], sems.at[12 + 3 * n + m]
            )
            fetch.start()
            fetches.append(fetch)
    owned = jnp.sum(jnp.where(owners[...] == lax.axis_index("chan"), 1, 0))
    to, of = iota((rows, rows), 0), iota((rows, rows), 1)
    spread = jnp.zeros((rows, rows), jnp.bool_)
    for r in range(8):
        inside = (of >= r * slots) & (of < (r + 1) * slots)
        spread = spread | (inside & (to == 8 * (of - r * slots) + r))
    spread = onehot(spread)
    for z in range(4):
        got = jnp.concatenate(
            [grads[16 * (r // 4) + 4 * z + r % 4].astype(F32) for r in range(8)], 0
        )
        grad[:, 256 * z : 256 * z + 256] = dot(spread, got.astype(BF16))
    copies = []
    for n, part in enumerate(parts):
        for m in range(3):
            fetches[3 * n + m].wait()
        old_f, old_s, old_m = (ref[part, :] for ref in old)
        new = grad[part, :]
        keep = n * (rows // 4) + iota((rows // 4, 1), 0) < 8 * owned
        first_new = MOMENT_DECAY * old_f + (1.0 - MOMENT_DECAY) * new
        second_new = MOMENT_DECAY * old_s + (1.0 - MOMENT_DECAY) * new * new
        first_hat = first_new / (1.0 - MOMENT_DECAY**STEP)
        second_hat = second_new / (1.0 - MOMENT_DECAY**STEP)
        stepped = old_m - STEP_RATE * (
            first_hat / (jnp.sqrt(second_hat) + EPSILON) + WEIGHT_DECAY * old_m
        )
        held[0][part, :] = jnp.where(keep, first_new, old_f)
        held[1][part, :] = jnp.where(keep, second_new, old_s)
        held[2][part, :] = jnp.where(keep, stepped, old_m)
        for m in range(3):
            copy = pltpu.make_async_copy(
                held[m].at[part, :], outs[m].at[part, :], sems.at[3 * n + m]
            )
            copy.start()
            copies.append(copy)
    for copy in copies:
        copy.wait()


BOTH = ("tm", "chan")


def swap(x, k):
    n = lax.axis_size("chan")
    return lax.ppermute(x, "chan", [(i, i ^ k) for i in range(n)])


def local(
    signal, mel_frames, speaker_ids, owners, master, first_moment, second_moment, res_cot, skip_cot
):
    slots_dev = master.shape[0]
    slots = 16 * slots_dev
    sig, res, skp, mel = signal.T, res_cot.T, skip_cot.T, mel_frames.T
    own_row = owners.reshape(1, NBLK)
    share = [[16 * y + 4 * z + j for y in range(2) for j in range(4)] for z in range(4)]
    sds = jax.ShapeDtypeStruct
    dma = pltpu.SemaphoreType.DMA

    sent, edges = call(
        begin,
        (sds((16, slots_dev, 256), BF16), sds((192, 128), BF16)),
        (SMEM,) + (HBM,) * 5,
        scratch=(pltpu.VMEM((4, slots_dev, 8, 256), F32), dma((8,))),
        room=MIB // 16,
    )(speaker_ids, master, sig, res, skp, mel)
    arrived = lax.all_to_all(sent, "chan", 0, 0, tiled=True)
    other = lax.ppermute(edges, "tm", [(0, 1), (1, 0)])
    piece = sds((PIECE, 256), BF16)
    o = call(pack_tokens, (piece,) * 4, (VMEM,) * 4)(sig, res, skp, other)
    mine = jnp.stack([o[0], swap(o[1], 1), swap(o[2], 2), swap(o[3], 3)])
    p1, p2, p3 = (swap(mine, 4 * k) for k in (1, 2, 3))

    at_col, at_row = call(
        functools.partial(place_blocks, slots_dev=slots_dev),
        (sds((PACKED, 128), jnp.int32), sds((8, PACKED), jnp.int32)),
        (SMEM, VMEM, VMEM),
    )(speaker_ids, own_row, other)
    arrived, _ = lax.optimization_barrier((arrived, mine))
    gathered = call(gather_blocks, sds((8, PACKED, 256), BF16), (VMEM, VMEM))(
        at_col, arrived.reshape(slots, 256)
    )
    packed = lax.all_to_all(gathered, BOTH, 0, 0, axis_index_groups=share)
    cots = sds((RESID, 384), BF16)
    ready = call(
        prepare,
        (sds((8, OUT_AT, 384), BF16), cots, cots),
        (SMEM,) + (VMEM,) * 6,
        gflops=200,
    )(speaker_ids, mine, p1, p2, p3, mel, other)

    quad = sds((4, 96, 256), BF16)
    grads, z0, z1, z2, z3 = call(
        layer, (sds((8, PACKED, 256), BF16), quad, quad, quad, quad), (VMEM,) * 4
    )(packed, *ready)

    parts = lax.all_to_all(grads, BOTH, 0, 0, axis_index_groups=share)
    t1, t2, t3 = (swap(z, 4 * k) for k, z in ((1, z1), (2, z2), (3, z3)))
    spread = call(scatter_blocks, sds((2, slots, 256), BF16), (VMEM, VMEM))(
        at_row, parts
    )
    returned = lax.all_to_all(spread.reshape(32, slots_dev, 256), BOTH, 0, 0)
    o = call(sum_units, (sds((96, 256), BF16),) * 4, (VMEM,) * 4, gflops=20)(z0, t1, t2, t3)
    o = (o[0], swap(o[1], 1), swap(o[2], 2), swap(o[3], 3))
    narrow = sds(sig.shape, F32)
    residual, skipped, grad_in = call(finish_tokens, (narrow,) * 3, (VMEM,) * 6)(*o, sig, res)
    flat = (8 * slots_dev, GATES)
    new = call(
        update,
        (sds(flat, F32),) * 3,
        (VMEM, VMEM, HBM, HBM, HBM),
        scratch=(pltpu.VMEM(flat, F32),) * 7 + (dma((24,)),),
        out_space=HBM,
        room=6 * MIB // 5,
    )(
        own_row,
        returned,
        master.reshape(flat),
        first_moment.reshape(flat),
        second_moment.reshape(flat),
    )
    return (residual.T, skipped.T, grad_in.T, *(x.reshape(master.shape) for x in new))


def place_index(owners, slots_dev):
    count = owners.shape[0]
    matches = owners[:, None] == owners[None, :]
    before = jnp.arange(count)[None, :] < jnp.arange(count)[:, None]
    ranks = jnp.sum((matches & before).astype(jnp.int32), axis=1)
    return owners * slots_dev + ranks


def local_plain(
    signal, mel_frames, speaker_ids, owners, master, first_moment, second_moment, res_cot, skip_cot
):
    chans = lax.axis_size("chan")
    slots_dev = master.shape[0]
    tok_count = signal.shape[0]
    hid_local = HIDDEN_SIZE // chans
    col_count = GATES // chans
    seg_count = speaker_ids.shape[0]
    spk_start = 2 * RESID + MELS
    out_start = spk_start + SPEAKERS
    places = place_index(owners, slots_dev)
    table = places[:, None] == jnp.arange(chans * slots_dev)[None, :]
    received = lax.all_to_all(
        master.astype(BF16), "chan", split_axis=2, concat_axis=0, tiled=True
    ).reshape(chans * slots_dev, BLOCK * col_count)
    params = jnp.dot(table.astype(BF16), received, preferred_element_type=F32)
    params = params.astype(BF16).reshape(ROWS, col_count)
    tap_prev, tap_now = params[:RESID], params[RESID : 2 * RESID]
    mel_proj = params[2 * RESID : spk_start]
    speaker_table = params[spk_start:out_start]
    out_cols = params[out_start:].reshape(RESID, hid_local, 2)
    n_tm = lax.axis_size("tm")
    tail_prev = lax.ppermute(signal[-DILATION:], "tm", [(i, i + 1) for i in range(n_tm - 1)])
    inputs = lax.all_gather(signal, "chan", axis=1, tiled=True)
    tail_full = lax.all_gather(tail_prev, "chan", axis=1, tiled=True)
    shifted = jnp.concatenate([tail_full, inputs[:-DILATION]], 0)
    pre_act = jnp.dot(shifted, tap_prev, preferred_element_type=F32)
    pre_act = pre_act + jnp.dot(inputs, tap_now, preferred_element_type=F32)
    pre_act = pre_act + jnp.dot(mel_frames, mel_proj, preferred_element_type=F32)
    one_hot = (speaker_ids[:, None] == jnp.arange(SPEAKERS)[None, :]).astype(BF16)
    embedded = jnp.dot(one_hot, speaker_table, preferred_element_type=F32)
    pre_act = (pre_act.reshape(seg_count, SEG, col_count) + embedded[:, None, :]).reshape(
        tok_count, col_count
    )
    filt = jnp.tanh(pre_act[:, 0::2])
    gates = jax.nn.sigmoid(pre_act[:, 1::2])
    hidden = (filt * gates).astype(BF16)
    summed = lax.psum_scatter(
        jnp.einsum("cuw,tu->cwt", out_cols, hidden, preferred_element_type=F32),
        "chan",
        scatter_dimension=0,
        tiled=True,
    )
    cots = lax.all_gather(
        jnp.stack([res_cot.T, skip_cot.T], axis=1), "chan", axis=0, tiled=True
    )
    grad_hid = jnp.einsum("cwt,cuw->tu", cots, out_cols, preferred_element_type=F32)
    term = jnp.einsum("cwt,tu->cuw", cots, hidden, preferred_element_type=F32)
    grad_filt = grad_hid * gates * (1.0 - filt * filt)
    grad_gate = grad_hid * filt * gates * (1.0 - gates)
    grad_pre = (
        jnp.stack([grad_filt, grad_gate], axis=2).reshape(tok_count, col_count).astype(BF16)
    )
    ahead = lax.ppermute(grad_pre[:DILATION], "tm", [(i + 1, i) for i in range(n_tm - 1)])
    later = jnp.concatenate([grad_pre[DILATION:], ahead], 0)
    input_part = lax.psum_scatter(
        dot(tap_now, grad_pre, NT) + dot(tap_prev, later, NT),
        "chan",
        scatter_dimension=0,
        tiled=True,
    )
    seg_sums = jnp.sum(grad_pre.astype(F32).reshape(seg_count, SEG, col_count), axis=1)
    grad_spk = lax.dot_general(
        one_hot.astype(F32),
        seg_sums,
        TN,
        precision=lax.Precision.HIGHEST,
        preferred_element_type=F32,
    )
    grad_params = jnp.concatenate(
        [
            dot(shifted, grad_pre, TN),
            dot(inputs, grad_pre, TN),
            dot(mel_frames, grad_pre, TN),
            grad_spk,
            term.reshape(RESID, col_count),
        ],
        0,
    )
    grad_params = lax.psum(grad_params, "tm").reshape(NBLK, BLOCK * col_count)
    outgoing = lax.dot_general(
        table.astype(F32), grad_params, TN, precision=lax.Precision.HIGHEST
    ).reshape(chans * slots_dev, BLOCK, col_count)
    grad_slots = lax.all_to_all(outgoing, "chan", split_axis=0, concat_axis=2, tiled=True)
    owned = jnp.sum((owners == lax.axis_index("chan")).astype(jnp.int32))
    keep = (jnp.arange(slots_dev) < owned)[:, None, None]
    first_new = MOMENT_DECAY * first_moment + (1.0 - MOMENT_DECAY) * grad_slots
    second_new = MOMENT_DECAY * second_moment + (1.0 - MOMENT_DECAY) * grad_slots * grad_slots
    first_hat = first_new / (1.0 - MOMENT_DECAY**STEP)
    second_hat = second_new / (1.0 - MOMENT_DECAY**STEP)
    stepped = master - STEP_RATE * (
        first_hat / (jnp.sqrt(second_hat) + EPSILON) + WEIGHT_DECAY * master
    )
    return (
        signal.astype(F32) + summed[:, 0, :].T,
        summed[:, 1, :].T,
        res_cot.astype(F32) + input_part.T,
        jnp.where(keep, first_new, first_moment),
        jnp.where(keep, second_new, second_moment),
        jnp.where(keep, stepped, master),
    )


def solution(mesh):
    wide = P("tm", "chan")
    slots = P("chan", None, None)
    packed_mesh = mesh.shape["tm"] == 2 and mesh.shape["chan"] == 16
    return jax.shard_map(
        local if packed_mesh else local_plain,
        mesh=mesh,
        in_specs=(wide, P("tm", None), P("tm"), P(), slots, slots, slots, wide, wide),
        out_specs=(wide, wide, wide, slots, slots, slots),
        check_vma=False,
    )
```

```python
import functools

import jax
import jax.numpy as jnp
from jax import lax
from jax.experimental import pallas as pl
from jax.experimental.pallas import tpu as pltpu
from jax.sharding import PartitionSpec as P

RESID = 512
HIDDEN_SIZE = 512
MELS = 80
SPEAKERS = 944
DILATION = 8
SEG = 128
BLOCK = 8
STEP = 5
GATES = 1024
ROWS = 2560
NBLK = 320

MOMENT_DECAY = 0.5
STEP_RATE = 0.03
WEIGHT_DECAY = 0.01
EPSILON = 1e-08

F32 = jnp.float32
BF16 = jnp.bfloat16
NN = (((1,), (0,)), ((), ()))
NT = (((1,), (1,)), ((), ()))
TN = (((0,), (0,)), ((), ()))

TAPS = 2 * RESID // BLOCK
MEL_AT = TAPS
MEL_BLOCKS = MELS // BLOCK
SEG_AT = 144
OUT_AT = 160
PACKED = 224
SPK_BLOCK = TAPS + MEL_BLOCKS
OUT_BLOCK = SPK_BLOCK + SPEAKERS // BLOCK
PIECE = 112


def dot(a, b, dims=NN):
    return lax.dot_general(a, b, dims, preferred_element_type=F32)


def iota(shape, dim):
    return lax.broadcasted_iota(jnp.int32, shape, dim)


def onehot(cond):
    return jnp.where(cond, 1.0, 0.0).astype(BF16)


KIB, MIB = 2**10, 2**20
VMEM, SMEM, HBM = pltpu.VMEM, pltpu.SMEM, pltpu.HBM


def call(kernel, out, spaces, gflops=0, scratch=(), out_space=VMEM):
    run = pl.pallas_call(
        kernel,
        out_shape=out,
        in_specs=[pl.BlockSpec(memory_space=space) for space in spaces],
        out_specs=jax.tree.map(lambda _: pl.BlockSpec(memory_space=out_space), out),
        scratch_shapes=list(scratch),
        compiler_params=pltpu.CompilerParams(vmem_limit_bytes=24 * MIB),
        cost_estimate=pl.CostEstimate(
            flops=gflops * 10**9, bytes_accessed=MIB, transcendentals=0
        ),
    )
    pin = pltpu.with_memory_space_constraint
    return lambda *args: run(*(pin(x, HBM) if space == HBM else x for x, space in zip(args, spaces, strict=True)))


def gate_order(dim):
    natural, split = iota((256, 256), dim), iota((256, 256), 1 - dim)
    return onehot(natural == 2 * (split & 127) + (split >> 7))


def begin(speakers, master, sig, res, skp, mel, sent, edges, strips, spk, sems):
    half = lax.axis_index("tm")
    slots = master.shape[0]
    rows = 4 * slots
    cut = pl.ds(pl.multiple_of((1 - half) * 896, 128), 128)
    tiles = []
    for n, part in enumerate((sig, res, skp, mel)):
        to = edges.at[32 * n : 32 * n + part.shape[0], :]
        tiles.append(pltpu.make_async_copy(part.at[:, cut], to, sems.at[4 + n]))
    copies = []
    for z in range(4):
        part = master.at[:, :, 256 * z : 256 * z + 256]
        copies.append(pltpu.make_async_copy(part, strips.at[z], sems.at[z]))
    names = pltpu.make_async_copy(speakers, spk, sems.at[8])
    for copy in (names, *copies, *tiles):
        copy.start()
    names.wait()
    row, lane = iota((16, 128), 0), iota((16, 128), 1)
    table = jnp.zeros((16, 128), jnp.int32)
    for s in range(8):
        code = jnp.where(row == 0, spk[s] >> 3, spk[s] & 7)
        table = jnp.where((lane == s) & (row < 2), code, table)
    edges[176:192, :] = table.astype(F32).astype(BF16)
    here = iota((rows, 8 * slots), 0)
    there = iota((rows, 8 * slots), 1)
    row, slot = jnp.zeros_like(here), here
    for step in range(1, 4):
        past = here >= step * slots
        row = jnp.where(past, step, row)
        slot = jnp.where(past, here - step * slots, slot)
    pick = onehot(there == 8 * slot + 4 * half + row)
    for z in range(4):
        copies[z].wait()
        got = dot(pick, strips[z].reshape(8 * slots, 256).astype(BF16))
        for j in range(4):
            sent[4 * z + j] = got[j * slots : (j + 1) * slots].astype(BF16)
    for tile in tiles:
        tile.wait()


def pack_tokens(sig_hbm, res_hbm, skp_hbm, other, o0, o1, o2, o3, held, sems):
    copies = [
        pltpu.make_async_copy(part, held.at[n], sems.at[n])
        for n, part in enumerate((sig_hbm, res_hbm, skp_hbm))
    ]
    for copy in copies:
        copy.start()
    for copy in copies:
        copy.wait()
    sig, res, skp = (held.at[n] for n in range(3))
    half, j = lax.axis_index("tm"), lax.axis_index("chan") & 3
    outs = (o0, o1, o2, o3)
    parts = (sig, res, skp)
    befores, nexts = [], ([], [], [])
    for k in range(4):
        to = j ^ k
        cut = pl.ds(pl.multiple_of(to * 256, 256), 256)
        for n, part in enumerate(parts):
            outs[k][32 * n : 32 * n + 32, :] = part[:, cut]
        cut = pl.ds(pl.multiple_of(jnp.maximum(to * 256 - 128, 0), 128), 128)
        edge = jnp.where(half == 1, other[0:32, :].astype(F32), 0.0)
        befores.append(jnp.where(to == 0, edge, sig[:, cut].astype(F32)))
        cut = pl.ds(pl.multiple_of(jnp.minimum(to * 256 + 256, 896), 128), 128)
        for n, part in enumerate(parts):
            edge = jnp.where(half == 0, other[32 * n : 32 * n + 32, :].astype(F32), 0.0)
            nexts[n].append(jnp.where(to == 3, edge, part[:, cut].astype(F32)))
    tall = [jnp.concatenate(x, 0).astype(BF16) for x in (befores, *nexts)]
    t, lane = iota((16, 128), 0), iota((16, 128), 1)
    top, low = t < DILATION, t >= DILATION
    head_top = onehot(top & (lane == t))
    head_low = onehot(low & (lane == t - DILATION))
    last_top = onehot(top & (lane == t + 120))
    rows = (
        dot(last_top, tall[0], NT) + dot(head_low, tall[1], NT),
        dot(head_top, tall[2], NT) + dot(head_low, tall[3], NT),
    )
    for k in range(4):
        for n in range(2):
            outs[k][96:112, 128 * n : 128 * n + 128] = jnp.where(
                (lane >> 5) == k, rows[n], 0.0
            ).astype(BF16)


def join(o0, o1, o2, o3, out):
    ends = o0[96:112, :].astype(F32)
    for piece in (o1, o2, o3):
        ends = ends + piece[96:112, :].astype(F32)
    for k, piece in enumerate((o0, o1, o2, o3)):
        out[96 * k : 96 * k + 96, :] = piece[0:96, :]
    out[384:400, :] = ends.astype(BF16)


def place_blocks(spk_ids, owners, other, at_col, at_row, owned, *, slots_dev):
    half = lax.axis_index("tm")
    own_row = owners[...]
    mine = jnp.where(own_row == lax.axis_index("chan"), 1, 0)
    owned[...] = jnp.broadcast_to(jnp.sum(mine, axis=1, keepdims=True), owned.shape)
    down, across = iota((NBLK, NBLK), 0), iota((NBLK, NBLK), 1)
    row_all = jnp.broadcast_to(own_row, (NBLK, NBLK))
    own_col = jnp.sum(jnp.where(down == across, row_all, 0), axis=1, keepdims=True)
    before = (own_col == row_all) & (down < across)
    rank = jnp.sum(jnp.where(before, 1, 0), axis=0, keepdims=True)
    place = own_row * slots_dev + rank
    n = iota((PACKED, 128), 0)
    far = n - SEG_AT - 8 * (1 - half) == iota((PACKED, 128), 1)
    blocks = jnp.broadcast_to(other[176:192, :].astype(F32)[0:1], (PACKED, 128))
    spk = jnp.sum(jnp.where(far, blocks, 0.0), axis=1, keepdims=True).astype(jnp.int32)
    n = iota((PACKED, 1), 0)
    for s in range(8):
        spk = jnp.where(n == SEG_AT + 8 * half + s, spk_ids[s] >> 3, spk)
    blk = jnp.where(
        n < SPK_BLOCK,
        n,
        jnp.where(n < SEG_AT, -1, jnp.where(n < OUT_AT, SPK_BLOCK + spk, n + (OUT_BLOCK - OUT_AT))),
    )
    match = jnp.broadcast_to(blk, (PACKED, NBLK)) == iota((PACKED, NBLK), 1)
    at = jnp.sum(jnp.where(match, jnp.broadcast_to(place, (PACKED, NBLK)), 0), axis=1, keepdims=True)
    at = jnp.where(blk < 0, -1, at)
    at_col[...] = jnp.broadcast_to(at, (PACKED, 128))
    same = iota((PACKED, PACKED), 0) == iota((PACKED, PACKED), 1)
    row = jnp.sum(jnp.where(same, jnp.broadcast_to(at, (PACKED, PACKED)), 0), axis=0, keepdims=True)
    at_row[...] = jnp.broadcast_to(row, (8, PACKED))


def gather_blocks(at_col, slots, out):
    shape = (PACKED, slots.shape[0])
    pick = onehot(jnp.broadcast_to(at_col[:, 0:1], shape) == iota(shape, 1))
    got = dot(pick, slots[...]).astype(BF16)
    got = dot(got, gate_order(0)).astype(BF16)
    for n in range(8):
        out[n] = got


def sum_cores(kept, got, *outs):
    i = 2 * lax.axis_index("tm") + ((lax.axis_index("chan") >> 1) & 1)
    for k, out in enumerate(outs):
        out[...] = (kept[i ^ k].astype(F32) + got[i ^ k].astype(F32)).astype(BF16)


def scatter_blocks(at_row, p0, p1, p2, p3, out):
    total = p0[...].astype(F32)
    for part in (p1, p2, p3):
        total = total + part[...].astype(F32)
    natural = dot(total.astype(BF16), gate_order(1)).astype(BF16)
    shape = (out.shape[1], PACKED)
    put = onehot(jnp.broadcast_to(at_row[0:1, :], shape) == iota(shape, 0))
    spread = dot(put, natural).astype(BF16)
    out[0] = spread
    out[1] = spread


def sum_units(z0, z1, z2, z3, o0, o1, o2, o3):
    for i, out in enumerate((o0, o1, o2, o3)):
        out[...] = (
            z0[i].astype(F32) + z1[i].astype(F32) + z2[i].astype(F32) + z3[i].astype(F32)
        ).astype(BF16)


def channel_of(pos, ch):
    return ((pos >> 5) ^ ch) * 32 + (pos & 31)


def to_major(ch, dim):
    shape = (RESID, RESID)
    major = iota(shape, dim)
    return onehot(channel_of(iota(shape, 1 - dim), ch) == 8 * (major & 63) + (major >> 6))


def prepare(spk, p0, p1, p2, p3, mel, other, features, res, skp):
    half, ch = lax.axis_index("tm"), lax.axis_index("chan")
    j = ch & 3
    got = (p0, p1, p2, p3)
    tokens, wide = 256, 384
    order = to_major(ch, 0)

    def stacked(n):
        return jnp.concatenate(
            [got[k][96 * i + 32 * n : 96 * i + 32 * n + 32, :] for k in range(4) for i in range(4)], 0
        )

    ends = [part[384:400, :].astype(F32) for part in got]
    ends = [jnp.concatenate([e[:, 128 * n : 128 * n + 128] for e in ends], 1) for n in range(2)]
    gap = jnp.zeros((120, RESID), F32)
    ends = jnp.concatenate(
        [ends[0][8:16], gap[:112], ends[0][0:8], ends[1][0:8], gap, ends[1][8:16], gap], 0
    ).astype(BF16)
    ends = dot(order, ends, NT)
    sig = jnp.concatenate([dot(order, stacked(0)), ends[:, 0:128]], 1)
    res[...] = jnp.concatenate([dot(order, stacked(1)), ends[:, 128:256]], 1).astype(BF16)
    skp[...] = jnp.concatenate([dot(order, stacked(2)), ends[:, 256:384]], 1).astype(BF16)
    shifted = pltpu.roll(sig, DILATION, 1).astype(BF16)
    sig = sig.astype(BF16)
    m = iota((128, MELS), 0)
    mel_pick = onehot(((m & 15) < MEL_BLOCKS) & (iota((128, MELS), 1) == 8 * (m & 15) + (m >> 4)))
    cut = pl.ds(pl.multiple_of(j * tokens, tokens), tokens)
    far = pl.ds(pl.multiple_of(jnp.minimum(j * tokens + tokens, 896), 128), 128)
    ahead = jnp.where(j == 3, other[96:176, :].astype(F32), mel[:, far].astype(F32)).astype(BF16)
    mels = jnp.concatenate([dot(mel_pick, mel[:, cut]), dot(mel_pick, ahead)], 1).astype(BF16)
    seg = 8 * half + 2 * j
    row, lane = iota((16, wide), 0), iota((16, wide), 1)
    beyond = other[176:192, :].astype(F32)[1:2, 0:1].astype(jnp.int32)
    beyond = jnp.where(j == 3, beyond, spk[jnp.minimum(2 * j + 2, 7)] & 7)
    sub = jnp.where(
        lane < SEG,
        spk[2 * j] & 7,
        jnp.where(lane < 2 * SEG, spk[2 * j + 1] & 7, jnp.broadcast_to(beyond, (16, wide))),
    )
    for r in range(8):
        features[r, 0:64] = shifted[64 * r : 64 * r + 64]
        features[r, 64:128] = sig[64 * r : 64 * r + 64]
        features[r, 128:144] = mels[16 * r : 16 * r + 16]
        features[r, 144:160] = onehot((row == seg + (lane >> 7)) & (sub == r))


def layer(packed, feat, res, skp, kept, given, z0, z1, z2, z3):
    tokens, wide = 256, 384
    to_place = to_major(lax.axis_index("chan"), 1)
    features = feat[...].reshape(8 * OUT_AT, wide)
    conv = packed[:, 0:OUT_AT, :].reshape(8 * OUT_AT, 256)
    pre = dot(conv, features, TN)
    filt = jnp.tanh(pre[:128])
    gate = jax.nn.sigmoid(pre[128:])
    hidden = (filt[:, :tokens] * gate[:, :tokens]).astype(BF16)
    out_res = packed[:, OUT_AT:PACKED, 0:128].reshape(RESID, 128)
    out_skp = packed[:, OUT_AT:PACKED, 128:256].reshape(RESID, 128)
    res_part = dot(out_res, hidden).astype(BF16)
    skp_part = dot(out_skp, hidden).astype(BF16)
    grad_hidden = dot(out_res, res[...], TN) + dot(out_skp, skp[...], TN)
    grad_pre = jnp.concatenate(
        [
            grad_hidden * gate * (1.0 - filt * filt),
            grad_hidden * filt * gate * (1.0 - gate),
        ],
        0,
    ).astype(BF16)
    prev = packed[:, 0:64, :].reshape(RESID, 256)
    now = packed[:, 64:128, :].reshape(RESID, 256)
    later = pltpu.roll(dot(prev, grad_pre), wide - DILATION, 1)[:, :tokens]
    grad_pre = grad_pre[:, :tokens]
    in_part = (dot(now, grad_pre) + later).astype(BF16)
    conv_grad = dot(features[:, :tokens], grad_pre, NT).astype(BF16)
    res_grad = dot(res[:, :tokens], hidden, NT).astype(BF16)
    skp_grad = dot(skp[:, :tokens], hidden, NT).astype(BF16)
    core = lax.axis_index("chan") & 1
    for part, rows, cols in (
        (conv_grad.reshape(8, OUT_AT, 256), slice(0, OUT_AT), slice(0, 256)),
        (res_grad.reshape(8, 64, 128), slice(OUT_AT, PACKED), slice(0, 128)),
        (skp_grad.reshape(8, 64, 128), slice(OUT_AT, PACKED), slice(128, 256)),
    ):
        for i in range(4):
            even, odd = part[2 * i], part[2 * i + 1]
            kept[i, rows, cols] = jnp.where(core == 0, even, odd)
            given[i, rows, cols] = jnp.where(core == 0, odd, even)
    parts = [dot(to_place, part).astype(BF16) for part in (res_part, skp_part, in_part)]
    for k, out in enumerate((z0, z1, z2, z3)):
        for i in range(4):
            at = 128 * k + 32 * i
            for n in range(3):
                out[i, 32 * n : 32 * n + 32] = parts[n][at : at + 32]


def finish_tokens(o0, o1, o2, o3, sig, res, residual, skipped, grad_in):
    j = lax.axis_index("chan") & 3
    for k, piece in enumerate((o0, o1, o2, o3)):
        cut = pl.ds(pl.multiple_of((j ^ k) * 256, 256), 256)
        residual[:, cut] = sig[:, cut].astype(F32) + piece[0:32, :].astype(F32)
        skipped[:, cut] = piece[32:64, :].astype(F32)
        grad_in[:, cut] = res[:, cut].astype(F32) + piece[64:96, :].astype(F32)


def update(owned, grads, master, first, second, *refs):
    outs, held, old, grad, sems = refs[:3], refs[3:6], refs[6:9], refs[9], refs[10]
    slots = grads.shape[1]
    rows = 8 * slots
    parts = [slice(n * rows // 4, (n + 1) * rows // 4) for n in range(4)]
    fetches = []
    for n, part in enumerate(parts):
        for m, source in enumerate((first, second, master)):
            fetch = pltpu.make_async_copy(
                source.at[part, :], old[m].at[part, :], sems.at[12 + 3 * n + m]
            )
            fetch.start()
            fetches.append(fetch)
    to, of = iota((rows, rows), 0), iota((rows, rows), 1)
    spread = jnp.zeros((rows, rows), jnp.bool_)
    for r in range(8):
        inside = (of >= r * slots) & (of < (r + 1) * slots)
        spread = spread | (inside & (to == 8 * (of - r * slots) + r))
    spread = onehot(spread)
    for z in range(4):
        got = jnp.concatenate(
            [grads[16 * (r // 4) + 4 * z + r % 4].astype(F32) for r in range(8)], 0
        )
        grad[:, 256 * z : 256 * z + 256] = dot(spread, got.astype(BF16))
    copies = []
    for n, part in enumerate(parts):
        for m in range(3):
            fetches[3 * n + m].wait()
        old_f, old_s, old_m = (ref[part, :] for ref in old)
        new = grad[part, :]
        keep = n * (rows // 4) + iota((rows // 4, 1), 0) < 8 * owned[0:1, 0:1]
        first_new = MOMENT_DECAY * old_f + (1.0 - MOMENT_DECAY) * new
        second_new = MOMENT_DECAY * old_s + (1.0 - MOMENT_DECAY) * new * new
        first_hat = first_new / (1.0 - MOMENT_DECAY**STEP)
        second_hat = second_new / (1.0 - MOMENT_DECAY**STEP)
        stepped = old_m - STEP_RATE * (
            first_hat / (jnp.sqrt(second_hat) + EPSILON) + WEIGHT_DECAY * old_m
        )
        held[0][part, :] = jnp.where(keep, first_new, old_f)
        held[1][part, :] = jnp.where(keep, second_new, old_s)
        held[2][part, :] = jnp.where(keep, stepped, old_m)
        for m in range(3):
            copy = pltpu.make_async_copy(
                held[m].at[part, :], outs[m].at[part, :], sems.at[3 * n + m]
            )
            copy.start()
            copies.append(copy)
    for copy in copies:
        copy.wait()


BOTH = ("tm", "chan")


def swap(x, k):
    n = lax.axis_size("chan")
    return lax.ppermute(x, "chan", [(i, i ^ k) for i in range(n)])


def local(
    signal, mel_frames, speaker_ids, owners, master, first_moment, second_moment, res_cot, skip_cot
):
    slots_dev = master.shape[0]
    slots = 16 * slots_dev
    sig, res, skp, mel = signal.T, res_cot.T, skip_cot.T, mel_frames.T
    own_row = owners.reshape(1, NBLK)
    share = [[16 * y + 4 * z + j for y in range(2) for j in range(4)] for z in range(4)]
    sds = jax.ShapeDtypeStruct
    dma = pltpu.SemaphoreType.DMA

    sent, edges = call(
        begin,
        (sds((16, slots_dev, 256), BF16), sds((192, 128), BF16)),
        (HBM,) * 6,
        scratch=(
            pltpu.VMEM((4, slots_dev, 8, 256), F32),
            pltpu.SMEM(speaker_ids.shape, jnp.int32),
            dma((9,)),
        ),
    )(speaker_ids, master, sig, res, skp, mel)
    other = lax.ppermute(edges, "tm", [(0, 1), (1, 0)])
    arrived = lax.all_to_all(sent, "chan", 0, 0, tiled=True)
    piece = sds((PIECE, 256), BF16)
    o = call(
        pack_tokens,
        (piece,) * 4,
        (HBM,) * 3 + (VMEM,),
        gflops=200,
        scratch=(pltpu.VMEM((3, *sig.shape), BF16), dma((3,))),
    )(sig, res, skp, other)
    mine = call(join, sds((400, 256), BF16), (VMEM,) * 4)(
        o[0], swap(o[1], 1), swap(o[2], 2), swap(o[3], 3)
    )
    p1, p2, p3 = (swap(mine, 4 * k) for k in (1, 2, 3))

    at_col, at_row, owned = call(
        functools.partial(place_blocks, slots_dev=slots_dev),
        (
            sds((PACKED, 128), jnp.int32),
            sds((8, PACKED), jnp.int32),
            sds((8, 128), jnp.int32),
        ),
        (SMEM, VMEM, VMEM),
    )(speaker_ids, own_row, other)
    arrived, _ = lax.optimization_barrier((arrived, mine))
    gathered = call(gather_blocks, sds((8, PACKED, 256), BF16), (VMEM, VMEM))(
        at_col, arrived.reshape(slots, 256)
    )
    packed = lax.all_to_all(gathered, BOTH, 0, 0, axis_index_groups=share)
    cots = sds((RESID, 384), BF16)
    ready = call(
        prepare,
        (sds((8, OUT_AT, 384), BF16), cots, cots),
        (SMEM,) + (VMEM,) * 6,
        gflops=200,
    )(speaker_ids, mine, p1, p2, p3, mel, other)

    quad = sds((4, 96, 256), BF16)
    rows = sds((4, PACKED, 256), BF16)
    kept, given, z0, z1, z2, z3 = call(layer, (rows, rows, quad, quad, quad, quad), (VMEM,) * 4)(
        packed, *ready
    )

    n = lax.axis_size("chan")
    g = call(sum_cores, (sds((PACKED, 256), BF16),) * 4, (VMEM,) * 2)(kept, swap(given, 1))
    across = [(16 * y + i, 16 * (1 - y) + (i ^ 2)) for y in range(2) for i in range(n)]
    g = (g[0], swap(g[1], 2), lax.ppermute(g[2], "tm", [(0, 1), (1, 0)]), lax.ppermute(g[3], BOTH, across))
    t1, t2, t3 = (swap(z, 4 * k) for k, z in ((1, z1), (2, z2), (3, z3)))
    spread = call(scatter_blocks, sds((2, slots, 256), BF16), (VMEM,) * 5)(at_row, *g)
    returned = lax.all_to_all(spread.reshape(32, slots_dev, 256), BOTH, 0, 0)
    o = call(sum_units, (sds((96, 256), BF16),) * 4, (VMEM,) * 4, gflops=20)(z0, t1, t2, t3)
    o = (o[0], swap(o[1], 1), swap(o[2], 2), swap(o[3], 3))
    narrow = sds(sig.shape, F32)
    residual, skipped, grad_in = call(finish_tokens, (narrow,) * 3, (VMEM,) * 6)(*o, sig, res)
    flat = (8 * slots_dev, GATES)
    new = call(
        update,
        (sds(flat, F32),) * 3,
        (VMEM, VMEM, HBM, HBM, HBM),
        scratch=(pltpu.VMEM(flat, F32),) * 7 + (dma((24,)),),
        out_space=HBM,
    )(
        owned,
        returned,
        master.reshape(flat),
        first_moment.reshape(flat),
        second_moment.reshape(flat),
    )
    return (residual.T, skipped.T, grad_in.T, *(x.reshape(master.shape) for x in new))


def place_index(owners, slots_dev):
    count = owners.shape[0]
    matches = owners[:, None] == owners[None, :]
    before = jnp.arange(count)[None, :] < jnp.arange(count)[:, None]
    ranks = jnp.sum((matches & before).astype(jnp.int32), axis=1)
    return owners * slots_dev + ranks


def local_plain(
    signal, mel_frames, speaker_ids, owners, master, first_moment, second_moment, res_cot, skip_cot
):
    chans = lax.axis_size("chan")
    slots_dev = master.shape[0]
    tok_count = signal.shape[0]
    hid_local = HIDDEN_SIZE // chans
    col_count = GATES // chans
    seg_count = speaker_ids.shape[0]
    spk_start = 2 * RESID + MELS
    out_start = spk_start + SPEAKERS
    places = place_index(owners, slots_dev)
    table = places[:, None] == jnp.arange(chans * slots_dev)[None, :]
    received = lax.all_to_all(
        master.astype(BF16), "chan", split_axis=2, concat_axis=0, tiled=True
    ).reshape(chans * slots_dev, BLOCK * col_count)
    params = jnp.dot(table.astype(BF16), received, preferred_element_type=F32)
    params = params.astype(BF16).reshape(ROWS, col_count)
    tap_prev, tap_now = params[:RESID], params[RESID : 2 * RESID]
    mel_proj = params[2 * RESID : spk_start]
    speaker_table = params[spk_start:out_start]
    out_cols = params[out_start:].reshape(RESID, hid_local, 2)
    n_tm = lax.axis_size("tm")
    tail_prev = lax.ppermute(signal[-DILATION:], "tm", [(i, i + 1) for i in range(n_tm - 1)])
    inputs = lax.all_gather(signal, "chan", axis=1, tiled=True)
    tail_full = lax.all_gather(tail_prev, "chan", axis=1, tiled=True)
    shifted = jnp.concatenate([tail_full, inputs[:-DILATION]], 0)
    pre_act = jnp.dot(shifted, tap_prev, preferred_element_type=F32)
    pre_act = pre_act + jnp.dot(inputs, tap_now, preferred_element_type=F32)
    pre_act = pre_act + jnp.dot(mel_frames, mel_proj, preferred_element_type=F32)
    one_hot = (speaker_ids[:, None] == jnp.arange(SPEAKERS)[None, :]).astype(BF16)
    embedded = jnp.dot(one_hot, speaker_table, preferred_element_type=F32)
    pre_act = (pre_act.reshape(seg_count, SEG, col_count) + embedded[:, None, :]).reshape(
        tok_count, col_count
    )
    filt = jnp.tanh(pre_act[:, 0::2])
    gates = jax.nn.sigmoid(pre_act[:, 1::2])
    hidden = (filt * gates).astype(BF16)
    summed = lax.psum_scatter(
        jnp.einsum("cuw,tu->cwt", out_cols, hidden, preferred_element_type=F32),
        "chan",
        scatter_dimension=0,
        tiled=True,
    )
    cots = lax.all_gather(
        jnp.stack([res_cot.T, skip_cot.T], axis=1), "chan", axis=0, tiled=True
    )
    grad_hid = jnp.einsum("cwt,cuw->tu", cots, out_cols, preferred_element_type=F32)
    term = jnp.einsum("cwt,tu->cuw", cots, hidden, preferred_element_type=F32)
    grad_filt = grad_hid * gates * (1.0 - filt * filt)
    grad_gate = grad_hid * filt * gates * (1.0 - gates)
    grad_pre = (
        jnp.stack([grad_filt, grad_gate], axis=2).reshape(tok_count, col_count).astype(BF16)
    )
    ahead = lax.ppermute(grad_pre[:DILATION], "tm", [(i + 1, i) for i in range(n_tm - 1)])
    later = jnp.concatenate([grad_pre[DILATION:], ahead], 0)
    input_part = lax.psum_scatter(
        dot(tap_now, grad_pre, NT) + dot(tap_prev, later, NT),
        "chan",
        scatter_dimension=0,
        tiled=True,
    )
    seg_sums = jnp.sum(grad_pre.astype(F32).reshape(seg_count, SEG, col_count), axis=1)
    grad_spk = lax.dot_general(
        one_hot.astype(F32),
        seg_sums,
        TN,
        precision=lax.Precision.HIGHEST,
        preferred_element_type=F32,
    )
    grad_params = jnp.concatenate(
        [
            dot(shifted, grad_pre, TN),
            dot(inputs, grad_pre, TN),
            dot(mel_frames, grad_pre, TN),
            grad_spk,
            term.reshape(RESID, col_count),
        ],
        0,
    )
    grad_params = lax.psum(grad_params, "tm").reshape(NBLK, BLOCK * col_count)
    outgoing = lax.dot_general(
        table.astype(F32), grad_params, TN, precision=lax.Precision.HIGHEST
    ).reshape(chans * slots_dev, BLOCK, col_count)
    grad_slots = lax.all_to_all(outgoing, "chan", split_axis=0, concat_axis=2, tiled=True)
    owned = jnp.sum((owners == lax.axis_index("chan")).astype(jnp.int32))
    keep = (jnp.arange(slots_dev) < owned)[:, None, None]
    first_new = MOMENT_DECAY * first_moment + (1.0 - MOMENT_DECAY) * grad_slots
    second_new = MOMENT_DECAY * second_moment + (1.0 - MOMENT_DECAY) * grad_slots * grad_slots
    first_hat = first_new / (1.0 - MOMENT_DECAY**STEP)
    second_hat = second_new / (1.0 - MOMENT_DECAY**STEP)
    stepped = master - STEP_RATE * (
        first_hat / (jnp.sqrt(second_hat) + EPSILON) + WEIGHT_DECAY * master
    )
    return (
        signal.astype(F32) + summed[:, 0, :].T,
        summed[:, 1, :].T,
        res_cot.astype(F32) + input_part.T,
        jnp.where(keep, first_new, first_moment),
        jnp.where(keep, second_new, second_moment),
        jnp.where(keep, stepped, master),
    )


def solution(mesh):
    wide = P("tm", "chan")
    slots = P("chan", None, None)
    packed_mesh = mesh.shape["tm"] == 2 and mesh.shape["chan"] == 16
    return jax.shard_map(
        local if packed_mesh else local_plain,
        mesh=mesh,
        in_specs=(wide, P("tm", None), P("tm"), P(), slots, slots, slots, wide, wide),
        out_specs=(wide, wide, wide, slots, slots, slots),
        check_vma=False,
    )
```

```python
import functools

import jax
import jax.numpy as jnp
from jax import lax
from jax.experimental import pallas as pl
from jax.experimental.pallas import tpu as pltpu
from jax.sharding import PartitionSpec as P

RESID = 512
HIDDEN_SIZE = 512
MELS = 80
SPEAKERS = 944
DILATION = 8
SEG = 128
BLOCK = 8
STEP = 5
GATES = 1024
ROWS = 2560
NBLK = 320

MOMENT_DECAY = 0.5
STEP_RATE = 0.03
WEIGHT_DECAY = 0.01
EPSILON = 1e-08

F32 = jnp.float32
BF16 = jnp.bfloat16
NN = (((1,), (0,)), ((), ()))
NT = (((1,), (1,)), ((), ()))
TN = (((0,), (0,)), ((), ()))

TAPS = 2 * RESID // BLOCK
MEL_AT = TAPS
MEL_BLOCKS = MELS // BLOCK
SEG_AT = 144
OUT_AT = 160
PACKED = 224
SPK_BLOCK = TAPS + MEL_BLOCKS
OUT_BLOCK = SPK_BLOCK + SPEAKERS // BLOCK
PIECE = 112


def dot(a, b, dims=NN):
    return lax.dot_general(a, b, dims, preferred_element_type=F32)


def iota(shape, dim):
    return lax.broadcasted_iota(jnp.int32, shape, dim)


def onehot(cond):
    return jnp.where(cond, 1.0, 0.0).astype(BF16)


KIB, MIB = 2**10, 2**20
VMEM, SMEM, HBM = pltpu.VMEM, pltpu.SMEM, pltpu.HBM


def call(kernel, out, spaces, gflops=0, scratch=(), out_space=VMEM):
    run = pl.pallas_call(
        kernel,
        out_shape=out,
        in_specs=[pl.BlockSpec(memory_space=space) for space in spaces],
        out_specs=jax.tree.map(lambda _: pl.BlockSpec(memory_space=out_space), out),
        scratch_shapes=list(scratch),
        compiler_params=pltpu.CompilerParams(vmem_limit_bytes=24 * MIB),
        cost_estimate=pl.CostEstimate(
            flops=gflops * 10**9, bytes_accessed=MIB, transcendentals=0
        ),
    )
    pin = pltpu.with_memory_space_constraint
    return lambda *args: run(*(pin(x, HBM) if space == HBM else x for x, space in zip(args, spaces, strict=True)))


def gate_order(dim):
    natural, split = iota((256, 256), dim), iota((256, 256), 1 - dim)
    return onehot(natural == 2 * (split & 127) + (split >> 7))


def begin(speakers, master, sig, res, skp, mel, sent, edges, strips, spk, sems):
    half = lax.axis_index("tm")
    slots = master.shape[0]
    rows = 4 * slots
    cut = pl.ds(pl.multiple_of((1 - half) * 896, 128), 128)
    tiles = []
    for n, part in enumerate((sig, res, skp, mel)):
        to = edges.at[32 * n : 32 * n + part.shape[0], :]
        tiles.append(pltpu.make_async_copy(part.at[:, cut], to, sems.at[4 + n]))
    copies = []
    for z in range(4):
        part = master.at[:, :, 256 * z : 256 * z + 256]
        copies.append(pltpu.make_async_copy(part, strips.at[z], sems.at[z]))
    names = pltpu.make_async_copy(speakers, spk, sems.at[8])
    for copy in (names, *copies, *tiles):
        copy.start()
    names.wait()
    row, lane = iota((16, 128), 0), iota((16, 128), 1)
    table = jnp.zeros((16, 128), jnp.int32)
    for s in range(8):
        code = jnp.where(row == 0, spk[s] >> 3, spk[s] & 7)
        table = jnp.where((lane == s) & (row < 2), code, table)
    edges[176:192, :] = table.astype(F32).astype(BF16)
    here = iota((rows, 8 * slots), 0)
    there = iota((rows, 8 * slots), 1)
    row, slot = jnp.zeros_like(here), here
    for step in range(1, 4):
        past = here >= step * slots
        row = jnp.where(past, step, row)
        slot = jnp.where(past, here - step * slots, slot)
    pick = onehot(there == 8 * slot + 4 * half + row)
    for z in range(4):
        copies[z].wait()
        got = dot(pick, strips[z].reshape(8 * slots, 256).astype(BF16))
        for j in range(4):
            sent[4 * z + j] = got[j * slots : (j + 1) * slots].astype(BF16)
    for tile in tiles:
        tile.wait()


def pack_tokens(sig_hbm, res_hbm, skp_hbm, other, o0, o1, o2, o3, held, sems):
    copies = [
        pltpu.make_async_copy(part, held.at[n], sems.at[n])
        for n, part in enumerate((sig_hbm, res_hbm, skp_hbm))
    ]
    for copy in copies:
        copy.start()
    for copy in copies:
        copy.wait()
    sig, res, skp = (held.at[n] for n in range(3))
    half, j = lax.axis_index("tm"), lax.axis_index("chan") & 3
    outs = (o0, o1, o2, o3)
    parts = (sig, res, skp)
    befores, nexts = [], ([], [], [])
    for k in range(4):
        to = j ^ k
        cut = pl.ds(pl.multiple_of(to * 256, 256), 256)
        for n, part in enumerate(parts):
            outs[k][32 * n : 32 * n + 32, :] = part[:, cut]
        cut = pl.ds(pl.multiple_of(jnp.maximum(to * 256 - 128, 0), 128), 128)
        edge = jnp.where(half == 1, other[0:32, :].astype(F32), 0.0)
        befores.append(jnp.where(to == 0, edge, sig[:, cut].astype(F32)))
        cut = pl.ds(pl.multiple_of(jnp.minimum(to * 256 + 256, 896), 128), 128)
        for n, part in enumerate(parts):
            edge = jnp.where(half == 0, other[32 * n : 32 * n + 32, :].astype(F32), 0.0)
            nexts[n].append(jnp.where(to == 3, edge, part[:, cut].astype(F32)))
    tall = [jnp.concatenate(x, 0).astype(BF16) for x in (befores, *nexts)]
    t, lane = iota((16, 128), 0), iota((16, 128), 1)
    top, low = t < DILATION, t >= DILATION
    head_top = onehot(top & (lane == t))
    head_low = onehot(low & (lane == t - DILATION))
    last_top = onehot(top & (lane == t + 120))
    rows = (
        dot(last_top, tall[0], NT) + dot(head_low, tall[1], NT),
        dot(head_top, tall[2], NT) + dot(head_low, tall[3], NT),
    )
    for k in range(4):
        for n in range(2):
            outs[k][96:112, 128 * n : 128 * n + 128] = jnp.where(
                (lane >> 5) == k, rows[n], 0.0
            ).astype(BF16)


def join(o0, o1, o2, o3, out):
    ends = o0[96:112, :].astype(F32)
    for piece in (o1, o2, o3):
        ends = ends + piece[96:112, :].astype(F32)
    for k, piece in enumerate((o0, o1, o2, o3)):
        out[96 * k : 96 * k + 96, :] = piece[0:96, :]
    out[384:400, :] = ends.astype(BF16)


def place_blocks(spk_ids, owners, other, at_col, at_row, owned, *, slots_dev):
    half = lax.axis_index("tm")
    own_row = owners[...]
    mine = jnp.where(own_row == lax.axis_index("chan"), 1, 0)
    owned[...] = jnp.broadcast_to(jnp.sum(mine, axis=1, keepdims=True), owned.shape)
    down, across = iota((NBLK, NBLK), 0), iota((NBLK, NBLK), 1)
    row_all = jnp.broadcast_to(own_row, (NBLK, NBLK))
    own_col = jnp.sum(jnp.where(down == across, row_all, 0), axis=1, keepdims=True)
    before = (own_col == row_all) & (down < across)
    rank = jnp.sum(jnp.where(before, 1, 0), axis=0, keepdims=True)
    place = own_row * slots_dev + rank
    n = iota((PACKED, 128), 0)
    far = n - SEG_AT - 8 * (1 - half) == iota((PACKED, 128), 1)
    blocks = jnp.broadcast_to(other[176:192, :].astype(F32)[0:1], (PACKED, 128))
    spk = jnp.sum(jnp.where(far, blocks, 0.0), axis=1, keepdims=True).astype(jnp.int32)
    n = iota((PACKED, 1), 0)
    for s in range(8):
        spk = jnp.where(n == SEG_AT + 8 * half + s, spk_ids[s] >> 3, spk)
    blk = jnp.where(
        n < SPK_BLOCK,
        n,
        jnp.where(n < SEG_AT, -1, jnp.where(n < OUT_AT, SPK_BLOCK + spk, n + (OUT_BLOCK - OUT_AT))),
    )
    match = jnp.broadcast_to(blk, (PACKED, NBLK)) == iota((PACKED, NBLK), 1)
    at = jnp.sum(jnp.where(match, jnp.broadcast_to(place, (PACKED, NBLK)), 0), axis=1, keepdims=True)
    at = jnp.where(blk < 0, -1, at)
    at_col[...] = jnp.broadcast_to(at, (PACKED, 128))
    same = iota((PACKED, PACKED), 0) == iota((PACKED, PACKED), 1)
    row = jnp.sum(jnp.where(same, jnp.broadcast_to(at, (PACKED, PACKED)), 0), axis=0, keepdims=True)
    at_row[...] = jnp.broadcast_to(row, (8, PACKED))


def gather_blocks(at_col, slots, out):
    shape = (PACKED, slots.shape[0])
    pick = onehot(jnp.broadcast_to(at_col[:, 0:1], shape) == iota(shape, 1))
    got = dot(pick, slots[...]).astype(BF16)
    out[...] = dot(got, gate_order(0)).astype(BF16)


def sum_cores(kept, got, *outs):
    i = 2 * lax.axis_index("tm") + ((lax.axis_index("chan") >> 1) & 1)
    for k, out in enumerate(outs):
        out[...] = (kept[i ^ k].astype(F32) + got[i ^ k].astype(F32)).astype(BF16)


def scatter_blocks(at_row, p0, p1, p2, p3, out):
    total = p0[...].astype(F32)
    for part in (p1, p2, p3):
        total = total + part[...].astype(F32)
    natural = dot(total.astype(BF16), gate_order(1)).astype(BF16)
    shape = (out.shape[1], PACKED)
    put = onehot(jnp.broadcast_to(at_row[0:1, :], shape) == iota(shape, 0))
    spread = dot(put, natural).astype(BF16)
    out[0] = spread
    out[1] = spread


def sum_units(z0, z1, z2, z3, o0, o1, o2, o3):
    for i, out in enumerate((o0, o1, o2, o3)):
        out[...] = (
            z0[i].astype(F32) + z1[i].astype(F32) + z2[i].astype(F32) + z3[i].astype(F32)
        ).astype(BF16)


def channel_of(pos, ch):
    return ((pos >> 5) ^ ch) * 32 + (pos & 31)


def to_major(ch, dim):
    shape = (RESID, RESID)
    major = iota(shape, dim)
    return onehot(channel_of(iota(shape, 1 - dim), ch) == 8 * (major & 63) + (major >> 6))


def prepare(spk, p0, p1, p2, p3, mel, other, features, res, skp):
    half, ch = lax.axis_index("tm"), lax.axis_index("chan")
    j = ch & 3
    got = (p0, p1, p2, p3)
    tokens, wide = 256, 384
    order = to_major(ch, 0)

    def stacked(n):
        return jnp.concatenate(
            [got[k][96 * i + 32 * n : 96 * i + 32 * n + 32, :] for k in range(4) for i in range(4)], 0
        )

    ends = [part[384:400, :].astype(F32) for part in got]
    ends = [jnp.concatenate([e[:, 128 * n : 128 * n + 128] for e in ends], 1) for n in range(2)]
    gap = jnp.zeros((120, RESID), F32)
    ends = jnp.concatenate(
        [ends[0][8:16], gap[:112], ends[0][0:8], ends[1][0:8], gap, ends[1][8:16], gap], 0
    ).astype(BF16)
    ends = dot(order, ends, NT)
    sig = jnp.concatenate([dot(order, stacked(0)), ends[:, 0:128]], 1)
    res[...] = jnp.concatenate([dot(order, stacked(1)), ends[:, 128:256]], 1).astype(BF16)
    skp[...] = jnp.concatenate([dot(order, stacked(2)), ends[:, 256:384]], 1).astype(BF16)
    shifted = pltpu.roll(sig, DILATION, 1).astype(BF16)
    sig = sig.astype(BF16)
    m = iota((128, MELS), 0)
    mel_pick = onehot(((m & 15) < MEL_BLOCKS) & (iota((128, MELS), 1) == 8 * (m & 15) + (m >> 4)))
    cut = pl.ds(pl.multiple_of(j * tokens, tokens), tokens)
    far = pl.ds(pl.multiple_of(jnp.minimum(j * tokens + tokens, 896), 128), 128)
    ahead = jnp.where(j == 3, other[96:176, :].astype(F32), mel[:, far].astype(F32)).astype(BF16)
    mels = jnp.concatenate([dot(mel_pick, mel[:, cut]), dot(mel_pick, ahead)], 1).astype(BF16)
    seg = 8 * half + 2 * j
    row, lane = iota((16, wide), 0), iota((16, wide), 1)
    beyond = other[176:192, :].astype(F32)[1:2, 0:1].astype(jnp.int32)
    beyond = jnp.where(j == 3, beyond, spk[jnp.minimum(2 * j + 2, 7)] & 7)
    sub = jnp.where(
        lane < SEG,
        spk[2 * j] & 7,
        jnp.where(lane < 2 * SEG, spk[2 * j + 1] & 7, jnp.broadcast_to(beyond, (16, wide))),
    )
    for r in range(8):
        features[r, 0:64] = shifted[64 * r : 64 * r + 64]
        features[r, 64:128] = sig[64 * r : 64 * r + 64]
        features[r, 128:144] = mels[16 * r : 16 * r + 16]
        features[r, 144:160] = onehot((row == seg + (lane >> 7)) & (sub == r))


def layer(packed, feat, res, skp, kept, given, z0, z1, z2, z3):
    tokens, wide = 256, 384
    to_place = to_major(lax.axis_index("chan"), 1)
    features = feat[...].reshape(8 * OUT_AT, wide)
    conv = packed[:, 0:OUT_AT, :].reshape(8 * OUT_AT, 256)
    pre = dot(conv, features, TN)
    filt = jnp.tanh(pre[:128])
    gate = jax.nn.sigmoid(pre[128:])
    hidden = (filt[:, :tokens] * gate[:, :tokens]).astype(BF16)
    out_res = packed[:, OUT_AT:PACKED, 0:128].reshape(RESID, 128)
    out_skp = packed[:, OUT_AT:PACKED, 128:256].reshape(RESID, 128)
    res_part = dot(out_res, hidden).astype(BF16)
    skp_part = dot(out_skp, hidden).astype(BF16)
    grad_hidden = dot(out_res, res[...], TN) + dot(out_skp, skp[...], TN)
    grad_pre = jnp.concatenate(
        [
            grad_hidden * gate * (1.0 - filt * filt),
            grad_hidden * filt * gate * (1.0 - gate),
        ],
        0,
    ).astype(BF16)
    prev = packed[:, 0:64, :].reshape(RESID, 256)
    now = packed[:, 64:128, :].reshape(RESID, 256)
    later = pltpu.roll(dot(prev, grad_pre), wide - DILATION, 1)[:, :tokens]
    grad_pre = grad_pre[:, :tokens]
    in_part = (dot(now, grad_pre) + later).astype(BF16)
    conv_grad = dot(features[:, :tokens], grad_pre, NT).astype(BF16)
    res_grad = dot(res[:, :tokens], hidden, NT).astype(BF16)
    skp_grad = dot(skp[:, :tokens], hidden, NT).astype(BF16)
    core = lax.axis_index("chan") & 1
    for part, rows, cols in (
        (conv_grad.reshape(8, OUT_AT, 256), slice(0, OUT_AT), slice(0, 256)),
        (res_grad.reshape(8, 64, 128), slice(OUT_AT, PACKED), slice(0, 128)),
        (skp_grad.reshape(8, 64, 128), slice(OUT_AT, PACKED), slice(128, 256)),
    ):
        for i in range(4):
            even, odd = part[2 * i], part[2 * i + 1]
            kept[i, rows, cols] = jnp.where(core == 0, even, odd)
            given[i, rows, cols] = jnp.where(core == 0, odd, even)
    parts = [dot(to_place, part).astype(BF16) for part in (res_part, skp_part, in_part)]
    for k, out in enumerate((z0, z1, z2, z3)):
        for i in range(4):
            at = 128 * k + 32 * i
            for n in range(3):
                out[i, 32 * n : 32 * n + 32] = parts[n][at : at + 32]


def finish_tokens(o0, o1, o2, o3, sig, res, residual, skipped, grad_in):
    j = lax.axis_index("chan") & 3
    for k, piece in enumerate((o0, o1, o2, o3)):
        cut = pl.ds(pl.multiple_of((j ^ k) * 256, 256), 256)
        residual[:, cut] = sig[:, cut].astype(F32) + piece[0:32, :].astype(F32)
        skipped[:, cut] = piece[32:64, :].astype(F32)
        grad_in[:, cut] = res[:, cut].astype(F32) + piece[64:96, :].astype(F32)


def update(owned, grads, master, first, second, *refs):
    outs, held, old, grad, sems = refs[:3], refs[3:6], refs[6:9], refs[9], refs[10]
    slots = grads.shape[1]
    rows = 8 * slots
    parts = [slice(n * rows // 4, (n + 1) * rows // 4) for n in range(4)]
    fetches = []
    for n, part in enumerate(parts):
        for m, source in enumerate((first, second, master)):
            fetch = pltpu.make_async_copy(
                source.at[part, :], old[m].at[part, :], sems.at[12 + 3 * n + m]
            )
            fetch.start()
            fetches.append(fetch)
    to, of = iota((rows, rows), 0), iota((rows, rows), 1)
    spread = jnp.zeros((rows, rows), jnp.bool_)
    for r in range(8):
        inside = (of >= r * slots) & (of < (r + 1) * slots)
        spread = spread | (inside & (to == 8 * (of - r * slots) + r))
    spread = onehot(spread)
    for z in range(4):
        got = jnp.concatenate(
            [grads[16 * (r // 4) + 4 * z + r % 4].astype(F32) for r in range(8)], 0
        )
        grad[:, 256 * z : 256 * z + 256] = dot(spread, got.astype(BF16))
    copies = []
    for n, part in enumerate(parts):
        for m in range(3):
            fetches[3 * n + m].wait()
        old_f, old_s, old_m = (ref[part, :] for ref in old)
        new = grad[part, :]
        keep = n * (rows // 4) + iota((rows // 4, 1), 0) < 8 * owned[0:1, 0:1]
        first_new = MOMENT_DECAY * old_f + (1.0 - MOMENT_DECAY) * new
        second_new = MOMENT_DECAY * old_s + (1.0 - MOMENT_DECAY) * new * new
        first_hat = first_new / (1.0 - MOMENT_DECAY**STEP)
        second_hat = second_new / (1.0 - MOMENT_DECAY**STEP)
        stepped = old_m - STEP_RATE * (
            first_hat / (jnp.sqrt(second_hat) + EPSILON) + WEIGHT_DECAY * old_m
        )
        held[0][part, :] = jnp.where(keep, first_new, old_f)
        held[1][part, :] = jnp.where(keep, second_new, old_s)
        held[2][part, :] = jnp.where(keep, stepped, old_m)
        for m in range(3):
            copy = pltpu.make_async_copy(
                held[m].at[part, :], outs[m].at[part, :], sems.at[3 * n + m]
            )
            copy.start()
            copies.append(copy)
    for copy in copies:
        copy.wait()


BOTH = ("tm", "chan")


def swap(x, k):
    n = lax.axis_size("chan")
    return lax.ppermute(x, "chan", [(i, i ^ k) for i in range(n)])


def local(
    signal, mel_frames, speaker_ids, owners, master, first_moment, second_moment, res_cot, skip_cot
):
    slots_dev = master.shape[0]
    slots = 16 * slots_dev
    sig, res, skp, mel = signal.T, res_cot.T, skip_cot.T, mel_frames.T
    own_row = owners.reshape(1, NBLK)
    share = [[16 * y + 4 * z + j for y in range(2) for j in range(4)] for z in range(4)]
    sds = jax.ShapeDtypeStruct
    dma = pltpu.SemaphoreType.DMA

    sent, edges = call(
        begin,
        (sds((16, slots_dev, 256), BF16), sds((192, 128), BF16)),
        (HBM,) * 6,
        scratch=(
            pltpu.VMEM((4, slots_dev, 8, 256), F32),
            pltpu.SMEM(speaker_ids.shape, jnp.int32),
            dma((9,)),
        ),
    )(speaker_ids, master, sig, res, skp, mel)
    other = lax.ppermute(edges, "tm", [(0, 1), (1, 0)])
    arrived = lax.all_to_all(sent, "chan", 0, 0, tiled=True)
    piece = sds((PIECE, 256), BF16)
    o = call(
        pack_tokens,
        (piece,) * 4,
        (HBM,) * 3 + (VMEM,),
        gflops=200,
        scratch=(pltpu.VMEM((3, *sig.shape), BF16), dma((3,))),
    )(sig, res, skp, other)
    mine = call(join, sds((400, 256), BF16), (VMEM,) * 4)(
        o[0], swap(o[1], 1), swap(o[2], 2), swap(o[3], 3)
    )
    p1, p2, p3 = (swap(mine, 4 * k) for k in (1, 2, 3))

    at_col, at_row, owned = call(
        functools.partial(place_blocks, slots_dev=slots_dev),
        (
            sds((PACKED, 128), jnp.int32),
            sds((8, PACKED), jnp.int32),
            sds((8, 128), jnp.int32),
        ),
        (SMEM, VMEM, VMEM),
    )(speaker_ids, own_row, other)
    arrived, _ = lax.optimization_barrier((arrived, mine))
    gathered = call(gather_blocks, sds((PACKED, 256), BF16), (VMEM, VMEM), gflops=200)(
        at_col, arrived.reshape(slots, 256)
    )
    packed = lax.all_gather(gathered, BOTH, axis_index_groups=share)
    mel, _ = lax.optimization_barrier((mel, packed))
    cots = sds((RESID, 384), BF16)
    ready = call(
        prepare,
        (sds((8, OUT_AT, 384), BF16), cots, cots),
        (SMEM,) + (VMEM,) * 6,
        gflops=200,
    )(speaker_ids, mine, p1, p2, p3, mel, other)

    quad = sds((4, 96, 256), BF16)
    rows = sds((4, PACKED, 256), BF16)
    kept, given, z0, z1, z2, z3 = call(layer, (rows, rows, quad, quad, quad, quad), (VMEM,) * 4)(
        packed, *ready
    )

    n = lax.axis_size("chan")
    g = call(sum_cores, (sds((PACKED, 256), BF16),) * 4, (VMEM,) * 2)(kept, swap(given, 1))
    across = [(16 * y + i, 16 * (1 - y) + (i ^ 2)) for y in range(2) for i in range(n)]
    g = (g[0], swap(g[1], 2), lax.ppermute(g[2], "tm", [(0, 1), (1, 0)]), lax.ppermute(g[3], BOTH, across))
    t1, t2, t3 = (swap(z, 4 * k) for k, z in ((1, z1), (2, z2), (3, z3)))
    spread = call(scatter_blocks, sds((2, slots, 256), BF16), (VMEM,) * 5)(at_row, *g)
    returned = lax.all_to_all(spread.reshape(32, slots_dev, 256), BOTH, 0, 0)
    o = call(sum_units, (sds((96, 256), BF16),) * 4, (VMEM,) * 4, gflops=20)(z0, t1, t2, t3)
    o = (o[0], swap(o[1], 1), swap(o[2], 2), swap(o[3], 3))
    narrow = sds(sig.shape, F32)
    residual, skipped, grad_in = call(finish_tokens, (narrow,) * 3, (VMEM,) * 6)(*o, sig, res)
    flat = (8 * slots_dev, GATES)
    new = call(
        update,
        (sds(flat, F32),) * 3,
        (VMEM, VMEM, HBM, HBM, HBM),
        scratch=(pltpu.VMEM(flat, F32),) * 7 + (dma((24,)),),
        out_space=HBM,
    )(
        owned,
        returned,
        master.reshape(flat),
        first_moment.reshape(flat),
        second_moment.reshape(flat),
    )
    return (residual.T, skipped.T, grad_in.T, *(x.reshape(master.shape) for x in new))


def place_index(owners, slots_dev):
    count = owners.shape[0]
    matches = owners[:, None] == owners[None, :]
    before = jnp.arange(count)[None, :] < jnp.arange(count)[:, None]
    ranks = jnp.sum((matches & before).astype(jnp.int32), axis=1)
    return owners * slots_dev + ranks


def local_plain(
    signal, mel_frames, speaker_ids, owners, master, first_moment, second_moment, res_cot, skip_cot
):
    chans = lax.axis_size("chan")
    slots_dev = master.shape[0]
    tok_count = signal.shape[0]
    hid_local = HIDDEN_SIZE // chans
    col_count = GATES // chans
    seg_count = speaker_ids.shape[0]
    spk_start = 2 * RESID + MELS
    out_start = spk_start + SPEAKERS
    places = place_index(owners, slots_dev)
    table = places[:, None] == jnp.arange(chans * slots_dev)[None, :]
    received = lax.all_to_all(
        master.astype(BF16), "chan", split_axis=2, concat_axis=0, tiled=True
    ).reshape(chans * slots_dev, BLOCK * col_count)
    params = jnp.dot(table.astype(BF16), received, preferred_element_type=F32)
    params = params.astype(BF16).reshape(ROWS, col_count)
    tap_prev, tap_now = params[:RESID], params[RESID : 2 * RESID]
    mel_proj = params[2 * RESID : spk_start]
    speaker_table = params[spk_start:out_start]
    out_cols = params[out_start:].reshape(RESID, hid_local, 2)
    n_tm = lax.axis_size("tm")
    tail_prev = lax.ppermute(signal[-DILATION:], "tm", [(i, i + 1) for i in range(n_tm - 1)])
    inputs = lax.all_gather(signal, "chan", axis=1, tiled=True)
    tail_full = lax.all_gather(tail_prev, "chan", axis=1, tiled=True)
    shifted = jnp.concatenate([tail_full, inputs[:-DILATION]], 0)
    pre_act = jnp.dot(shifted, tap_prev, preferred_element_type=F32)
    pre_act = pre_act + jnp.dot(inputs, tap_now, preferred_element_type=F32)
    pre_act = pre_act + jnp.dot(mel_frames, mel_proj, preferred_element_type=F32)
    one_hot = (speaker_ids[:, None] == jnp.arange(SPEAKERS)[None, :]).astype(BF16)
    embedded = jnp.dot(one_hot, speaker_table, preferred_element_type=F32)
    pre_act = (pre_act.reshape(seg_count, SEG, col_count) + embedded[:, None, :]).reshape(
        tok_count, col_count
    )
    filt = jnp.tanh(pre_act[:, 0::2])
    gates = jax.nn.sigmoid(pre_act[:, 1::2])
    hidden = (filt * gates).astype(BF16)
    summed = lax.psum_scatter(
        jnp.einsum("cuw,tu->cwt", out_cols, hidden, preferred_element_type=F32),
        "chan",
        scatter_dimension=0,
        tiled=True,
    )
    cots = lax.all_gather(
        jnp.stack([res_cot.T, skip_cot.T], axis=1), "chan", axis=0, tiled=True
    )
    grad_hid = jnp.einsum("cwt,cuw->tu", cots, out_cols, preferred_element_type=F32)
    term = jnp.einsum("cwt,tu->cuw", cots, hidden, preferred_element_type=F32)
    grad_filt = grad_hid * gates * (1.0 - filt * filt)
    grad_gate = grad_hid * filt * gates * (1.0 - gates)
    grad_pre = (
        jnp.stack([grad_filt, grad_gate], axis=2).reshape(tok_count, col_count).astype(BF16)
    )
    ahead = lax.ppermute(grad_pre[:DILATION], "tm", [(i + 1, i) for i in range(n_tm - 1)])
    later = jnp.concatenate([grad_pre[DILATION:], ahead], 0)
    input_part = lax.psum_scatter(
        dot(tap_now, grad_pre, NT) + dot(tap_prev, later, NT),
        "chan",
        scatter_dimension=0,
        tiled=True,
    )
    seg_sums = jnp.sum(grad_pre.astype(F32).reshape(seg_count, SEG, col_count), axis=1)
    grad_spk = lax.dot_general(
        one_hot.astype(F32),
        seg_sums,
        TN,
        precision=lax.Precision.HIGHEST,
        preferred_element_type=F32,
    )
    grad_params = jnp.concatenate(
        [
            dot(shifted, grad_pre, TN),
            dot(inputs, grad_pre, TN),
            dot(mel_frames, grad_pre, TN),
            grad_spk,
            term.reshape(RESID, col_count),
        ],
        0,
    )
    grad_params = lax.psum(grad_params, "tm").reshape(NBLK, BLOCK * col_count)
    outgoing = lax.dot_general(
        table.astype(F32), grad_params, TN, precision=lax.Precision.HIGHEST
    ).reshape(chans * slots_dev, BLOCK, col_count)
    grad_slots = lax.all_to_all(outgoing, "chan", split_axis=0, concat_axis=2, tiled=True)
    owned = jnp.sum((owners == lax.axis_index("chan")).astype(jnp.int32))
    keep = (jnp.arange(slots_dev) < owned)[:, None, None]
    first_new = MOMENT_DECAY * first_moment + (1.0 - MOMENT_DECAY) * grad_slots
    second_new = MOMENT_DECAY * second_moment + (1.0 - MOMENT_DECAY) * grad_slots * grad_slots
    first_hat = first_new / (1.0 - MOMENT_DECAY**STEP)
    second_hat = second_new / (1.0 - MOMENT_DECAY**STEP)
    stepped = master - STEP_RATE * (
        first_hat / (jnp.sqrt(second_hat) + EPSILON) + WEIGHT_DECAY * master
    )
    return (
        signal.astype(F32) + summed[:, 0, :].T,
        summed[:, 1, :].T,
        res_cot.astype(F32) + input_part.T,
        jnp.where(keep, first_new, first_moment),
        jnp.where(keep, second_new, second_moment),
        jnp.where(keep, stepped, master),
    )


def solution(mesh):
    wide = P("tm", "chan")
    slots = P("chan", None, None)
    packed_mesh = mesh.shape["tm"] == 2 and mesh.shape["chan"] == 16
    return jax.shard_map(
        local if packed_mesh else local_plain,
        mesh=mesh,
        in_specs=(wide, P("tm", None), P("tm"), P(), slots, slots, slots, wide, wide),
        out_specs=(wide, wide, wide, slots, slots, slots),
        check_vma=False,
    )
```

```python
import functools

import jax
import jax.numpy as jnp
from jax import lax
from jax.experimental import pallas as pl
from jax.experimental.pallas import tpu as pltpu
from jax.sharding import PartitionSpec as P

RESID = 512
HIDDEN_SIZE = 512
MELS = 80
SPEAKERS = 944
DILATION = 8
SEG = 128
BLOCK = 8
STEP = 5
GATES = 1024
ROWS = 2560
NBLK = 320

MOMENT_DECAY = 0.5
STEP_RATE = 0.03
WEIGHT_DECAY = 0.01
EPSILON = 1e-08

F32 = jnp.float32
BF16 = jnp.bfloat16
NN = (((1,), (0,)), ((), ()))
NT = (((1,), (1,)), ((), ()))
TN = (((0,), (0,)), ((), ()))

TAPS = 2 * RESID // BLOCK
MEL_AT = TAPS
MEL_BLOCKS = MELS // BLOCK
SEG_AT = 144
OUT_AT = 160
PACKED = 224
SPK_BLOCK = TAPS + MEL_BLOCKS
OUT_BLOCK = SPK_BLOCK + SPEAKERS // BLOCK
PIECE = 112


def dot(a, b, dims=NN):
    return lax.dot_general(a, b, dims, preferred_element_type=F32)


def iota(shape, dim):
    return lax.broadcasted_iota(jnp.int32, shape, dim)


def onehot(cond):
    return jnp.where(cond, 1.0, 0.0).astype(BF16)


KIB, MIB = 2**10, 2**20
VMEM, SMEM, HBM = pltpu.VMEM, pltpu.SMEM, pltpu.HBM


def call(kernel, out, spaces, gflops=0, scratch=(), out_space=VMEM, pinned=()):
    run = pl.pallas_call(
        kernel,
        out_shape=out,
        in_specs=[pl.BlockSpec(memory_space=space) for space in spaces],
        out_specs=jax.tree.map(lambda _: pl.BlockSpec(memory_space=out_space), out),
        scratch_shapes=list(scratch),
        compiler_params=pltpu.CompilerParams(vmem_limit_bytes=24 * MIB),
        cost_estimate=pl.CostEstimate(
            flops=gflops * 10**9, bytes_accessed=MIB, transcendentals=0
        ),
    )
    pin = pltpu.with_memory_space_constraint
    fixed = [space if space == HBM or n in pinned else None for n, space in enumerate(spaces)]
    return lambda *args: run(*(pin(x, f) if f else x for x, f in zip(args, fixed, strict=True)))


def gate_order(dim):
    natural, split = iota((256, 256), dim), iota((256, 256), 1 - dim)
    return onehot(natural == 2 * (split & 127) + (split >> 7))


def begin(speakers, master, sig, res, skp, mel, sent, edges, strips, spk, sems):
    half = lax.axis_index("tm")
    slots = sent.shape[1]
    cut = pl.ds(pl.multiple_of((1 - half) * 896, 128), 128)
    tiles = []
    for n, part in enumerate((sig, res, skp, mel)):
        to = edges.at[32 * n : 32 * n + part.shape[0], :]
        tiles.append(pltpu.make_async_copy(part.at[:, cut], to, sems.at[8 + n]))
    copies = []
    for t in range(8):
        part = master.at[:, 128 * t : 128 * t + 128]
        copies.append(pltpu.make_async_copy(part, strips.at[t], sems.at[t]))
    names = pltpu.make_async_copy(speakers, spk, sems.at[12])
    for copy in (names, *copies, *tiles):
        copy.start()
    names.wait()
    row, lane = iota((16, 128), 0), iota((16, 128), 1)
    table = jnp.zeros((16, 128), jnp.int32)
    for s in range(8):
        code = jnp.where(row == 0, spk[s] >> 3, spk[s] & 7)
        table = jnp.where((lane == s) & (row < 2), code, table)
    edges[176:192, :] = table.astype(F32).astype(BF16)
    for t in range(8):
        copies[t].wait()
        lanes = slice(128 * (t % 2), 128 * (t % 2) + 128)
        for j in range(4):
            low = strips[t, pl.ds(j, slots, stride=8), :]
            high = strips[t, pl.ds(4 + j, slots, stride=8), :]
            sent[4 * (t // 2) + j, :, lanes] = jnp.where(half == 0, low, high).astype(BF16)
    for tile in tiles:
        tile.wait()


def pack_tokens(sig_hbm, res_hbm, skp_hbm, other, o0, o1, o2, o3, held, sems):
    copies = [
        pltpu.make_async_copy(part, held.at[n], sems.at[n])
        for n, part in enumerate((sig_hbm, res_hbm, skp_hbm))
    ]
    for copy in copies:
        copy.start()
    for copy in copies:
        copy.wait()
    sig, res, skp = (held.at[n] for n in range(3))
    half, j = lax.axis_index("tm"), lax.axis_index("chan") & 3
    outs = (o0, o1, o2, o3)
    parts = (sig, res, skp)
    befores, nexts = [], ([], [], [])
    for k in range(4):
        to = j ^ k
        cut = pl.ds(pl.multiple_of(to * 256, 256), 256)
        for n, part in enumerate(parts):
            outs[k][32 * n : 32 * n + 32, :] = part[:, cut]
        cut = pl.ds(pl.multiple_of(jnp.maximum(to * 256 - 128, 0), 128), 128)
        edge = jnp.where(half == 1, other[0:32, :].astype(F32), 0.0)
        befores.append(jnp.where(to == 0, edge, sig[:, cut].astype(F32)))
        cut = pl.ds(pl.multiple_of(jnp.minimum(to * 256 + 256, 896), 128), 128)
        for n, part in enumerate(parts):
            edge = jnp.where(half == 0, other[32 * n : 32 * n + 32, :].astype(F32), 0.0)
            nexts[n].append(jnp.where(to == 3, edge, part[:, cut].astype(F32)))
    tall = [jnp.concatenate(x, 0).astype(BF16) for x in (befores, *nexts)]
    t, lane = iota((16, 128), 0), iota((16, 128), 1)
    top, low = t < DILATION, t >= DILATION
    head_top = onehot(top & (lane == t))
    head_low = onehot(low & (lane == t - DILATION))
    last_top = onehot(top & (lane == t + 120))
    rows = (
        dot(last_top, tall[0], NT) + dot(head_low, tall[1], NT),
        dot(head_top, tall[2], NT) + dot(head_low, tall[3], NT),
    )
    for k in range(4):
        for n in range(2):
            outs[k][96:112, 128 * n : 128 * n + 128] = jnp.where(
                (lane >> 5) == k, rows[n], 0.0
            ).astype(BF16)


def join(o0, o1, o2, o3, out):
    ends = o0[96:112, :].astype(F32)
    for piece in (o1, o2, o3):
        ends = ends + piece[96:112, :].astype(F32)
    for k, piece in enumerate((o0, o1, o2, o3)):
        out[96 * k : 96 * k + 96, :] = piece[0:96, :]
    out[384:400, :] = ends.astype(BF16)


def place_blocks(spk_ids, owners, other, at_col, put, owned, *, slots_dev):
    half = lax.axis_index("tm")
    own_row = owners[...]
    mine = jnp.where(own_row == lax.axis_index("chan"), 1, 0)
    owned[...] = jnp.broadcast_to(jnp.sum(mine, axis=1, keepdims=True), owned.shape)
    down, across = iota((NBLK, NBLK), 0), iota((NBLK, NBLK), 1)
    row_all = jnp.broadcast_to(own_row, (NBLK, NBLK))
    own_col = jnp.sum(jnp.where(down == across, row_all, 0), axis=1, keepdims=True)
    before = (own_col == row_all) & (down < across)
    rank = jnp.sum(jnp.where(before, 1, 0), axis=0, keepdims=True)
    place = own_row * slots_dev + rank
    n = iota((PACKED, 128), 0)
    far = n - SEG_AT - 8 * (1 - half) == iota((PACKED, 128), 1)
    blocks = jnp.broadcast_to(other[176:192, :].astype(F32)[0:1], (PACKED, 128))
    spk = jnp.sum(jnp.where(far, blocks, 0.0), axis=1, keepdims=True).astype(jnp.int32)
    n = iota((PACKED, 1), 0)
    for s in range(8):
        spk = jnp.where(n == SEG_AT + 8 * half + s, spk_ids[s] >> 3, spk)
    blk = jnp.where(
        n < SPK_BLOCK,
        n,
        jnp.where(n < SEG_AT, -1, jnp.where(n < OUT_AT, SPK_BLOCK + spk, n + (OUT_BLOCK - OUT_AT))),
    )
    match = jnp.broadcast_to(blk, (PACKED, NBLK)) == iota((PACKED, NBLK), 1)
    at = jnp.sum(jnp.where(match, jnp.broadcast_to(place, (PACKED, NBLK)), 0), axis=1, keepdims=True)
    at = jnp.where(blk < 0, -1, at)
    at_col[...] = jnp.broadcast_to(at, (PACKED, 128))
    same = iota((PACKED, PACKED), 0) == iota((PACKED, PACKED), 1)
    row = jnp.sum(jnp.where(same, jnp.broadcast_to(at, (PACKED, PACKED)), 0), axis=0, keepdims=True)
    put[...] = onehot(jnp.broadcast_to(row, put.shape) == iota(put.shape, 0))


def gather_blocks(at_col, slots, out):
    shape = (PACKED, slots.shape[0])
    pick = onehot(jnp.broadcast_to(at_col[:, 0:1], shape) == iota(shape, 1))
    got = dot(pick, slots[...]).astype(BF16)
    out[...] = dot(got, gate_order(0)).astype(BF16)


def sum_cores(kept, got, *outs):
    i = 2 * lax.axis_index("tm") + ((lax.axis_index("chan") >> 1) & 1)
    for k, out in enumerate(outs):
        out[...] = (kept[i ^ k].astype(F32) + got[i ^ k].astype(F32)).astype(BF16)


def scatter_blocks(put, p0, p1, p2, p3, out):
    total = p0[...].astype(F32)
    for part in (p1, p2, p3):
        total = total + part[...].astype(F32)
    natural = dot(total.astype(BF16), gate_order(1)).astype(BF16)
    spread = dot(put[...], natural).astype(BF16)
    out[0] = spread
    out[1] = spread


def sum_units(z0, z1, z2, z3, o0, o1, o2, o3):
    for i, out in enumerate((o0, o1, o2, o3)):
        out[...] = (
            z0[i].astype(F32) + z1[i].astype(F32) + z2[i].astype(F32) + z3[i].astype(F32)
        ).astype(BF16)


def prepare(spk, p0, p1, p2, p3, mel, other, features, res, skp, natural):
    half, ch = lax.axis_index("tm"), lax.axis_index("chan")
    j = ch & 3
    got = (p0, p1, p2, p3)
    tokens, wide = 256, 384
    for k in range(4):
        for i in range(4):
            rows = pl.ds(pl.multiple_of(32 * (ch ^ (4 * k + i)), 32), 32)
            for n in range(3):
                at = 96 * i + 32 * n
                for h in range(2):
                    natural[2 * n + h, rows, :] = got[k][at : at + 32, 128 * h : 128 * h + 128].astype(F32)

    ends = [part[384:400, :].astype(F32) for part in got]
    gap = jnp.zeros((96, 128), F32)
    for k, end in enumerate(ends):
        left, right = end[:, 0:128], end[:, 128:256]
        tile = jnp.concatenate([left[8:16], right, gap, left[0:8]], 0).T
        for i in range(4):
            rows = pl.ds(pl.multiple_of(32 * (ch ^ (4 * k + i)), 32), 32)
            natural[6, rows, :] = tile[32 * i : 32 * i + 32]

    def majors(n):
        return jnp.concatenate([natural[n, pl.ds(r, 64, stride=8), :] for r in range(8)], 0)

    tile = majors(6)
    sig = jnp.concatenate([majors(0), majors(1), tile], 1)
    for n, out in ((1, res), (2, skp)):
        out[:, 0:128] = majors(2 * n).astype(BF16)
        out[:, 128:256] = majors(2 * n + 1).astype(BF16)
        out[:, 256:384] = pltpu.roll(tile, 128 - 8 * n, 1).astype(BF16)
    shifted = pltpu.roll(sig, DILATION, 1).astype(BF16)
    sig = sig.astype(BF16)
    m = iota((128, MELS), 0)
    mel_pick = onehot(((m & 15) < MEL_BLOCKS) & (iota((128, MELS), 1) == 8 * (m & 15) + (m >> 4)))
    cut = pl.ds(pl.multiple_of(j * tokens, tokens), tokens)
    far = pl.ds(pl.multiple_of(jnp.minimum(j * tokens + tokens, 896), 128), 128)
    ahead = jnp.where(j == 3, other[96:176, :].astype(F32), mel[:, far].astype(F32)).astype(BF16)
    mels = jnp.concatenate([dot(mel_pick, mel[:, cut]), dot(mel_pick, ahead)], 1).astype(BF16)
    seg = 8 * half + 2 * j
    row, lane = iota((16, wide), 0), iota((16, wide), 1)
    beyond = other[176:192, :].astype(F32)[1:2, 0:1].astype(jnp.int32)
    beyond = jnp.where(j == 3, beyond, spk[jnp.minimum(2 * j + 2, 7)] & 7)
    sub = jnp.where(
        lane < SEG,
        spk[2 * j] & 7,
        jnp.where(lane < 2 * SEG, spk[2 * j + 1] & 7, jnp.broadcast_to(beyond, (16, wide))),
    )
    for r in range(8):
        features[r, 0:64] = shifted[64 * r : 64 * r + 64]
        features[r, 64:128] = sig[64 * r : 64 * r + 64]
        features[r, 128:144] = mels[16 * r : 16 * r + 16]
        features[r, 144:160] = onehot((row == seg + (lane >> 7)) & (sub == r))


def layer(packed, feat, res, skp, kept, given, z0, z1, z2, z3, natural):
    tokens, wide = 256, 384
    features = feat[...].reshape(8 * OUT_AT, wide)
    conv = packed[:, 0:OUT_AT, :].reshape(8 * OUT_AT, 256)
    pre = dot(conv, features, TN)
    filt = jnp.tanh(pre[:128])
    gate = jax.nn.sigmoid(pre[128:])
    hidden = (filt[:, :tokens] * gate[:, :tokens]).astype(BF16)
    out_res = packed[:, OUT_AT:PACKED, 0:128].reshape(RESID, 128)
    out_skp = packed[:, OUT_AT:PACKED, 128:256].reshape(RESID, 128)
    res_part = dot(out_res, hidden)
    skp_part = dot(out_skp, hidden)
    grad_hidden = dot(out_res, res[...], TN) + dot(out_skp, skp[...], TN)
    grad_pre = jnp.concatenate(
        [
            grad_hidden * gate * (1.0 - filt * filt),
            grad_hidden * filt * gate * (1.0 - gate),
        ],
        0,
    ).astype(BF16)
    prev = packed[:, 0:64, :].reshape(RESID, 256)
    now = packed[:, 64:128, :].reshape(RESID, 256)
    later = pltpu.roll(dot(prev, grad_pre), wide - DILATION, 1)[:, :tokens]
    grad_pre = grad_pre[:, :tokens]
    in_part = dot(now, grad_pre) + later
    conv_grad = dot(features[:, :tokens], grad_pre, NT).astype(BF16)
    res_grad = dot(res[:, :tokens], hidden, NT).astype(BF16)
    skp_grad = dot(skp[:, :tokens], hidden, NT).astype(BF16)
    core = lax.axis_index("chan") & 1
    for part, rows, cols in (
        (conv_grad.reshape(8, OUT_AT, 256), slice(0, OUT_AT), slice(0, 256)),
        (res_grad.reshape(8, 64, 128), slice(OUT_AT, PACKED), slice(0, 128)),
        (skp_grad.reshape(8, 64, 128), slice(OUT_AT, PACKED), slice(128, 256)),
    ):
        for i in range(4):
            even, odd = part[2 * i], part[2 * i + 1]
            kept[i, rows, cols] = jnp.where(core == 0, even, odd)
            given[i, rows, cols] = jnp.where(core == 0, odd, even)
    for n, part in enumerate((res_part, skp_part, in_part)):
        for h in range(2):
            for r in range(8):
                natural[2 * n + h, pl.ds(r, 64, stride=8), :] = part[
                    64 * r : 64 * r + 64, 128 * h : 128 * h + 128
                ]
    ch = lax.axis_index("chan")
    for k, out in enumerate((z0, z1, z2, z3)):
        for i in range(4):
            rows = pl.ds(pl.multiple_of(32 * (ch ^ (4 * k + i)), 32), 32)
            for n in range(3):
                for h in range(2):
                    out[i, 32 * n : 32 * n + 32, 128 * h : 128 * h + 128] = natural[
                        2 * n + h, rows, :
                    ].astype(BF16)


def finish_tokens(o0, o1, o2, o3, sig, res, residual, skipped, grad_in):
    j = lax.axis_index("chan") & 3
    for k, piece in enumerate((o0, o1, o2, o3)):
        cut = pl.ds(pl.multiple_of((j ^ k) * 256, 256), 256)
        residual[:, cut] = sig[:, cut].astype(F32) + piece[0:32, :].astype(F32)
        skipped[:, cut] = piece[32:64, :].astype(F32)
        grad_in[:, cut] = res[:, cut].astype(F32) + piece[64:96, :].astype(F32)


def update(owned, grads, master, first, second, *refs):
    outs, held, old, grad, sems = refs[:3], refs[3:6], (*refs[6:8], first), refs[8], refs[9]
    slots = grads.shape[1]
    rows = 8 * slots
    steps = 8
    parts = [slice(n * rows // steps, (n + 1) * rows // steps) for n in range(steps)]
    fetches = []
    for n, part in enumerate(parts):
        for m, source in enumerate((second, master)):
            fetch = pltpu.make_async_copy(
                source.at[part, :], old[m].at[part, :], sems.at[3 * steps + 2 * n + m]
            )
            fetch.start()
            fetches.append(fetch)
    for r in range(8):
        for z in range(4):
            got = grads[16 * (r // 4) + 4 * z + r % 4].astype(F32)
            for h in range(2):
                grad[2 * z + h, pl.ds(r, slots, stride=8), :] = got[:, 128 * h : 128 * h + 128]
    unbias = 1.0 / (1.0 - MOMENT_DECAY**STEP)
    copies = []
    for n, part in enumerate(parts):
        for m in range(2):
            fetches[2 * n + m].wait()
        old_s, old_m, old_f = (ref[part, :] for ref in old)
        new = jnp.concatenate([grad[t, part, :] for t in range(8)], 1)
        keep = n * (rows // steps) + iota((rows // steps, 1), 0) < 8 * owned[0:1, 0:1]
        first_new = MOMENT_DECAY * old_f + (1.0 - MOMENT_DECAY) * new
        second_new = MOMENT_DECAY * old_s + (1.0 - MOMENT_DECAY) * new * new
        first_hat = first_new * unbias
        second_hat = second_new * unbias
        root = second_hat * lax.rsqrt(second_hat)
        stepped = old_m - STEP_RATE * (
            first_hat * pl.reciprocal(root + EPSILON) + WEIGHT_DECAY * old_m
        )
        held[0][part, :] = jnp.where(keep, first_new, old_f)
        held[1][part, :] = jnp.where(keep, second_new, old_s)
        held[2][part, :] = jnp.where(keep, stepped, old_m)
        for m in range(3):
            copy = pltpu.make_async_copy(
                held[m].at[part, :], outs[m].at[part, :], sems.at[3 * n + m]
            )
            copy.start()
            copies.append(copy)
    for copy in copies:
        copy.wait()


BOTH = ("tm", "chan")


def swap(x, k):
    n = lax.axis_size("chan")
    return lax.ppermute(x, "chan", [(i, i ^ k) for i in range(n)])


def local(
    signal, mel_frames, speaker_ids, owners, master, first_moment, second_moment, res_cot, skip_cot
):
    slots_dev = master.shape[0]
    slots = 16 * slots_dev
    flat = (8 * slots_dev, GATES)
    sig, res, skp, mel = signal.T, res_cot.T, skip_cot.T, mel_frames.T
    own_row = owners.reshape(1, NBLK)
    share = [[16 * y + 4 * z + j for y in range(2) for j in range(4)] for z in range(4)]
    sds = jax.ShapeDtypeStruct
    dma = pltpu.SemaphoreType.DMA

    sent, edges = call(
        begin,
        (sds((16, slots_dev, 256), BF16), sds((192, 128), BF16)),
        (HBM,) * 6,
        scratch=(
            pltpu.VMEM((8, 8 * slots_dev, 128), F32),
            pltpu.SMEM(speaker_ids.shape, jnp.int32),
            dma((13,)),
        ),
    )(speaker_ids, master.reshape(flat), sig, res, skp, mel)
    other = lax.ppermute(edges, "tm", [(0, 1), (1, 0)])
    arrived = lax.all_to_all(sent, "chan", 0, 0, tiled=True)
    piece = sds((PIECE, 256), BF16)
    o = call(
        pack_tokens,
        (piece,) * 4,
        (HBM,) * 3 + (VMEM,),
        gflops=200,
        scratch=(pltpu.VMEM((3, *sig.shape), BF16), dma((3,))),
    )(sig, res, skp, other)
    mine = call(join, sds((400, 256), BF16), (VMEM,) * 4)(
        o[0], swap(o[1], 1), swap(o[2], 2), swap(o[3], 3)
    )
    p1, p2, p3 = (swap(mine, 4 * k) for k in (1, 2, 3))

    at_col, put, owned = call(
        functools.partial(place_blocks, slots_dev=slots_dev),
        (
            sds((PACKED, 128), jnp.int32),
            sds((slots, PACKED), BF16),
            sds((8, 128), jnp.int32),
        ),
        (SMEM, VMEM, VMEM),
    )(speaker_ids, own_row, other)
    arrived, _ = lax.optimization_barrier((arrived, mine))
    gathered = call(gather_blocks, sds((PACKED, 256), BF16), (VMEM, VMEM), gflops=200)(
        at_col, arrived.reshape(slots, 256)
    )
    packed = lax.all_gather(gathered, BOTH, axis_index_groups=share)
    mel, _ = lax.optimization_barrier((mel, packed))
    cots = sds((RESID, 384), BF16)
    ready = call(
        prepare,
        (sds((8, OUT_AT, 384), BF16), cots, cots),
        (SMEM,) + (VMEM,) * 6,
        gflops=200,
        pinned=(1,),
        scratch=(pltpu.VMEM((7, RESID, 128), F32),),
    )(speaker_ids, mine, p1, p2, p3, mel, other)

    quad = sds((4, 96, 256), BF16)
    rows = sds((4, PACKED, 256), BF16)
    kept, given, z0, z1, z2, z3 = call(
        layer,
        (rows, rows, quad, quad, quad, quad),
        (VMEM,) * 4,
        scratch=(pltpu.VMEM((6, RESID, 128), F32),),
    )(packed, *ready)

    n = lax.axis_size("chan")
    g = call(sum_cores, (sds((PACKED, 256), BF16),) * 4, (VMEM,) * 2)(kept, swap(given, 1))
    across = [(16 * y + i, 16 * (1 - y) + (i ^ 2)) for y in range(2) for i in range(n)]
    g = (g[0], swap(g[1], 2), lax.ppermute(g[2], "tm", [(0, 1), (1, 0)]), lax.ppermute(g[3], BOTH, across))
    t1, t2, t3 = (swap(z, 4 * k) for k, z in ((1, z1), (2, z2), (3, z3)))
    spread = call(scatter_blocks, sds((2, slots, 256), BF16), (VMEM,) * 5)(put, *g)
    returned = lax.all_to_all(spread.reshape(32, slots_dev, 256), BOTH, 0, 0)
    o = call(sum_units, (sds((96, 256), BF16),) * 4, (VMEM,) * 4, gflops=20)(z0, t1, t2, t3)
    o = (o[0], swap(o[1], 1), swap(o[2], 2), swap(o[3], 3))
    narrow = sds(sig.shape, F32)
    residual, skipped, grad_in = call(finish_tokens, (narrow,) * 3, (VMEM,) * 6)(*o, sig, res)
    new = call(
        update,
        (sds(flat, F32),) * 3,
        (VMEM, VMEM, HBM, VMEM, HBM),
        scratch=(pltpu.VMEM(flat, F32),) * 5
        + (pltpu.VMEM((8, flat[0], 128), F32), dma((40,))),
        out_space=HBM,
    )(
        owned,
        returned,
        master.reshape(flat),
        first_moment.reshape(flat),
        second_moment.reshape(flat),
    )
    return (residual.T, skipped.T, grad_in.T, *(x.reshape(master.shape) for x in new))


def place_index(owners, slots_dev):
    count = owners.shape[0]
    matches = owners[:, None] == owners[None, :]
    before = jnp.arange(count)[None, :] < jnp.arange(count)[:, None]
    ranks = jnp.sum((matches & before).astype(jnp.int32), axis=1)
    return owners * slots_dev + ranks


def local_plain(
    signal, mel_frames, speaker_ids, owners, master, first_moment, second_moment, res_cot, skip_cot
):
    chans = lax.axis_size("chan")
    slots_dev = master.shape[0]
    tok_count = signal.shape[0]
    hid_local = HIDDEN_SIZE // chans
    col_count = GATES // chans
    seg_count = speaker_ids.shape[0]
    spk_start = 2 * RESID + MELS
    out_start = spk_start + SPEAKERS
    places = place_index(owners, slots_dev)
    table = places[:, None] == jnp.arange(chans * slots_dev)[None, :]
    received = lax.all_to_all(
        master.astype(BF16), "chan", split_axis=2, concat_axis=0, tiled=True
    ).reshape(chans * slots_dev, BLOCK * col_count)
    params = jnp.dot(table.astype(BF16), received, preferred_element_type=F32)
    params = params.astype(BF16).reshape(ROWS, col_count)
    tap_prev, tap_now = params[:RESID], params[RESID : 2 * RESID]
    mel_proj = params[2 * RESID : spk_start]
    speaker_table = params[spk_start:out_start]
    out_cols = params[out_start:].reshape(RESID, hid_local, 2)
    n_tm = lax.axis_size("tm")
    tail_prev = lax.ppermute(signal[-DILATION:], "tm", [(i, i + 1) for i in range(n_tm - 1)])
    inputs = lax.all_gather(signal, "chan", axis=1, tiled=True)
    tail_full = lax.all_gather(tail_prev, "chan", axis=1, tiled=True)
    shifted = jnp.concatenate([tail_full, inputs[:-DILATION]], 0)
    pre_act = jnp.dot(shifted, tap_prev, preferred_element_type=F32)
    pre_act = pre_act + jnp.dot(inputs, tap_now, preferred_element_type=F32)
    pre_act = pre_act + jnp.dot(mel_frames, mel_proj, preferred_element_type=F32)
    one_hot = (speaker_ids[:, None] == jnp.arange(SPEAKERS)[None, :]).astype(BF16)
    embedded = jnp.dot(one_hot, speaker_table, preferred_element_type=F32)
    pre_act = (pre_act.reshape(seg_count, SEG, col_count) + embedded[:, None, :]).reshape(
        tok_count, col_count
    )
    filt = jnp.tanh(pre_act[:, 0::2])
    gates = jax.nn.sigmoid(pre_act[:, 1::2])
    hidden = (filt * gates).astype(BF16)
    summed = lax.psum_scatter(
        jnp.einsum("cuw,tu->cwt", out_cols, hidden, preferred_element_type=F32),
        "chan",
        scatter_dimension=0,
        tiled=True,
    )
    cots = lax.all_gather(
        jnp.stack([res_cot.T, skip_cot.T], axis=1), "chan", axis=0, tiled=True
    )
    grad_hid = jnp.einsum("cwt,cuw->tu", cots, out_cols, preferred_element_type=F32)
    term = jnp.einsum("cwt,tu->cuw", cots, hidden, preferred_element_type=F32)
    grad_filt = grad_hid * gates * (1.0 - filt * filt)
    grad_gate = grad_hid * filt * gates * (1.0 - gates)
    grad_pre = (
        jnp.stack([grad_filt, grad_gate], axis=2).reshape(tok_count, col_count).astype(BF16)
    )
    ahead = lax.ppermute(grad_pre[:DILATION], "tm", [(i + 1, i) for i in range(n_tm - 1)])
    later = jnp.concatenate([grad_pre[DILATION:], ahead], 0)
    input_part = lax.psum_scatter(
        dot(tap_now, grad_pre, NT) + dot(tap_prev, later, NT),
        "chan",
        scatter_dimension=0,
        tiled=True,
    )
    seg_sums = jnp.sum(grad_pre.astype(F32).reshape(seg_count, SEG, col_count), axis=1)
    grad_spk = lax.dot_general(
        one_hot.astype(F32),
        seg_sums,
        TN,
        precision=lax.Precision.HIGHEST,
        preferred_element_type=F32,
    )
    grad_params = jnp.concatenate(
        [
            dot(shifted, grad_pre, TN),
            dot(inputs, grad_pre, TN),
            dot(mel_frames, grad_pre, TN),
            grad_spk,
            term.reshape(RESID, col_count),
        ],
        0,
    )
    grad_params = lax.psum(grad_params, "tm").reshape(NBLK, BLOCK * col_count)
    outgoing = lax.dot_general(
        table.astype(F32), grad_params, TN, precision=lax.Precision.HIGHEST
    ).reshape(chans * slots_dev, BLOCK, col_count)
    grad_slots = lax.all_to_all(outgoing, "chan", split_axis=0, concat_axis=2, tiled=True)
    owned = jnp.sum((owners == lax.axis_index("chan")).astype(jnp.int32))
    keep = (jnp.arange(slots_dev) < owned)[:, None, None]
    first_new = MOMENT_DECAY * first_moment + (1.0 - MOMENT_DECAY) * grad_slots
    second_new = MOMENT_DECAY * second_moment + (1.0 - MOMENT_DECAY) * grad_slots * grad_slots
    first_hat = first_new / (1.0 - MOMENT_DECAY**STEP)
    second_hat = second_new / (1.0 - MOMENT_DECAY**STEP)
    stepped = master - STEP_RATE * (
        first_hat / (jnp.sqrt(second_hat) + EPSILON) + WEIGHT_DECAY * master
    )
    return (
        signal.astype(F32) + summed[:, 0, :].T,
        summed[:, 1, :].T,
        res_cot.astype(F32) + input_part.T,
        jnp.where(keep, first_new, first_moment),
        jnp.where(keep, second_new, second_moment),
        jnp.where(keep, stepped, master),
    )


def solution(mesh):
    wide = P("tm", "chan")
    slots = P("chan", None, None)
    packed_mesh = mesh.shape["tm"] == 2 and mesh.shape["chan"] == 16
    return jax.shard_map(
        local if packed_mesh else local_plain,
        mesh=mesh,
        in_specs=(wide, P("tm", None), P("tm"), P(), slots, slots, slots, wide, wide),
        out_specs=(wide, wide, wide, slots, slots, slots),
        check_vma=False,
    )
```

```python
import functools

import jax
import jax.numpy as jnp
from jax import lax
from jax.experimental import pallas as pl
from jax.experimental.pallas import tpu as pltpu
from jax.sharding import PartitionSpec as P

RESID = 512
HIDDEN_SIZE = 512
MELS = 80
SPEAKERS = 944
DILATION = 8
SEG = 128
BLOCK = 8
STEP = 5
GATES = 1024
ROWS = 2560
NBLK = 320

MOMENT_DECAY = 0.5
STEP_RATE = 0.03
WEIGHT_DECAY = 0.01
EPSILON = 1e-08

F32 = jnp.float32
BF16 = jnp.bfloat16
NN = (((1,), (0,)), ((), ()))
NT = (((1,), (1,)), ((), ()))
TN = (((0,), (0,)), ((), ()))

TAPS = 2 * RESID // BLOCK
MEL_AT = TAPS
MEL_BLOCKS = MELS // BLOCK
SEG_AT = 144
OUT_AT = 160
PACKED = 224
SPK_BLOCK = TAPS + MEL_BLOCKS
OUT_BLOCK = SPK_BLOCK + SPEAKERS // BLOCK
PIECE = 112


def dot(a, b, dims=NN):
    return lax.dot_general(a, b, dims, preferred_element_type=F32)


def iota(shape, dim):
    return lax.broadcasted_iota(jnp.int32, shape, dim)


def onehot(cond):
    return jnp.where(cond, 1.0, 0.0).astype(BF16)


KIB, MIB = 2**10, 2**20
VMEM, SMEM, HBM = pltpu.VMEM, pltpu.SMEM, pltpu.HBM


def call(kernel, out, spaces, gflops=0, scratch=(), out_space=VMEM, pinned=()):
    run = pl.pallas_call(
        kernel,
        out_shape=out,
        in_specs=[pl.BlockSpec(memory_space=space) for space in spaces],
        out_specs=jax.tree.map(lambda _: pl.BlockSpec(memory_space=out_space), out),
        scratch_shapes=list(scratch),
        compiler_params=pltpu.CompilerParams(vmem_limit_bytes=24 * MIB),
        cost_estimate=pl.CostEstimate(
            flops=gflops * 10**9, bytes_accessed=MIB, transcendentals=0
        ),
    )
    pin = pltpu.with_memory_space_constraint
    fixed = [space if space == HBM or n in pinned else None for n, space in enumerate(spaces)]
    return lambda *args: run(*(pin(x, f) if f else x for x, f in zip(args, fixed, strict=True)))


def gate_order(dim):
    natural, split = iota((256, 256), dim), iota((256, 256), 1 - dim)
    return onehot(natural == 2 * (split & 127) + (split >> 7))


def pack_weights(master, sent, strips, sems):
    half = lax.axis_index("tm")
    slots = sent.shape[1]
    copies = []
    for t in range(8):
        part = master.at[:, 128 * t : 128 * t + 128]
        copies.append(pltpu.make_async_copy(part, strips.at[t], sems.at[t]))
    for copy in copies:
        copy.start()
    for t in range(8):
        copies[t].wait()
        lanes = slice(128 * (t % 2), 128 * (t % 2) + 128)
        for j in range(4):
            low = strips[t, pl.ds(j, slots, stride=8), :]
            high = strips[t, pl.ds(4 + j, slots, stride=8), :]
            sent[4 * (t // 2) + j, :, lanes] = jnp.where(half == 0, low, high).astype(BF16)


def begin(speakers, sig, res, skp, mel, acts, edges, spk, sems):
    cut = pl.ds(pl.multiple_of((1 - lax.axis_index("tm")) * 896, 128), 128)
    copies = [
        pltpu.make_async_copy(speakers, spk, sems.at[0]),
        pltpu.make_async_copy(mel.at[:, cut], edges.at[96:176, :], sems.at[1]),
    ]
    for n, part in enumerate((sig, res, skp)):
        copies.append(pltpu.make_async_copy(part, acts.at[n], sems.at[2 + n]))
    for copy in copies:
        copy.start()
    copies[0].wait()
    row, lane = iota((16, 128), 0), iota((16, 128), 1)
    table = jnp.zeros((16, 128), jnp.int32)
    for s in range(8):
        code = jnp.where(row == 0, spk[s] >> 3, spk[s] & 7)
        table = jnp.where((lane == s) & (row < 2), code, table)
    edges[176:192, :] = table.astype(F32).astype(BF16)
    for copy in copies[1:]:
        copy.wait()
    for n in range(3):
        edges[32 * n : 32 * n + 32, :] = acts[n, :, cut]


def pack_tokens(acts, other, o0, o1, o2, o3):
    sig, res, skp = (acts.at[n] for n in range(3))
    half, j = lax.axis_index("tm"), lax.axis_index("chan") & 3
    outs = (o0, o1, o2, o3)
    parts = (sig, res, skp)
    befores, nexts = [], ([], [], [])
    for k in range(4):
        to = j ^ k
        cut = pl.ds(pl.multiple_of(to * 256, 256), 256)
        for n, part in enumerate(parts):
            outs[k][32 * n : 32 * n + 32, :] = part[:, cut]
        cut = pl.ds(pl.multiple_of(jnp.maximum(to * 256 - 128, 0), 128), 128)
        edge = jnp.where(half == 1, other[0:32, :].astype(F32), 0.0)
        befores.append(jnp.where(to == 0, edge, sig[:, cut].astype(F32)))
        cut = pl.ds(pl.multiple_of(jnp.minimum(to * 256 + 256, 896), 128), 128)
        for n, part in enumerate(parts):
            edge = jnp.where(half == 0, other[32 * n : 32 * n + 32, :].astype(F32), 0.0)
            nexts[n].append(jnp.where(to == 3, edge, part[:, cut].astype(F32)))
    tall = [jnp.concatenate(x, 0).astype(BF16) for x in (befores, *nexts)]
    t, lane = iota((16, 128), 0), iota((16, 128), 1)
    top, low = t < DILATION, t >= DILATION
    head_top = onehot(top & (lane == t))
    head_low = onehot(low & (lane == t - DILATION))
    last_top = onehot(top & (lane == t + 120))
    rows = (
        dot(last_top, tall[0], NT) + dot(head_low, tall[1], NT),
        dot(head_top, tall[2], NT) + dot(head_low, tall[3], NT),
    )
    for k in range(4):
        for n in range(2):
            outs[k][96:112, 128 * n : 128 * n + 128] = jnp.where(
                (lane >> 5) == k, rows[n], 0.0
            ).astype(BF16)


def join(o0, o1, o2, o3, out):
    ends = o0[96:112, :].astype(F32)
    for piece in (o1, o2, o3):
        ends = ends + piece[96:112, :].astype(F32)
    for k, piece in enumerate((o0, o1, o2, o3)):
        out[96 * k : 96 * k + 96, :] = piece[0:96, :]
    out[384:400, :] = ends.astype(BF16)


def place_blocks(spk_ids, owners, other, at_col, put, owned, *, slots_dev):
    half = lax.axis_index("tm")
    own_row = owners[...]
    mine = jnp.where(own_row == lax.axis_index("chan"), 1, 0)
    owned[...] = jnp.broadcast_to(jnp.sum(mine, axis=1, keepdims=True), owned.shape)
    down, across = iota((NBLK, NBLK), 0), iota((NBLK, NBLK), 1)
    row_all = jnp.broadcast_to(own_row, (NBLK, NBLK))
    own_col = jnp.sum(jnp.where(down == across, row_all, 0), axis=1, keepdims=True)
    before = (own_col == row_all) & (down < across)
    rank = jnp.sum(jnp.where(before, 1, 0), axis=0, keepdims=True)
    place = own_row * slots_dev + rank
    n = iota((PACKED, 128), 0)
    far = n - SEG_AT - 8 * (1 - half) == iota((PACKED, 128), 1)
    blocks = jnp.broadcast_to(other[176:192, :].astype(F32)[0:1], (PACKED, 128))
    spk = jnp.sum(jnp.where(far, blocks, 0.0), axis=1, keepdims=True).astype(jnp.int32)
    n = iota((PACKED, 1), 0)
    for s in range(8):
        spk = jnp.where(n == SEG_AT + 8 * half + s, spk_ids[s] >> 3, spk)
    blk = jnp.where(
        n < SPK_BLOCK,
        n,
        jnp.where(n < SEG_AT, -1, jnp.where(n < OUT_AT, SPK_BLOCK + spk, n + (OUT_BLOCK - OUT_AT))),
    )
    match = jnp.broadcast_to(blk, (PACKED, NBLK)) == iota((PACKED, NBLK), 1)
    at = jnp.sum(jnp.where(match, jnp.broadcast_to(place, (PACKED, NBLK)), 0), axis=1, keepdims=True)
    at = jnp.where(blk < 0, -1, at)
    at_col[...] = jnp.broadcast_to(at, (PACKED, 128))
    same = iota((PACKED, PACKED), 0) == iota((PACKED, PACKED), 1)
    row = jnp.sum(jnp.where(same, jnp.broadcast_to(at, (PACKED, PACKED)), 0), axis=0, keepdims=True)
    put[...] = onehot(jnp.broadcast_to(row, put.shape) == iota(put.shape, 0))


def gather_blocks(at_col, slots, out):
    shape = (PACKED, slots.shape[0])
    pick = onehot(jnp.broadcast_to(at_col[:, 0:1], shape) == iota(shape, 1))
    got = dot(pick, slots[...]).astype(BF16)
    out[...] = dot(got, gate_order(0)).astype(BF16)


def sum_cores(kept, got, *outs):
    i = 2 * lax.axis_index("tm") + ((lax.axis_index("chan") >> 1) & 1)
    for k, out in enumerate(outs):
        out[...] = (kept[i ^ k].astype(F32) + got[i ^ k].astype(F32)).astype(BF16)


def scatter_blocks(put, p0, p1, p2, p3, out):
    total = p0[...].astype(F32)
    for part in (p1, p2, p3):
        total = total + part[...].astype(F32)
    natural = dot(total.astype(BF16), gate_order(1)).astype(BF16)
    spread = dot(put[...], natural).astype(BF16)
    out[0] = spread
    out[1] = spread


def sum_units(z0, z1, z2, z3, o0, o1, o2, o3):
    for i, out in enumerate((o0, o1, o2, o3)):
        out[...] = (
            z0[i].astype(F32) + z1[i].astype(F32) + z2[i].astype(F32) + z3[i].astype(F32)
        ).astype(BF16)


def layer(spk, packed, p0, p1, p2, p3, mel, other, kept, given, hidden_out, grad_out, feat, res, skp, natural):
    half, ch = lax.axis_index("tm"), lax.axis_index("chan")
    j = ch & 3
    got = (p0, p1, p2, p3)
    tokens, wide = 256, 384
    for k in range(4):
        for i in range(4):
            rows = pl.ds(pl.multiple_of(32 * (ch ^ (4 * k + i)), 32), 32)
            for n in range(3):
                at = 96 * i + 32 * n
                for h in range(2):
                    natural[2 * n + h, rows, :] = got[k][at : at + 32, 128 * h : 128 * h + 128].astype(F32)

    ends = [part[384:400, :].astype(F32) for part in got]
    gap = jnp.zeros((96, 128), F32)
    for k, end in enumerate(ends):
        left, right = end[:, 0:128], end[:, 128:256]
        tile = jnp.concatenate([left[8:16], right, gap, left[0:8]], 0).T
        for i in range(4):
            rows = pl.ds(pl.multiple_of(32 * (ch ^ (4 * k + i)), 32), 32)
            natural[6, rows, :] = tile[32 * i : 32 * i + 32]

    def majors(n):
        return jnp.concatenate([natural[n, pl.ds(r, 64, stride=8), :] for r in range(8)], 0)

    tile = majors(6)
    sig = jnp.concatenate([majors(0), majors(1), tile], 1)
    for n, out in ((1, res), (2, skp)):
        out[:, 0:128] = majors(2 * n).astype(BF16)
        out[:, 128:256] = majors(2 * n + 1).astype(BF16)
        out[:, 256:384] = pltpu.roll(tile, 128 - 8 * n, 1).astype(BF16)
    shifted = pltpu.roll(sig, DILATION, 1).astype(BF16)
    sig = sig.astype(BF16)
    m = iota((128, MELS), 0)
    mel_pick = onehot(((m & 15) < MEL_BLOCKS) & (iota((128, MELS), 1) == 8 * (m & 15) + (m >> 4)))
    cut = pl.ds(pl.multiple_of(j * tokens, tokens), tokens)
    far = pl.ds(pl.multiple_of(jnp.minimum(j * tokens + tokens, 896), 128), 128)
    ahead = jnp.where(j == 3, other[96:176, :].astype(F32), mel[:, far].astype(F32)).astype(BF16)
    mels = jnp.concatenate([dot(mel_pick, mel[:, cut]), dot(mel_pick, ahead)], 1).astype(BF16)
    seg = 8 * half + 2 * j
    row, lane = iota((16, wide), 0), iota((16, wide), 1)
    beyond = other[176:192, :].astype(F32)[1:2, 0:1].astype(jnp.int32)
    beyond = jnp.where(j == 3, beyond, spk[jnp.minimum(2 * j + 2, 7)] & 7)
    sub = jnp.where(
        lane < SEG,
        spk[2 * j] & 7,
        jnp.where(lane < 2 * SEG, spk[2 * j + 1] & 7, jnp.broadcast_to(beyond, (16, wide))),
    )
    for r in range(8):
        feat[r, 0:64] = shifted[64 * r : 64 * r + 64]
        feat[r, 64:128] = sig[64 * r : 64 * r + 64]
        feat[r, 128:144] = mels[16 * r : 16 * r + 16]
        feat[r, 144:160] = onehot((row == seg + (lane >> 7)) & (sub == r))
    features = feat[...].reshape(8 * OUT_AT, wide)
    conv = packed[:, 0:OUT_AT, :].reshape(8 * OUT_AT, 256)
    pre = dot(conv, features, TN)
    filt = jnp.tanh(pre[:128])
    gate = jax.nn.sigmoid(pre[128:])
    hidden = (filt[:, :tokens] * gate[:, :tokens]).astype(BF16)
    out_res = packed[:, OUT_AT:PACKED, 0:128].reshape(RESID, 128)
    out_skp = packed[:, OUT_AT:PACKED, 128:256].reshape(RESID, 128)
    hidden_out[...] = hidden
    grad_hidden = dot(out_res, res[...], TN) + dot(out_skp, skp[...], TN)
    grad_pre = jnp.concatenate(
        [
            grad_hidden * gate * (1.0 - filt * filt),
            grad_hidden * filt * gate * (1.0 - gate),
        ],
        0,
    ).astype(BF16)
    grad_out[...] = grad_pre
    grad_pre = grad_pre[:, :tokens]
    conv_grad = dot(features[:, :tokens], grad_pre, NT).astype(BF16)
    res_grad = dot(res[:, :tokens], hidden, NT).astype(BF16)
    skp_grad = dot(skp[:, :tokens], hidden, NT).astype(BF16)
    core = ch & 1
    for part, rows, cols in (
        (conv_grad.reshape(8, OUT_AT, 256), slice(0, OUT_AT), slice(0, 256)),
        (res_grad.reshape(8, 64, 128), slice(OUT_AT, PACKED), slice(0, 128)),
        (skp_grad.reshape(8, 64, 128), slice(OUT_AT, PACKED), slice(128, 256)),
    ):
        for i in range(4):
            even, odd = part[2 * i], part[2 * i + 1]
            kept[i, rows, cols] = jnp.where(core == 0, even, odd)
            given[i, rows, cols] = jnp.where(core == 0, odd, even)


def outputs(packed, hidden, grad_pre, z0, z1, z2, z3, natural):
    ch = lax.axis_index("chan")
    tokens, wide = 256, 384
    hidden = hidden[...]
    res_part = dot(packed[:, OUT_AT:PACKED, 0:128].reshape(RESID, 128), hidden)
    skp_part = dot(packed[:, OUT_AT:PACKED, 128:256].reshape(RESID, 128), hidden)
    prev = packed[:, 0:64, :].reshape(RESID, 256)
    now = packed[:, 64:128, :].reshape(RESID, 256)
    later = pltpu.roll(dot(prev, grad_pre[...]), wide - DILATION, 1)[:, :tokens]
    in_part = dot(now, grad_pre[:, :tokens]) + later
    for n, part in enumerate((res_part, skp_part, in_part)):
        for h in range(2):
            for r in range(8):
                natural[2 * n + h, pl.ds(r, 64, stride=8), :] = part[
                    64 * r : 64 * r + 64, 128 * h : 128 * h + 128
                ]
    for k, out in enumerate((z0, z1, z2, z3)):
        for i in range(4):
            rows = pl.ds(pl.multiple_of(32 * (ch ^ (4 * k + i)), 32), 32)
            for n in range(3):
                for h in range(2):
                    out[i, 32 * n : 32 * n + 32, 128 * h : 128 * h + 128] = natural[
                        2 * n + h, rows, :
                    ].astype(BF16)


def finish_tokens(o0, o1, o2, o3, sig, res, residual, skipped, grad_in):
    j = lax.axis_index("chan") & 3
    for k, piece in enumerate((o0, o1, o2, o3)):
        cut = pl.ds(pl.multiple_of((j ^ k) * 256, 256), 256)
        residual[:, cut] = sig[:, cut].astype(F32) + piece[0:32, :].astype(F32)
        skipped[:, cut] = piece[32:64, :].astype(F32)
        grad_in[:, cut] = res[:, cut].astype(F32) + piece[64:96, :].astype(F32)


def update(owned, grads, master, first, second, *refs):
    outs, held, old, grad, sems = refs[:3], refs[3:6], (*refs[6:8], first), refs[8], refs[9]
    slots = grads.shape[1]
    rows = 8 * slots
    steps = 8
    parts = [slice(n * rows // steps, (n + 1) * rows // steps) for n in range(steps)]
    fetches = []
    for n, part in enumerate(parts):
        for m, source in enumerate((second, master)):
            fetch = pltpu.make_async_copy(
                source.at[part, :], old[m].at[part, :], sems.at[3 * steps + 2 * n + m]
            )
            fetch.start()
            fetches.append(fetch)
    for r in range(8):
        for z in range(4):
            got = grads[16 * (r // 4) + 4 * z + r % 4].astype(F32)
            for h in range(2):
                grad[2 * z + h, pl.ds(r, slots, stride=8), :] = got[:, 128 * h : 128 * h + 128]
    unbias = 1.0 / (1.0 - MOMENT_DECAY**STEP)
    copies = []
    for n, part in enumerate(parts):
        for m in range(2):
            fetches[2 * n + m].wait()
        old_s, old_m, old_f = (ref[part, :] for ref in old)
        new = jnp.concatenate([grad[t, part, :] for t in range(8)], 1)
        keep = n * (rows // steps) + iota((rows // steps, 1), 0) < 8 * owned[0:1, 0:1]
        first_new = MOMENT_DECAY * old_f + (1.0 - MOMENT_DECAY) * new
        second_new = MOMENT_DECAY * old_s + (1.0 - MOMENT_DECAY) * new * new
        first_hat = first_new * unbias
        second_hat = second_new * unbias
        root = second_hat * lax.rsqrt(second_hat)
        stepped = old_m - STEP_RATE * (
            first_hat * pl.reciprocal(root + EPSILON) + WEIGHT_DECAY * old_m
        )
        held[0][part, :] = jnp.where(keep, first_new, old_f)
        held[1][part, :] = jnp.where(keep, second_new, old_s)
        held[2][part, :] = jnp.where(keep, stepped, old_m)
        for m in range(3):
            copy = pltpu.make_async_copy(
                held[m].at[part, :], outs[m].at[part, :], sems.at[3 * n + m]
            )
            copy.start()
            copies.append(copy)
    for copy in copies:
        copy.wait()


BOTH = ("tm", "chan")


def swap(x, k):
    n = lax.axis_size("chan")
    return lax.ppermute(x, "chan", [(i, i ^ k) for i in range(n)])


def local(
    signal, mel_frames, speaker_ids, owners, master, first_moment, second_moment, res_cot, skip_cot
):
    slots_dev = master.shape[0]
    slots = 16 * slots_dev
    flat = (8 * slots_dev, GATES)
    sig, res, skp, mel = signal.T, res_cot.T, skip_cot.T, mel_frames.T
    own_row = owners.reshape(1, NBLK)
    share = [[16 * y + 4 * z + j for y in range(2) for j in range(4)] for z in range(4)]
    sds = jax.ShapeDtypeStruct
    dma = pltpu.SemaphoreType.DMA

    acts, edges = call(
        begin,
        (sds((3, *sig.shape), BF16), sds((192, 128), BF16)),
        (HBM,) * 5,
        scratch=(pltpu.SMEM(speaker_ids.shape, jnp.int32), dma((5,))),
    )(speaker_ids, sig, res, skp, mel)
    other = lax.ppermute(edges, "tm", [(0, 1), (1, 0)])
    sent = call(
        pack_weights,
        sds((16, slots_dev, 256), BF16),
        (HBM,),
        scratch=(pltpu.VMEM((8, 8 * slots_dev, 128), F32), dma((8,))),
    )(master.reshape(flat))
    piece = sds((PIECE, 256), BF16)
    o = call(pack_tokens, (piece,) * 4, (VMEM,) * 2, gflops=200)(acts, other)
    arrived = lax.all_to_all(sent, "chan", 0, 0, tiled=True)
    mine = call(join, sds((400, 256), BF16), (VMEM,) * 4, gflops=0)(
        o[0], swap(o[1], 1), swap(o[2], 2), swap(o[3], 3)
    )
    p1, p2, p3 = (swap(mine, 4 * k) for k in (1, 2, 3))

    at_col, put, owned = call(
        functools.partial(place_blocks, slots_dev=slots_dev),
        (
            sds((PACKED, 128), jnp.int32),
            sds((slots, PACKED), BF16),
            sds((8, 128), jnp.int32),
        ),
        (SMEM, VMEM, VMEM),
    )(speaker_ids, own_row, other)
    arrived, _ = lax.optimization_barrier((arrived, mine))
    gathered = call(gather_blocks, sds((PACKED, 256), BF16), (VMEM, VMEM), gflops=200)(
        at_col, arrived.reshape(slots, 256)
    )
    packed = lax.all_gather(gathered, BOTH, axis_index_groups=share)
    rows = sds((4, PACKED, 256), BF16)
    kept, given, hidden, grad_pre = call(
        layer,
        (rows, rows, sds((128, 256), BF16), sds((256, 384), BF16)),
        (SMEM,) + (VMEM,) * 7,
        gflops=200,
        pinned=(2,),
        scratch=(
            pltpu.VMEM((8, OUT_AT, 384), BF16),
            pltpu.VMEM((RESID, 384), BF16),
            pltpu.VMEM((RESID, 384), BF16),
            pltpu.VMEM((7, RESID, 128), F32),
        ),
    )(speaker_ids, packed, mine, p1, p2, p3, mel, other)
    z0, z1, z2, z3 = call(
        outputs,
        (sds((4, 96, 256), BF16),) * 4,
        (VMEM,) * 3,
        gflops=0,
        scratch=(pltpu.VMEM((6, RESID, 128), F32),),
    )(packed, hidden, grad_pre)

    kept, _ = lax.optimization_barrier((kept, z0))
    n = lax.axis_size("chan")
    g = call(sum_cores, (sds((PACKED, 256), BF16),) * 4, (VMEM,) * 2)(kept, swap(given, 1))
    across = [(16 * y + i, 16 * (1 - y) + (i ^ 2)) for y in range(2) for i in range(n)]
    g = (g[0], swap(g[1], 2), lax.ppermute(g[2], "tm", [(0, 1), (1, 0)]), lax.ppermute(g[3], BOTH, across))
    t1, t2, t3 = (swap(z, 4 * k) for k, z in ((1, z1), (2, z2), (3, z3)))
    spread = call(scatter_blocks, sds((2, slots, 256), BF16), (VMEM,) * 5)(put, *g)
    returned = lax.all_to_all(spread.reshape(32, slots_dev, 256), BOTH, 0, 0)
    o = call(sum_units, (sds((96, 256), BF16),) * 4, (VMEM,) * 4, gflops=20)(z0, t1, t2, t3)
    o = (o[0], swap(o[1], 1), swap(o[2], 2), swap(o[3], 3))
    narrow = sds(sig.shape, F32)
    residual, skipped, grad_in = call(finish_tokens, (narrow,) * 3, (VMEM,) * 6)(*o, sig, res)
    new = call(
        update,
        (sds(flat, F32),) * 3,
        (VMEM, VMEM, HBM, VMEM, HBM),
        scratch=(pltpu.VMEM(flat, F32),) * 5
        + (pltpu.VMEM((8, flat[0], 128), F32), dma((40,))),
        out_space=HBM,
    )(
        owned,
        returned,
        master.reshape(flat),
        first_moment.reshape(flat),
        second_moment.reshape(flat),
    )
    return (residual.T, skipped.T, grad_in.T, *(x.reshape(master.shape) for x in new))


def place_index(owners, slots_dev):
    count = owners.shape[0]
    matches = owners[:, None] == owners[None, :]
    before = jnp.arange(count)[None, :] < jnp.arange(count)[:, None]
    ranks = jnp.sum((matches & before).astype(jnp.int32), axis=1)
    return owners * slots_dev + ranks


def local_plain(
    signal, mel_frames, speaker_ids, owners, master, first_moment, second_moment, res_cot, skip_cot
):
    chans = lax.axis_size("chan")
    slots_dev = master.shape[0]
    tok_count = signal.shape[0]
    hid_local = HIDDEN_SIZE // chans
    col_count = GATES // chans
    seg_count = speaker_ids.shape[0]
    spk_start = 2 * RESID + MELS
    out_start = spk_start + SPEAKERS
    places = place_index(owners, slots_dev)
    table = places[:, None] == jnp.arange(chans * slots_dev)[None, :]
    received = lax.all_to_all(
        master.astype(BF16), "chan", split_axis=2, concat_axis=0, tiled=True
    ).reshape(chans * slots_dev, BLOCK * col_count)
    params = jnp.dot(table.astype(BF16), received, preferred_element_type=F32)
    params = params.astype(BF16).reshape(ROWS, col_count)
    tap_prev, tap_now = params[:RESID], params[RESID : 2 * RESID]
    mel_proj = params[2 * RESID : spk_start]
    speaker_table = params[spk_start:out_start]
    out_cols = params[out_start:].reshape(RESID, hid_local, 2)
    n_tm = lax.axis_size("tm")
    tail_prev = lax.ppermute(signal[-DILATION:], "tm", [(i, i + 1) for i in range(n_tm - 1)])
    inputs = lax.all_gather(signal, "chan", axis=1, tiled=True)
    tail_full = lax.all_gather(tail_prev, "chan", axis=1, tiled=True)
    shifted = jnp.concatenate([tail_full, inputs[:-DILATION]], 0)
    pre_act = jnp.dot(shifted, tap_prev, preferred_element_type=F32)
    pre_act = pre_act + jnp.dot(inputs, tap_now, preferred_element_type=F32)
    pre_act = pre_act + jnp.dot(mel_frames, mel_proj, preferred_element_type=F32)
    one_hot = (speaker_ids[:, None] == jnp.arange(SPEAKERS)[None, :]).astype(BF16)
    embedded = jnp.dot(one_hot, speaker_table, preferred_element_type=F32)
    pre_act = (pre_act.reshape(seg_count, SEG, col_count) + embedded[:, None, :]).reshape(
        tok_count, col_count
    )
    filt = jnp.tanh(pre_act[:, 0::2])
    gates = jax.nn.sigmoid(pre_act[:, 1::2])
    hidden = (filt * gates).astype(BF16)
    summed = lax.psum_scatter(
        jnp.einsum("cuw,tu->cwt", out_cols, hidden, preferred_element_type=F32),
        "chan",
        scatter_dimension=0,
        tiled=True,
    )
    cots = lax.all_gather(
        jnp.stack([res_cot.T, skip_cot.T], axis=1), "chan", axis=0, tiled=True
    )
    grad_hid = jnp.einsum("cwt,cuw->tu", cots, out_cols, preferred_element_type=F32)
    term = jnp.einsum("cwt,tu->cuw", cots, hidden, preferred_element_type=F32)
    grad_filt = grad_hid * gates * (1.0 - filt * filt)
    grad_gate = grad_hid * filt * gates * (1.0 - gates)
    grad_pre = (
        jnp.stack([grad_filt, grad_gate], axis=2).reshape(tok_count, col_count).astype(BF16)
    )
    ahead = lax.ppermute(grad_pre[:DILATION], "tm", [(i + 1, i) for i in range(n_tm - 1)])
    later = jnp.concatenate([grad_pre[DILATION:], ahead], 0)
    input_part = lax.psum_scatter(
        dot(tap_now, grad_pre, NT) + dot(tap_prev, later, NT),
        "chan",
        scatter_dimension=0,
        tiled=True,
    )
    seg_sums = jnp.sum(grad_pre.astype(F32).reshape(seg_count, SEG, col_count), axis=1)
    grad_spk = lax.dot_general(
        one_hot.astype(F32),
        seg_sums,
        TN,
        precision=lax.Precision.HIGHEST,
        preferred_element_type=F32,
    )
    grad_params = jnp.concatenate(
        [
            dot(shifted, grad_pre, TN),
            dot(inputs, grad_pre, TN),
            dot(mel_frames, grad_pre, TN),
            grad_spk,
            term.reshape(RESID, col_count),
        ],
        0,
    )
    grad_params = lax.psum(grad_params, "tm").reshape(NBLK, BLOCK * col_count)
    outgoing = lax.dot_general(
        table.astype(F32), grad_params, TN, precision=lax.Precision.HIGHEST
    ).reshape(chans * slots_dev, BLOCK, col_count)
    grad_slots = lax.all_to_all(outgoing, "chan", split_axis=0, concat_axis=2, tiled=True)
    owned = jnp.sum((owners == lax.axis_index("chan")).astype(jnp.int32))
    keep = (jnp.arange(slots_dev) < owned)[:, None, None]
    first_new = MOMENT_DECAY * first_moment + (1.0 - MOMENT_DECAY) * grad_slots
    second_new = MOMENT_DECAY * second_moment + (1.0 - MOMENT_DECAY) * grad_slots * grad_slots
    first_hat = first_new / (1.0 - MOMENT_DECAY**STEP)
    second_hat = second_new / (1.0 - MOMENT_DECAY**STEP)
    stepped = master - STEP_RATE * (
        first_hat / (jnp.sqrt(second_hat) + EPSILON) + WEIGHT_DECAY * master
    )
    return (
        signal.astype(F32) + summed[:, 0, :].T,
        summed[:, 1, :].T,
        res_cot.astype(F32) + input_part.T,
        jnp.where(keep, first_new, first_moment),
        jnp.where(keep, second_new, second_moment),
        jnp.where(keep, stepped, master),
    )


def solution(mesh):
    wide = P("tm", "chan")
    slots = P("chan", None, None)
    packed_mesh = mesh.shape["tm"] == 2 and mesh.shape["chan"] == 16
    return jax.shard_map(
        local if packed_mesh else local_plain,
        mesh=mesh,
        in_specs=(wide, P("tm", None), P("tm"), P(), slots, slots, slots, wide, wide),
        out_specs=(wide, wide, wide, slots, slots, slots),
        check_vma=False,
    )
```

```python
import functools

import jax
import jax.numpy as jnp
from jax import lax
from jax.experimental import pallas as pl
from jax.experimental.pallas import tpu as pltpu
from jax.sharding import PartitionSpec as P

RESID = 512
HIDDEN_SIZE = 512
MELS = 80
SPEAKERS = 944
DILATION = 8
SEG = 128
BLOCK = 8
STEP = 5
GATES = 1024
ROWS = 2560
NBLK = 320

MOMENT_DECAY = 0.5
STEP_RATE = 0.03
WEIGHT_DECAY = 0.01
EPSILON = 1e-08

F32 = jnp.float32
BF16 = jnp.bfloat16
NN = (((1,), (0,)), ((), ()))
NT = (((1,), (1,)), ((), ()))
TN = (((0,), (0,)), ((), ()))

TAPS = 2 * RESID // BLOCK
MEL_AT = TAPS
MEL_BLOCKS = MELS // BLOCK
SEG_AT = 144
OUT_AT = 160
PACKED = 224
SPK_BLOCK = TAPS + MEL_BLOCKS
OUT_BLOCK = SPK_BLOCK + SPEAKERS // BLOCK
PIECE = 112


def dot(a, b, dims=NN):
    return lax.dot_general(a, b, dims, preferred_element_type=F32)


def iota(shape, dim):
    return lax.broadcasted_iota(jnp.int32, shape, dim)


def onehot(cond):
    return jnp.where(cond, 1.0, 0.0).astype(BF16)


KIB, MIB = 2**10, 2**20
VMEM, SMEM, HBM = pltpu.VMEM, pltpu.SMEM, pltpu.HBM


def call(kernel, out, spaces, gflops=0, scratch=(), out_space=VMEM, pinned=()):
    run = pl.pallas_call(
        kernel,
        out_shape=out,
        in_specs=[pl.BlockSpec(memory_space=space) for space in spaces],
        out_specs=jax.tree.map(lambda _: pl.BlockSpec(memory_space=out_space), out),
        scratch_shapes=list(scratch),
        compiler_params=pltpu.CompilerParams(vmem_limit_bytes=24 * MIB),
        cost_estimate=pl.CostEstimate(
            flops=gflops * 10**9, bytes_accessed=MIB, transcendentals=0
        ),
    )
    pin = pltpu.with_memory_space_constraint
    fixed = [space if space == HBM or n in pinned else None for n, space in enumerate(spaces)]
    return lambda *args: run(*(pin(x, f) if f else x for x, f in zip(args, fixed, strict=True)))


def gate_order(dim):
    natural, split = iota((256, 256), dim), iota((256, 256), 1 - dim)
    return onehot(natural == 2 * (split & 127) + (split >> 7))


def begin(speakers, master, sig, res, skp, mel, sent, acts, edges, strips, spk, sems):
    half = lax.axis_index("tm")
    slots = sent.shape[1]
    cut = pl.ds(pl.multiple_of((1 - half) * 896, 128), 128)
    moves = [(speakers, spk)]
    moves += [(part, acts.at[n]) for n, part in enumerate((sig, res, skp))]
    moves += [(mel.at[:, cut], edges.at[96:176, :])]
    moves += [(master.at[:, 128 * t : 128 * t + 128], strips.at[t]) for t in range(8)]
    copies = [pltpu.make_async_copy(a, b, sems.at[n]) for n, (a, b) in enumerate(moves)]
    for copy in copies:
        copy.start()
    copies[0].wait()
    row, lane = iota((16, 128), 0), iota((16, 128), 1)
    table = jnp.zeros((16, 128), jnp.int32)
    for s in range(8):
        code = jnp.where(row == 0, spk[s] >> 3, spk[s] & 7)
        table = jnp.where((lane == s) & (row < 2), code, table)
    edges[176:192, :] = table.astype(F32).astype(BF16)
    for copy in copies[1:5]:
        copy.wait()
    for n in range(3):
        edges[32 * n : 32 * n + 32, :] = acts[n, :, cut]
    for t in range(8):
        copies[5 + t].wait()
        lanes = slice(128 * (t % 2), 128 * (t % 2) + 128)
        for j in range(4):
            low = strips[t, pl.ds(j, slots, stride=8), :]
            high = strips[t, pl.ds(4 + j, slots, stride=8), :]
            sent[4 * (t // 2) + j, :, lanes] = jnp.where(half == 0, low, high).astype(BF16)


def pack_tokens(acts, other, o0, o1, o2, o3):
    sig, res, skp = (acts.at[n] for n in range(3))
    half, j = lax.axis_index("tm"), lax.axis_index("chan") & 3
    outs = (o0, o1, o2, o3)
    parts = (sig, res, skp)
    befores, nexts = [], ([], [], [])
    for k in range(4):
        to = j ^ k
        cut = pl.ds(pl.multiple_of(to * 256, 256), 256)
        for n, part in enumerate(parts):
            outs[k][32 * n : 32 * n + 32, :] = part[:, cut]
        cut = pl.ds(pl.multiple_of(jnp.maximum(to * 256 - 128, 0), 128), 128)
        edge = jnp.where(half == 1, other[0:32, :].astype(F32), 0.0)
        befores.append(jnp.where(to == 0, edge, sig[:, cut].astype(F32)))
        cut = pl.ds(pl.multiple_of(jnp.minimum(to * 256 + 256, 896), 128), 128)
        for n, part in enumerate(parts):
            edge = jnp.where(half == 0, other[32 * n : 32 * n + 32, :].astype(F32), 0.0)
            nexts[n].append(jnp.where(to == 3, edge, part[:, cut].astype(F32)))
    tall = [jnp.concatenate(x, 0).astype(BF16) for x in (befores, *nexts)]
    t, lane = iota((16, 128), 0), iota((16, 128), 1)
    top, low = t < DILATION, t >= DILATION
    head_top = onehot(top & (lane == t))
    head_low = onehot(low & (lane == t - DILATION))
    last_top = onehot(top & (lane == t + 120))
    rows = (
        dot(last_top, tall[0], NT) + dot(head_low, tall[1], NT),
        dot(head_top, tall[2], NT) + dot(head_low, tall[3], NT),
    )
    for k in range(4):
        for n in range(2):
            outs[k][96:112, 128 * n : 128 * n + 128] = jnp.where(
                (lane >> 5) == k, rows[n], 0.0
            ).astype(BF16)


def join(o0, o1, o2, o3, out):
    ends = o0[96:112, :].astype(F32)
    for piece in (o1, o2, o3):
        ends = ends + piece[96:112, :].astype(F32)
    for k, piece in enumerate((o0, o1, o2, o3)):
        out[96 * k : 96 * k + 96, :] = piece[0:96, :]
    out[384:400, :] = ends.astype(BF16)


def place_blocks(spk_ids, owners, other, at_col, put, owned, *, slots_dev):
    half = lax.axis_index("tm")
    own_row = owners[...]
    mine = jnp.where(own_row == lax.axis_index("chan"), 1, 0)
    owned[...] = jnp.broadcast_to(jnp.sum(mine, axis=1, keepdims=True), owned.shape)
    down, across = iota((NBLK, NBLK), 0), iota((NBLK, NBLK), 1)
    row_all = jnp.broadcast_to(own_row, (NBLK, NBLK))
    own_col = jnp.sum(jnp.where(down == across, row_all, 0), axis=1, keepdims=True)
    before = (own_col == row_all) & (down < across)
    rank = jnp.sum(jnp.where(before, 1, 0), axis=0, keepdims=True)
    place = own_row * slots_dev + rank
    n = iota((PACKED, 128), 0)
    far = n - SEG_AT - 8 * (1 - half) == iota((PACKED, 128), 1)
    blocks = jnp.broadcast_to(other[176:192, :].astype(F32)[0:1], (PACKED, 128))
    spk = jnp.sum(jnp.where(far, blocks, 0.0), axis=1, keepdims=True).astype(jnp.int32)
    n = iota((PACKED, 1), 0)
    for s in range(8):
        spk = jnp.where(n == SEG_AT + 8 * half + s, spk_ids[s] >> 3, spk)
    blk = jnp.where(
        n < SPK_BLOCK,
        n,
        jnp.where(n < SEG_AT, -1, jnp.where(n < OUT_AT, SPK_BLOCK + spk, n + (OUT_BLOCK - OUT_AT))),
    )
    match = jnp.broadcast_to(blk, (PACKED, NBLK)) == iota((PACKED, NBLK), 1)
    at = jnp.sum(jnp.where(match, jnp.broadcast_to(place, (PACKED, NBLK)), 0), axis=1, keepdims=True)
    at = jnp.where(blk < 0, -1, at)
    at_col[...] = jnp.broadcast_to(at, (PACKED, 128))
    same = iota((PACKED, PACKED), 0) == iota((PACKED, PACKED), 1)
    row = jnp.sum(jnp.where(same, jnp.broadcast_to(at, (PACKED, PACKED)), 0), axis=0, keepdims=True)
    put[...] = onehot(jnp.broadcast_to(row, put.shape) == iota(put.shape, 0))


def gather_blocks(at_col, slots, out):
    shape = (PACKED, slots.shape[0])
    pick = onehot(jnp.broadcast_to(at_col[:, 0:1], shape) == iota(shape, 1))
    got = dot(pick, slots[...]).astype(BF16)
    out[...] = dot(got, gate_order(0)).astype(BF16)


def sum_cores(kept, got, *outs):
    i = 2 * lax.axis_index("tm") + ((lax.axis_index("chan") >> 1) & 1)
    for k, out in enumerate(outs):
        out[...] = (kept[i ^ k] + got[i ^ k].astype(F32)).astype(out.dtype)


def scatter_blocks(put, p0, p1, p2, p3, out):
    total = p0[...].astype(F32)
    for part in (p1, p2, p3):
        total = total + part[...].astype(F32)
    natural = dot(total.astype(BF16), gate_order(1)).astype(BF16)
    spread = dot(put[...], natural).astype(BF16)
    out[0] = spread
    out[1] = spread


def sum_units(z0, z1, z2, z3, o0, o1, o2, o3):
    for i, out in enumerate((o0, o1, o2, o3)):
        out[...] = (
            z0[i].astype(F32) + z1[i].astype(F32) + z2[i].astype(F32) + z3[i].astype(F32)
        ).astype(BF16)


def layer(spk, packed, o0, o1, o2, o3, p1, p2, p3, mel, other, kept, given, hidden_out, grad_out, feat, res, skp, natural, p0):
    join(o0, o1, o2, o3, p0)
    half, ch = lax.axis_index("tm"), lax.axis_index("chan")
    j = ch & 3
    got = (p0, p1, p2, p3)
    tokens, wide = 256, 384
    for k in range(4):
        for i in range(4):
            rows = pl.ds(pl.multiple_of(32 * (ch ^ (4 * k + i)), 32), 32)
            for n in range(3):
                at = 96 * i + 32 * n
                for h in range(2):
                    natural[2 * n + h, rows, :] = got[k][at : at + 32, 128 * h : 128 * h + 128].astype(F32)

    ends = [part[384:400, :].astype(F32) for part in got]
    gap = jnp.zeros((96, 128), F32)
    for k, end in enumerate(ends):
        left, right = end[:, 0:128], end[:, 128:256]
        tile = jnp.concatenate([left[8:16], right, gap, left[0:8]], 0).T
        for i in range(4):
            rows = pl.ds(pl.multiple_of(32 * (ch ^ (4 * k + i)), 32), 32)
            natural[6, rows, :] = tile[32 * i : 32 * i + 32]

    def majors(n):
        return jnp.concatenate([natural[n, pl.ds(r, 64, stride=8), :] for r in range(8)], 0)

    tile = majors(6)
    sig = jnp.concatenate([majors(0), majors(1), tile], 1)
    for n, out in ((1, res), (2, skp)):
        out[:, 0:128] = majors(2 * n).astype(BF16)
        out[:, 128:256] = majors(2 * n + 1).astype(BF16)
        out[:, 256:384] = pltpu.roll(tile, 128 - 8 * n, 1).astype(BF16)
    shifted = pltpu.roll(sig, DILATION, 1).astype(BF16)
    sig = sig.astype(BF16)
    m = iota((128, MELS), 0)
    mel_pick = onehot(((m & 15) < MEL_BLOCKS) & (iota((128, MELS), 1) == 8 * (m & 15) + (m >> 4)))
    cut = pl.ds(pl.multiple_of(j * tokens, tokens), tokens)
    far = pl.ds(pl.multiple_of(jnp.minimum(j * tokens + tokens, 896), 128), 128)
    ahead = jnp.where(j == 3, other[96:176, :].astype(F32), mel[:, far].astype(F32)).astype(BF16)
    mels = jnp.concatenate([dot(mel_pick, mel[:, cut]), dot(mel_pick, ahead)], 1).astype(BF16)
    seg = 8 * half + 2 * j
    row, lane = iota((16, wide), 0), iota((16, wide), 1)
    beyond = other[176:192, :].astype(F32)[1:2, 0:1].astype(jnp.int32)
    beyond = jnp.where(j == 3, beyond, spk[jnp.minimum(2 * j + 2, 7)] & 7)
    sub = jnp.where(
        lane < SEG,
        spk[2 * j] & 7,
        jnp.where(lane < 2 * SEG, spk[2 * j + 1] & 7, jnp.broadcast_to(beyond, (16, wide))),
    )
    for r in range(8):
        feat[r, 0:64] = shifted[64 * r : 64 * r + 64]
        feat[r, 64:128] = sig[64 * r : 64 * r + 64]
        feat[r, 128:144] = mels[16 * r : 16 * r + 16]
        feat[r, 144:160] = onehot((row == seg + (lane >> 7)) & (sub == r))
    features = feat[...].reshape(8 * OUT_AT, wide)
    conv = packed[:, 0:OUT_AT, :].reshape(8 * OUT_AT, 256)
    pre = dot(conv, features, TN)
    filt = jnp.tanh(pre[:128])
    gate = jax.nn.sigmoid(pre[128:])
    hidden = (filt[:, :tokens] * gate[:, :tokens]).astype(BF16)
    out_res = packed[:, OUT_AT:PACKED, 0:128].reshape(RESID, 128)
    out_skp = packed[:, OUT_AT:PACKED, 128:256].reshape(RESID, 128)
    hidden_out[...] = hidden
    grad_hidden = dot(out_res, res[...], TN) + dot(out_skp, skp[...], TN)
    grad_pre = jnp.concatenate(
        [
            grad_hidden * gate * (1.0 - filt * filt),
            grad_hidden * filt * gate * (1.0 - gate),
        ],
        0,
    ).astype(BF16)
    grad_out[...] = grad_pre
    grad_pre = grad_pre[:, :tokens]
    conv_grad = dot(features[:, :tokens], grad_pre, NT)
    res_grad = dot(res[:, :tokens], hidden, NT)
    skp_grad = dot(skp[:, :tokens], hidden, NT)
    core = ch & 1
    for part, rows, cols in (
        (conv_grad.reshape(8, OUT_AT, 256), slice(0, OUT_AT), slice(0, 256)),
        (res_grad.reshape(8, 64, 128), slice(OUT_AT, PACKED), slice(0, 128)),
        (skp_grad.reshape(8, 64, 128), slice(OUT_AT, PACKED), slice(128, 256)),
    ):
        for i in range(4):
            even, odd = part[2 * i], part[2 * i + 1]
            kept[i, rows, cols] = jnp.where(core == 0, even, odd)
            given[i, rows, cols] = jnp.where(core == 0, odd, even).astype(BF16)


def outputs(packed, hidden, grad_pre, z0, z1, z2, z3, natural):
    ch = lax.axis_index("chan")
    tokens, wide = 256, 384
    hidden = hidden[...]
    res_part = dot(packed[:, OUT_AT:PACKED, 0:128].reshape(RESID, 128), hidden)
    skp_part = dot(packed[:, OUT_AT:PACKED, 128:256].reshape(RESID, 128), hidden)
    prev = packed[:, 0:64, :].reshape(RESID, 256)
    now = packed[:, 64:128, :].reshape(RESID, 256)
    later = pltpu.roll(dot(prev, grad_pre[...]), wide - DILATION, 1)[:, :tokens]
    in_part = dot(now, grad_pre[:, :tokens]) + later
    for n, part in enumerate((res_part, skp_part, in_part)):
        for h in range(2):
            for r in range(8):
                natural[2 * n + h, pl.ds(r, 64, stride=8), :] = part[
                    64 * r : 64 * r + 64, 128 * h : 128 * h + 128
                ]
    for k, out in enumerate((z0, z1, z2, z3)):
        for i in range(4):
            rows = pl.ds(pl.multiple_of(32 * (ch ^ (4 * k + i)), 32), 32)
            for n in range(3):
                for h in range(2):
                    out[i, 32 * n : 32 * n + 32, 128 * h : 128 * h + 128] = natural[
                        2 * n + h, rows, :
                    ].astype(BF16)


def finish_tokens(o0, o1, o2, o3, sig, res, residual, skipped, grad_in):
    j = lax.axis_index("chan") & 3
    for k, piece in enumerate((o0, o1, o2, o3)):
        cut = pl.ds(pl.multiple_of((j ^ k) * 256, 256), 256)
        residual[:, cut] = sig[:, cut].astype(F32) + piece[0:32, :].astype(F32)
        skipped[:, cut] = piece[32:64, :].astype(F32)
        grad_in[:, cut] = res[:, cut].astype(F32) + piece[64:96, :].astype(F32)


def update(owned, grads, master, first, second, *refs):
    outs, held, old, grad, sems = refs[:3], refs[3:6], (*refs[6:8], first), refs[8], refs[9]
    slots = grads.shape[1]
    rows = 8 * slots
    steps = 8
    parts = [slice(n * rows // steps, (n + 1) * rows // steps) for n in range(steps)]
    fetches = []
    for n, part in enumerate(parts):
        for m, source in enumerate((second, master)):
            fetch = pltpu.make_async_copy(
                source.at[part, :], old[m].at[part, :], sems.at[3 * steps + 2 * n + m]
            )
            fetch.start()
            fetches.append(fetch)
    for r in range(8):
        for z in range(4):
            got = grads[16 * (r // 4) + 4 * z + r % 4].astype(F32)
            for h in range(2):
                grad[2 * z + h, pl.ds(r, slots, stride=8), :] = got[:, 128 * h : 128 * h + 128]
    unbias = 1.0 / (1.0 - MOMENT_DECAY**STEP)
    copies = []
    for n, part in enumerate(parts):
        for m in range(2):
            fetches[2 * n + m].wait()
        old_s, old_m, old_f = (ref[part, :] for ref in old)
        new = jnp.concatenate([grad[t, part, :] for t in range(8)], 1)
        keep = n * (rows // steps) + iota((rows // steps, 1), 0) < 8 * owned[0:1, 0:1]
        first_new = MOMENT_DECAY * old_f + (1.0 - MOMENT_DECAY) * new
        second_new = MOMENT_DECAY * old_s + (1.0 - MOMENT_DECAY) * new * new
        first_hat = first_new * unbias
        second_hat = second_new * unbias
        root = second_hat * lax.rsqrt(second_hat)
        stepped = old_m - STEP_RATE * (
            first_hat * pl.reciprocal(root + EPSILON) + WEIGHT_DECAY * old_m
        )
        held[0][part, :] = jnp.where(keep, first_new, old_f)
        held[1][part, :] = jnp.where(keep, second_new, old_s)
        held[2][part, :] = jnp.where(keep, stepped, old_m)
        for m in range(3):
            copy = pltpu.make_async_copy(
                held[m].at[part, :], outs[m].at[part, :], sems.at[3 * n + m]
            )
            copy.start()
            copies.append(copy)
    for copy in copies:
        copy.wait()


BOTH = ("tm", "chan")


def swap(x, k):
    n = lax.axis_size("chan")
    return lax.ppermute(x, "chan", [(i, i ^ k) for i in range(n)])


def local(
    signal, mel_frames, speaker_ids, owners, master, first_moment, second_moment, res_cot, skip_cot
):
    slots_dev = master.shape[0]
    slots = 16 * slots_dev
    flat = (8 * slots_dev, GATES)
    sig, res, skp, mel = signal.T, res_cot.T, skip_cot.T, mel_frames.T
    own_row = owners.reshape(1, NBLK)
    share = [[16 * y + 4 * z + j for y in range(2) for j in range(4)] for z in range(4)]
    sds = jax.ShapeDtypeStruct
    dma = pltpu.SemaphoreType.DMA

    sent, acts, edges = call(
        begin,
        (sds((16, slots_dev, 256), BF16), sds((3, *sig.shape), BF16), sds((192, 128), BF16)),
        (HBM,) * 6,
        scratch=(
            pltpu.VMEM((8, 8 * slots_dev, 128), F32),
            pltpu.SMEM(speaker_ids.shape, jnp.int32),
            dma((13,)),
        ),
    )(speaker_ids, master.reshape(flat), sig, res, skp, mel)
    other = lax.ppermute(edges, "tm", [(0, 1), (1, 0)])
    piece = sds((PIECE, 256), BF16)
    o = call(pack_tokens, (piece,) * 4, (VMEM,) * 2, gflops=200)(acts, other)
    arrived = lax.all_to_all(sent, "chan", 0, 0, tiled=True)
    o = (o[0], swap(o[1], 1), swap(o[2], 2), swap(o[3], 3))
    mine = call(join, sds((400, 256), BF16), (VMEM,) * 4)(*o)
    p1, p2, p3 = (swap(mine, 4 * k) for k in (1, 2, 3))

    at_col, put, owned = call(
        functools.partial(place_blocks, slots_dev=slots_dev),
        (
            sds((PACKED, 128), jnp.int32),
            sds((slots, PACKED), BF16),
            sds((8, 128), jnp.int32),
        ),
        (SMEM, VMEM, VMEM),
    )(speaker_ids, own_row, other)
    arrived, _ = lax.optimization_barrier((arrived, mine))
    gathered = call(gather_blocks, sds((PACKED, 256), BF16), (VMEM, VMEM), gflops=200)(
        at_col, arrived.reshape(slots, 256)
    )
    packed = lax.all_gather(gathered, BOTH, axis_index_groups=share)
    rows = (4, PACKED, 256)
    kept, given, hidden, grad_pre = call(
        layer,
        (sds(rows, F32), sds(rows, BF16), sds((128, 256), BF16), sds((256, 384), BF16)),
        (SMEM,) + (VMEM,) * 10,
        gflops=200,
        scratch=(
            pltpu.VMEM((8, OUT_AT, 384), BF16),
            pltpu.VMEM((RESID, 384), BF16),
            pltpu.VMEM((RESID, 384), BF16),
            pltpu.VMEM((7, RESID, 128), F32),
            pltpu.VMEM((400, 256), BF16),
        ),
    )(speaker_ids, packed, *o, p1, p2, p3, mel, other)
    z0, z1, z2, z3 = call(
        outputs,
        (sds((4, 96, 256), BF16),) * 4,
        (VMEM,) * 3,
        gflops=0,
        scratch=(pltpu.VMEM((6, RESID, 128), F32),),
    )(packed, hidden, grad_pre)

    kept, _ = lax.optimization_barrier((kept, z0))
    n = lax.axis_size("chan")
    g = call(sum_cores, tuple(sds((PACKED, 256), t) for t in (F32, BF16, BF16, BF16)), (VMEM,) * 2)(kept, swap(given, 1))
    across = [(16 * y + i, 16 * (1 - y) + (i ^ 2)) for y in range(2) for i in range(n)]
    g = (g[0], swap(g[1], 2), lax.ppermute(g[2], "tm", [(0, 1), (1, 0)]), lax.ppermute(g[3], BOTH, across))
    t1, t2, t3 = (swap(z, 4 * k) for k, z in ((1, z1), (2, z2), (3, z3)))
    spread = call(scatter_blocks, sds((2, slots, 256), BF16), (VMEM,) * 5)(put, *g)
    returned = lax.all_to_all(spread.reshape(32, slots_dev, 256), BOTH, 0, 0)
    o = call(sum_units, (sds((96, 256), BF16),) * 4, (VMEM,) * 4, gflops=20)(z0, t1, t2, t3)
    o = (o[0], swap(o[1], 1), swap(o[2], 2), swap(o[3], 3))
    narrow = sds(sig.shape, F32)
    residual, skipped, grad_in = call(finish_tokens, (narrow,) * 3, (VMEM,) * 6)(*o, sig, res)
    new = call(
        update,
        (sds(flat, F32),) * 3,
        (VMEM, VMEM, HBM, VMEM, HBM),
        scratch=(pltpu.VMEM(flat, F32),) * 5
        + (pltpu.VMEM((8, flat[0], 128), F32), dma((40,))),
        out_space=HBM,
    )(
        owned,
        returned,
        master.reshape(flat),
        first_moment.reshape(flat),
        second_moment.reshape(flat),
    )
    return (residual.T, skipped.T, grad_in.T, *(x.reshape(master.shape) for x in new))


def place_index(owners, slots_dev):
    count = owners.shape[0]
    matches = owners[:, None] == owners[None, :]
    before = jnp.arange(count)[None, :] < jnp.arange(count)[:, None]
    ranks = jnp.sum((matches & before).astype(jnp.int32), axis=1)
    return owners * slots_dev + ranks


def local_plain(
    signal, mel_frames, speaker_ids, owners, master, first_moment, second_moment, res_cot, skip_cot
):
    chans = lax.axis_size("chan")
    slots_dev = master.shape[0]
    tok_count = signal.shape[0]
    hid_local = HIDDEN_SIZE // chans
    col_count = GATES // chans
    seg_count = speaker_ids.shape[0]
    spk_start = 2 * RESID + MELS
    out_start = spk_start + SPEAKERS
    places = place_index(owners, slots_dev)
    table = places[:, None] == jnp.arange(chans * slots_dev)[None, :]
    received = lax.all_to_all(
        master.astype(BF16), "chan", split_axis=2, concat_axis=0, tiled=True
    ).reshape(chans * slots_dev, BLOCK * col_count)
    params = jnp.dot(table.astype(BF16), received, preferred_element_type=F32)
    params = params.astype(BF16).reshape(ROWS, col_count)
    tap_prev, tap_now = params[:RESID], params[RESID : 2 * RESID]
    mel_proj = params[2 * RESID : spk_start]
    speaker_table = params[spk_start:out_start]
    out_cols = params[out_start:].reshape(RESID, hid_local, 2)
    n_tm = lax.axis_size("tm")
    tail_prev = lax.ppermute(signal[-DILATION:], "tm", [(i, i + 1) for i in range(n_tm - 1)])
    inputs = lax.all_gather(signal, "chan", axis=1, tiled=True)
    tail_full = lax.all_gather(tail_prev, "chan", axis=1, tiled=True)
    shifted = jnp.concatenate([tail_full, inputs[:-DILATION]], 0)
    pre_act = jnp.dot(shifted, tap_prev, preferred_element_type=F32)
    pre_act = pre_act + jnp.dot(inputs, tap_now, preferred_element_type=F32)
    pre_act = pre_act + jnp.dot(mel_frames, mel_proj, preferred_element_type=F32)
    one_hot = (speaker_ids[:, None] == jnp.arange(SPEAKERS)[None, :]).astype(BF16)
    embedded = jnp.dot(one_hot, speaker_table, preferred_element_type=F32)
    pre_act = (pre_act.reshape(seg_count, SEG, col_count) + embedded[:, None, :]).reshape(
        tok_count, col_count
    )
    filt = jnp.tanh(pre_act[:, 0::2])
    gates = jax.nn.sigmoid(pre_act[:, 1::2])
    hidden = (filt * gates).astype(BF16)
    summed = lax.psum_scatter(
        jnp.einsum("cuw,tu->cwt", out_cols, hidden, preferred_element_type=F32),
        "chan",
        scatter_dimension=0,
        tiled=True,
    )
    cots = lax.all_gather(
        jnp.stack([res_cot.T, skip_cot.T], axis=1), "chan", axis=0, tiled=True
    )
    grad_hid = jnp.einsum("cwt,cuw->tu", cots, out_cols, preferred_element_type=F32)
    term = jnp.einsum("cwt,tu->cuw", cots, hidden, preferred_element_type=F32)
    grad_filt = grad_hid * gates * (1.0 - filt * filt)
    grad_gate = grad_hid * filt * gates * (1.0 - gates)
    grad_pre = (
        jnp.stack([grad_filt, grad_gate], axis=2).reshape(tok_count, col_count).astype(BF16)
    )
    ahead = lax.ppermute(grad_pre[:DILATION], "tm", [(i + 1, i) for i in range(n_tm - 1)])
    later = jnp.concatenate([grad_pre[DILATION:], ahead], 0)
    input_part = lax.psum_scatter(
        dot(tap_now, grad_pre, NT) + dot(tap_prev, later, NT),
        "chan",
        scatter_dimension=0,
        tiled=True,
    )
    seg_sums = jnp.sum(grad_pre.astype(F32).reshape(seg_count, SEG, col_count), axis=1)
    grad_spk = lax.dot_general(
        one_hot.astype(F32),
        seg_sums,
        TN,
        precision=lax.Precision.HIGHEST,
        preferred_element_type=F32,
    )
    grad_params = jnp.concatenate(
        [
            dot(shifted, grad_pre, TN),
            dot(inputs, grad_pre, TN),
            dot(mel_frames, grad_pre, TN),
            grad_spk,
            term.reshape(RESID, col_count),
        ],
        0,
    )
    grad_params = lax.psum(grad_params, "tm").reshape(NBLK, BLOCK * col_count)
    outgoing = lax.dot_general(
        table.astype(F32), grad_params, TN, precision=lax.Precision.HIGHEST
    ).reshape(chans * slots_dev, BLOCK, col_count)
    grad_slots = lax.all_to_all(outgoing, "chan", split_axis=0, concat_axis=2, tiled=True)
    owned = jnp.sum((owners == lax.axis_index("chan")).astype(jnp.int32))
    keep = (jnp.arange(slots_dev) < owned)[:, None, None]
    first_new = MOMENT_DECAY * first_moment + (1.0 - MOMENT_DECAY) * grad_slots
    second_new = MOMENT_DECAY * second_moment + (1.0 - MOMENT_DECAY) * grad_slots * grad_slots
    first_hat = first_new / (1.0 - MOMENT_DECAY**STEP)
    second_hat = second_new / (1.0 - MOMENT_DECAY**STEP)
    stepped = master - STEP_RATE * (
        first_hat / (jnp.sqrt(second_hat) + EPSILON) + WEIGHT_DECAY * master
    )
    return (
        signal.astype(F32) + summed[:, 0, :].T,
        summed[:, 1, :].T,
        res_cot.astype(F32) + input_part.T,
        jnp.where(keep, first_new, first_moment),
        jnp.where(keep, second_new, second_moment),
        jnp.where(keep, stepped, master),
    )


def solution(mesh):
    wide = P("tm", "chan")
    slots = P("chan", None, None)
    packed_mesh = mesh.shape["tm"] == 2 and mesh.shape["chan"] == 16
    return jax.shard_map(
        local if packed_mesh else local_plain,
        mesh=mesh,
        in_specs=(wide, P("tm", None), P("tm"), P(), slots, slots, slots, wide, wide),
        out_specs=(wide, wide, wide, slots, slots, slots),
        check_vma=False,
    )
```

```python
import functools

import jax
import jax.numpy as jnp
from jax import lax
from jax.experimental import pallas as pl
from jax.experimental.pallas import tpu as pltpu
from jax.sharding import PartitionSpec as P

RESID = 512
HIDDEN_SIZE = 512
MELS = 80
SPEAKERS = 944
DILATION = 8
SEG = 128
BLOCK = 8
STEP = 5
GATES = 1024
ROWS = 2560
NBLK = 320

MOMENT_DECAY = 0.5
STEP_RATE = 0.03
WEIGHT_DECAY = 0.01
EPSILON = 1e-08

F32 = jnp.float32
BF16 = jnp.bfloat16
NN = (((1,), (0,)), ((), ()))
NT = (((1,), (1,)), ((), ()))
TN = (((0,), (0,)), ((), ()))

TAPS = 2 * RESID // BLOCK
MEL_AT = TAPS
MEL_BLOCKS = MELS // BLOCK
SEG_AT = 144
OUT_AT = 160
PACKED = 224
SPK_BLOCK = TAPS + MEL_BLOCKS
OUT_BLOCK = SPK_BLOCK + SPEAKERS // BLOCK
PIECE = 112


def dot(a, b, dims=NN):
    return lax.dot_general(a, b, dims, preferred_element_type=F32)


def iota(shape, dim):
    return lax.broadcasted_iota(jnp.int32, shape, dim)


def onehot(cond):
    return jnp.where(cond, 1.0, 0.0).astype(BF16)


KIB, MIB = 2**10, 2**20
VMEM, SMEM, HBM = pltpu.VMEM, pltpu.SMEM, pltpu.HBM


def call(kernel, out, spaces, gflops=0, scratch=(), out_space=VMEM, pinned=()):
    out_spaces = out_space if isinstance(out_space, tuple) else jax.tree.map(lambda _: out_space, out)
    run = pl.pallas_call(
        kernel,
        out_shape=out,
        in_specs=[pl.BlockSpec(memory_space=space) for space in spaces],
        out_specs=jax.tree.map(lambda _, space: pl.BlockSpec(memory_space=space), out, out_spaces),
        scratch_shapes=list(scratch),
        compiler_params=pltpu.CompilerParams(vmem_limit_bytes=24 * MIB),
        cost_estimate=pl.CostEstimate(
            flops=gflops * 10**9, bytes_accessed=MIB, transcendentals=0
        ),
    )
    pin = pltpu.with_memory_space_constraint
    fixed = [space if space == HBM or n in pinned else None for n, space in enumerate(spaces)]
    return lambda *args: run(*(pin(x, f) if f else x for x, f in zip(args, fixed, strict=True)))


def gate_order(dim):
    natural, split = iota((256, 256), dim), iota((256, 256), 1 - dim)
    return onehot(natural == 2 * (split & 127) + (split >> 7))


def begin(speakers, master, sig, res, skp, mel, sent, acts, edges, strips, packed, spk, sems):
    half = lax.axis_index("tm")
    slots = sent.shape[1]
    cut = pl.ds(pl.multiple_of((1 - half) * 896, 128), 128)
    moves = [(speakers, spk)]
    moves += [(part, acts.at[n]) for n, part in enumerate((sig, res, skp))]
    moves += [(mel.at[:, cut], edges.at[96:176, :])]
    moves += [(master.at[:, 128 * t : 128 * t + 128], strips.at[t]) for t in range(8)]
    copies = [pltpu.make_async_copy(a, b, sems.at[n]) for n, (a, b) in enumerate(moves)]
    for copy in copies:
        copy.start()
    copies[0].wait()
    row, lane = iota((16, 128), 0), iota((16, 128), 1)
    table = jnp.zeros((16, 128), jnp.int32)
    for s in range(8):
        code = jnp.where(row == 0, spk[s] >> 3, spk[s] & 7)
        table = jnp.where((lane == s) & (row < 2), code, table)
    edges[176:192, :] = table.astype(F32).astype(BF16)
    for copy in copies[1:5]:
        copy.wait()
    for n in range(3):
        edges[32 * n : 32 * n + 32, :] = acts[n, :, cut]
    for t in range(8):
        copies[5 + t].wait()
        lanes = slice(128 * (t % 2), 128 * (t % 2) + 128)
        for j in range(4):
            low = strips[t, pl.ds(j, slots, stride=8), :]
            high = strips[t, pl.ds(4 + j, slots, stride=8), :]
            packed[4 * (t // 2) + j, :, lanes] = jnp.where(half == 0, low, high).astype(BF16)
        if t % 2:
            part = slice(2 * t - 2, 2 * t + 2)
            copies.append(pltpu.make_async_copy(packed.at[part], sent.at[part], sems.at[13 + t // 2]))
            copies[-1].start()
    for copy in copies[13:]:
        copy.wait()


def pack_tokens(acts, other, o0, o1, o2, o3):
    sig, res, skp = (acts.at[n] for n in range(3))
    half, j = lax.axis_index("tm"), lax.axis_index("chan") & 3
    outs = (o0, o1, o2, o3)
    parts = (sig, res, skp)
    befores, nexts = [], ([], [], [])
    for k in range(4):
        to = j ^ k
        cut = pl.ds(pl.multiple_of(to * 256, 256), 256)
        for n, part in enumerate(parts):
            outs[k][32 * n : 32 * n + 32, :] = part[:, cut]
        cut = pl.ds(pl.multiple_of(jnp.maximum(to * 256 - 128, 0), 128), 128)
        edge = jnp.where(half == 1, other[0:32, :].astype(F32), 0.0)
        befores.append(jnp.where(to == 0, edge, sig[:, cut].astype(F32)))
        cut = pl.ds(pl.multiple_of(jnp.minimum(to * 256 + 256, 896), 128), 128)
        for n, part in enumerate(parts):
            edge = jnp.where(half == 0, other[32 * n : 32 * n + 32, :].astype(F32), 0.0)
            nexts[n].append(jnp.where(to == 3, edge, part[:, cut].astype(F32)))
    tall = [jnp.concatenate(x, 0).astype(BF16) for x in (befores, *nexts)]
    t, lane = iota((16, 128), 0), iota((16, 128), 1)
    top, low = t < DILATION, t >= DILATION
    head_top = onehot(top & (lane == t))
    head_low = onehot(low & (lane == t - DILATION))
    last_top = onehot(top & (lane == t + 120))
    rows = (
        dot(last_top, tall[0], NT) + dot(head_low, tall[1], NT),
        dot(head_top, tall[2], NT) + dot(head_low, tall[3], NT),
    )
    for k in range(4):
        for n in range(2):
            outs[k][96:112, 128 * n : 128 * n + 128] = jnp.where(
                (lane >> 5) == k, rows[n], 0.0
            ).astype(BF16)


def join(o0, o1, o2, o3, out):
    ends = o0[96:112, :].astype(F32)
    for piece in (o1, o2, o3):
        ends = ends + piece[96:112, :].astype(F32)
    for k, piece in enumerate((o0, o1, o2, o3)):
        out[96 * k : 96 * k + 96, :] = piece[0:96, :]
    out[384:400, :] = ends.astype(BF16)


def place_blocks(spk_ids, owners, other, at_col, put, owned, *, slots_dev):
    half = lax.axis_index("tm")
    own_row = owners[...]
    mine = jnp.where(own_row == lax.axis_index("chan"), 1, 0)
    owned[...] = jnp.broadcast_to(jnp.sum(mine, axis=1, keepdims=True), owned.shape)
    down, across = iota((NBLK, NBLK), 0), iota((NBLK, NBLK), 1)
    row_all = jnp.broadcast_to(own_row, (NBLK, NBLK))
    own_col = jnp.sum(jnp.where(down == across, row_all, 0), axis=1, keepdims=True)
    before = (own_col == row_all) & (down < across)
    rank = jnp.sum(jnp.where(before, 1, 0), axis=0, keepdims=True)
    place = own_row * slots_dev + rank
    n = iota((PACKED, 128), 0)
    far = n - SEG_AT - 8 * (1 - half) == iota((PACKED, 128), 1)
    blocks = jnp.broadcast_to(other[176:192, :].astype(F32)[0:1], (PACKED, 128))
    spk = jnp.sum(jnp.where(far, blocks, 0.0), axis=1, keepdims=True).astype(jnp.int32)
    n = iota((PACKED, 1), 0)
    for s in range(8):
        spk = jnp.where(n == SEG_AT + 8 * half + s, spk_ids[s] >> 3, spk)
    blk = jnp.where(
        n < SPK_BLOCK,
        n,
        jnp.where(n < SEG_AT, -1, jnp.where(n < OUT_AT, SPK_BLOCK + spk, n + (OUT_BLOCK - OUT_AT))),
    )
    match = jnp.broadcast_to(blk, (PACKED, NBLK)) == iota((PACKED, NBLK), 1)
    at = jnp.sum(jnp.where(match, jnp.broadcast_to(place, (PACKED, NBLK)), 0), axis=1, keepdims=True)
    at = jnp.where(blk < 0, -1, at)
    at_col[...] = jnp.broadcast_to(at, (PACKED, 128))
    same = iota((PACKED, PACKED), 0) == iota((PACKED, PACKED), 1)
    row = jnp.sum(jnp.where(same, jnp.broadcast_to(at, (PACKED, PACKED)), 0), axis=0, keepdims=True)
    put[...] = onehot(jnp.broadcast_to(row, put.shape) == iota(put.shape, 0))


def gather_blocks(at_col, slots, out):
    shape = (PACKED, slots.shape[0])
    pick = onehot(jnp.broadcast_to(at_col[:, 0:1], shape) == iota(shape, 1))
    got = dot(pick, slots[...]).astype(BF16)
    out[...] = dot(got, gate_order(0)).astype(BF16)


def sum_cores(kept, got, *outs):
    i = 2 * lax.axis_index("tm") + ((lax.axis_index("chan") >> 1) & 1)
    for k, out in enumerate(outs):
        out[...] = (kept[i ^ k] + got[i ^ k].astype(F32)).astype(out.dtype)


def scatter_blocks(put, p0, p1, p2, p3, out, held, sems):
    total = p0[...].astype(F32)
    for part in (p1, p2, p3):
        total = total + part[...].astype(F32)
    natural = dot(total.astype(BF16), gate_order(1)).astype(BF16)
    copies = []
    rows = held.shape[0] // 2
    for n in range(2):
        part = slice(n * rows, (n + 1) * rows)
        held[part, :] = dot(put[part, :], natural).astype(BF16)
        for m in range(2):
            copy = pltpu.make_async_copy(held.at[part], out.at[m, part], sems.at[2 * n + m])
            copy.start()
            copies.append(copy)
    for copy in copies:
        copy.wait()


def sum_units(z0, z1, z2, z3, o0, o1, o2, o3):
    for i, out in enumerate((o0, o1, o2, o3)):
        out[...] = (
            z0[i].astype(F32) + z1[i].astype(F32) + z2[i].astype(F32) + z3[i].astype(F32)
        ).astype(BF16)


def turn(spk, packed, mel, other, conv, out, extra):
    half, j = lax.axis_index("tm"), lax.axis_index("chan") & 3
    tokens, wide = 256, 384
    same = onehot(iota((256, 256), 0) == iota((256, 256), 1))
    conv[...] = dot(same, packed[:, 0:OUT_AT, :].reshape(8 * OUT_AT, 256), NT).astype(BF16)
    out[...] = dot(same, packed[:, OUT_AT:PACKED, :].reshape(RESID, 256), NT).astype(BF16)
    m = iota((128, MELS), 0)
    mel_pick = onehot(((m & 15) < MEL_BLOCKS) & (iota((128, MELS), 1) == 8 * (m & 15) + (m >> 4)))
    cut = pl.ds(pl.multiple_of(j * tokens, tokens), tokens)
    far = pl.ds(pl.multiple_of(jnp.minimum(j * tokens + tokens, 896), 128), 128)
    ahead = jnp.where(j == 3, other[96:176, :].astype(F32), mel[:, far].astype(F32)).astype(BF16)
    mels = jnp.concatenate([dot(mel_pick, mel[:, cut]), dot(mel_pick, ahead)], 1).astype(BF16)
    seg = 8 * half + 2 * j
    row, lane = iota((16, wide), 0), iota((16, wide), 1)
    beyond = other[176:192, :].astype(F32)[1:2, 0:1].astype(jnp.int32)
    beyond = jnp.where(j == 3, beyond, spk[jnp.minimum(2 * j + 2, 7)] & 7)
    sub = jnp.where(
        lane < SEG,
        spk[2 * j] & 7,
        jnp.where(lane < 2 * SEG, spk[2 * j + 1] & 7, jnp.broadcast_to(beyond, (16, wide))),
    )
    for r in range(8):
        extra[r, 0:16] = mels[16 * r : 16 * r + 16]
        extra[r, 16:32] = onehot((row == seg + (lane >> 7)) & (sub == r))


def layer(conv, out, extra, o0, o1, o2, o3, p1, p2, p3, kept, given, hidden_out, grad_out, feat, res, skp, natural, p0):
    join(o0, o1, o2, o3, p0)
    ch = lax.axis_index("chan")
    got = (p0, p1, p2, p3)
    tokens, wide = 256, 384
    for k in range(4):
        for i in range(4):
            rows = pl.ds(pl.multiple_of(32 * (ch ^ (4 * k + i)), 32), 32)
            for n in range(3):
                at = 96 * i + 32 * n
                for h in range(2):
                    natural[2 * n + h, rows, :] = got[k][at : at + 32, 128 * h : 128 * h + 128].astype(F32)

    ends = [part[384:400, :].astype(F32) for part in got]
    gap = jnp.zeros((96, 128), F32)
    for k, end in enumerate(ends):
        left, right = end[:, 0:128], end[:, 128:256]
        tile = jnp.concatenate([left[8:16], right, gap, left[0:8]], 0).T
        for i in range(4):
            rows = pl.ds(pl.multiple_of(32 * (ch ^ (4 * k + i)), 32), 32)
            natural[6, rows, :] = tile[32 * i : 32 * i + 32]

    def majors(n):
        return jnp.concatenate([natural[n, pl.ds(r, 64, stride=8), :] for r in range(8)], 0)

    tile = majors(6)
    sig = jnp.concatenate([majors(0), majors(1), tile], 1)
    for n, cot in ((1, res), (2, skp)):
        cot[:, 0:128] = majors(2 * n).astype(BF16)
        cot[:, 128:256] = majors(2 * n + 1).astype(BF16)
        cot[:, 256:384] = pltpu.roll(tile, 128 - 8 * n, 1).astype(BF16)
    shifted = pltpu.roll(sig, DILATION, 1).astype(BF16)
    sig = sig.astype(BF16)
    for r in range(8):
        feat[r, 0:64] = shifted[64 * r : 64 * r + 64]
        feat[r, 64:128] = sig[64 * r : 64 * r + 64]
        feat[r, 128:160] = extra[r]
    features = feat[...].reshape(8 * OUT_AT, wide)
    pre = dot(conv[...], features)
    filt = jnp.tanh(pre[:128])
    gate = jax.nn.sigmoid(pre[128:])
    hidden = (filt[:, :tokens] * gate[:, :tokens]).astype(BF16)
    hidden_out[...] = hidden
    grad_hidden = dot(out[0:128, :], res[...]) + dot(out[128:256, :], skp[...])
    grad_pre = jnp.concatenate(
        [
            grad_hidden * gate * (1.0 - filt * filt),
            grad_hidden * filt * gate * (1.0 - gate),
        ],
        0,
    ).astype(BF16)
    grad_out[...] = grad_pre
    grad_pre = grad_pre[:, :tokens]
    conv_grad = dot(features[:, :tokens], grad_pre, NT)
    res_grad = dot(res[:, :tokens], hidden, NT)
    skp_grad = dot(skp[:, :tokens], hidden, NT)
    core = ch & 1
    for part, rows, cols in (
        (conv_grad.reshape(8, OUT_AT, 256), slice(0, OUT_AT), slice(0, 256)),
        (res_grad.reshape(8, 64, 128), slice(OUT_AT, PACKED), slice(0, 128)),
        (skp_grad.reshape(8, 64, 128), slice(OUT_AT, PACKED), slice(128, 256)),
    ):
        for i in range(4):
            even, odd = part[2 * i], part[2 * i + 1]
            kept[i, rows, cols] = jnp.where(core == 0, even, odd)
            given[i, rows, cols] = jnp.where(core == 0, odd, even).astype(BF16)


def outputs(packed, hidden, grad_pre, z0, z1, z2, z3, natural):
    ch = lax.axis_index("chan")
    tokens, wide = 256, 384
    hidden = hidden[...]
    res_part = dot(packed[:, OUT_AT:PACKED, 0:128].reshape(RESID, 128), hidden)
    skp_part = dot(packed[:, OUT_AT:PACKED, 128:256].reshape(RESID, 128), hidden)
    prev = packed[:, 0:64, :].reshape(RESID, 256)
    now = packed[:, 64:128, :].reshape(RESID, 256)
    later = pltpu.roll(dot(prev, grad_pre[...]), wide - DILATION, 1)[:, :tokens]
    in_part = dot(now, grad_pre[:, :tokens]) + later
    for n, part in enumerate((res_part, skp_part, in_part)):
        for h in range(2):
            for r in range(8):
                natural[2 * n + h, pl.ds(r, 64, stride=8), :] = part[
                    64 * r : 64 * r + 64, 128 * h : 128 * h + 128
                ]
    for k, out in enumerate((z0, z1, z2, z3)):
        for i in range(4):
            rows = pl.ds(pl.multiple_of(32 * (ch ^ (4 * k + i)), 32), 32)
            for n in range(3):
                for h in range(2):
                    out[i, 32 * n : 32 * n + 32, 128 * h : 128 * h + 128] = natural[
                        2 * n + h, rows, :
                    ].astype(BF16)


def finish_tokens(o0, o1, o2, o3, sig, res, residual, skipped, grad_in):
    j = lax.axis_index("chan") & 3
    for k, piece in enumerate((o0, o1, o2, o3)):
        cut = pl.ds(pl.multiple_of((j ^ k) * 256, 256), 256)
        residual[:, cut] = sig[:, cut].astype(F32) + piece[0:32, :].astype(F32)
        skipped[:, cut] = piece[32:64, :].astype(F32)
        grad_in[:, cut] = res[:, cut].astype(F32) + piece[64:96, :].astype(F32)


def update(owned, grads, master, first, second, *refs):
    outs, held, old, grad, sems = refs[:3], refs[3:6], (*refs[6:8], first), refs[8], refs[9]
    slots = grads.shape[1]
    rows = 8 * slots
    steps = 8
    parts = [slice(n * rows // steps, (n + 1) * rows // steps) for n in range(steps)]
    fetches = []
    for n, part in enumerate(parts):
        for m, source in enumerate((second, master)):
            fetch = pltpu.make_async_copy(
                source.at[part, :], old[m].at[part, :], sems.at[3 * steps + 2 * n + m]
            )
            fetch.start()
            fetches.append(fetch)
    for r in range(8):
        for z in range(4):
            got = grads[16 * (r // 4) + 4 * z + r % 4].astype(F32)
            for h in range(2):
                grad[2 * z + h, pl.ds(r, slots, stride=8), :] = got[:, 128 * h : 128 * h + 128]
    unbias = 1.0 / (1.0 - MOMENT_DECAY**STEP)
    copies = []
    for n, part in enumerate(parts):
        for m in range(2):
            fetches[2 * n + m].wait()
        old_s, old_m, old_f = (ref[part, :] for ref in old)
        new = jnp.concatenate([grad[t, part, :] for t in range(8)], 1)
        keep = n * (rows // steps) + iota((rows // steps, 1), 0) < 8 * owned[0:1, 0:1]
        first_new = MOMENT_DECAY * old_f + (1.0 - MOMENT_DECAY) * new
        second_new = MOMENT_DECAY * old_s + (1.0 - MOMENT_DECAY) * new * new
        first_hat = first_new * unbias
        second_hat = second_new * unbias
        root = second_hat * lax.rsqrt(second_hat)
        stepped = old_m - STEP_RATE * (
            first_hat * pl.reciprocal(root + EPSILON) + WEIGHT_DECAY * old_m
        )
        held[0][part, :] = jnp.where(keep, first_new, old_f)
        held[1][part, :] = jnp.where(keep, second_new, old_s)
        held[2][part, :] = jnp.where(keep, stepped, old_m)
        for m in range(3):
            copy = pltpu.make_async_copy(
                held[m].at[part, :], outs[m].at[part, :], sems.at[3 * n + m]
            )
            copy.start()
            copies.append(copy)
    for copy in copies:
        copy.wait()


BOTH = ("tm", "chan")


def swap(x, k):
    n = lax.axis_size("chan")
    return lax.ppermute(x, "chan", [(i, i ^ k) for i in range(n)])


def local(
    signal, mel_frames, speaker_ids, owners, master, first_moment, second_moment, res_cot, skip_cot
):
    slots_dev = master.shape[0]
    slots = 16 * slots_dev
    flat = (8 * slots_dev, GATES)
    sig, res, skp, mel = signal.T, res_cot.T, skip_cot.T, mel_frames.T
    own_row = owners.reshape(1, NBLK)
    share = [[16 * y + 4 * z + j for y in range(2) for j in range(4)] for z in range(4)]
    sds = jax.ShapeDtypeStruct
    dma = pltpu.SemaphoreType.DMA

    sent, acts, edges = call(
        begin,
        (sds((16, slots_dev, 256), BF16), sds((3, *sig.shape), BF16), sds((192, 128), BF16)),
        (HBM,) * 6,
        scratch=(
            pltpu.VMEM((8, 8 * slots_dev, 128), F32),
            pltpu.VMEM((16, slots_dev, 256), BF16),
            pltpu.SMEM(speaker_ids.shape, jnp.int32),
            dma((17,)),
        ),
        out_space=(HBM, VMEM, VMEM),
    )(speaker_ids, master.reshape(flat), sig, res, skp, mel)
    other = lax.ppermute(edges, "tm", [(0, 1), (1, 0)])
    piece = sds((PIECE, 256), BF16)
    o = call(pack_tokens, (piece,) * 4, (VMEM,) * 2, gflops=8)(acts, other)
    arrived = lax.all_to_all(sent, "chan", 0, 0, tiled=True)
    o = (o[0], swap(o[1], 1), swap(o[2], 2), swap(o[3], 3))
    mine = call(join, sds((400, 256), BF16), (VMEM,) * 4)(*o)
    p1, p2, p3 = (swap(mine, 4 * k) for k in (1, 2, 3))

    at_col, put, owned = call(
        functools.partial(place_blocks, slots_dev=slots_dev),
        (
            sds((PACKED, 128), jnp.int32),
            sds((slots, PACKED), BF16),
            sds((8, 128), jnp.int32),
        ),
        (SMEM, VMEM, VMEM),
    )(speaker_ids, own_row, other)
    arrived, _ = lax.optimization_barrier((arrived, mine))
    gathered = call(gather_blocks, sds((PACKED, 256), BF16), (VMEM, VMEM), gflops=8)(
        at_col, arrived.reshape(slots, 256)
    )
    packed = lax.all_gather(gathered, BOTH, axis_index_groups=share)
    rows = (4, PACKED, 256)
    turned = call(
        turn,
        (
            sds((256, 8 * OUT_AT), BF16),
            sds((256, RESID), BF16),
            sds((8, OUT_AT - TAPS, 384), BF16),
        ),
        (SMEM,) + (VMEM,) * 3,
        gflops=8,
    )(speaker_ids, packed, mel, other)
    kept, given, hidden, grad_pre = call(
        layer,
        (sds(rows, F32), sds(rows, BF16), sds((128, 256), BF16), sds((256, 384), BF16)),
        (VMEM,) * 10,
        gflops=0,
        scratch=(
            pltpu.VMEM((8, OUT_AT, 384), BF16),
            pltpu.VMEM((RESID, 384), BF16),
            pltpu.VMEM((RESID, 384), BF16),
            pltpu.VMEM((7, RESID, 128), F32),
            pltpu.VMEM((400, 256), BF16),
        ),
    )(*turned, *o, p1, p2, p3)
    z0, z1, z2, z3 = call(
        outputs,
        (sds((4, 96, 256), BF16),) * 4,
        (VMEM,) * 3,
        gflops=0,
        scratch=(pltpu.VMEM((6, RESID, 128), F32),),
    )(packed, hidden, grad_pre)

    kept, _ = lax.optimization_barrier((kept, z0))
    n = lax.axis_size("chan")
    g = call(sum_cores, tuple(sds((PACKED, 256), t) for t in (F32, BF16, BF16, BF16)), (VMEM,) * 2)(kept, swap(given, 1))
    across = [(16 * y + i, 16 * (1 - y) + (i ^ 2)) for y in range(2) for i in range(n)]
    g = (g[0], swap(g[1], 2), lax.ppermute(g[2], "tm", [(0, 1), (1, 0)]), lax.ppermute(g[3], BOTH, across))
    t1, t2, t3 = (swap(z, 4 * k) for k, z in ((1, z1), (2, z2), (3, z3)))
    spread = call(
        scatter_blocks,
        sds((2, slots, 256), BF16),
        (VMEM,) * 5,
        scratch=(pltpu.VMEM((slots, 256), BF16), dma((4,))),
        out_space=HBM,
    )(put, *g)
    returned = lax.all_to_all(spread.reshape(32, slots_dev, 256), BOTH, 0, 0)
    o = call(sum_units, (sds((96, 256), BF16),) * 4, (VMEM,) * 4, gflops=20)(z0, t1, t2, t3)
    o = (o[0], swap(o[1], 1), swap(o[2], 2), swap(o[3], 3))
    narrow = sds(sig.shape, F32)
    residual, skipped, grad_in = call(finish_tokens, (narrow,) * 3, (VMEM,) * 6)(*o, sig, res)
    new = call(
        update,
        (sds(flat, F32),) * 3,
        (VMEM, VMEM, HBM, VMEM, HBM),
        scratch=(pltpu.VMEM(flat, F32),) * 5
        + (pltpu.VMEM((8, flat[0], 128), F32), dma((40,))),
        out_space=HBM,
    )(
        owned,
        returned,
        master.reshape(flat),
        first_moment.reshape(flat),
        second_moment.reshape(flat),
    )
    return (residual.T, skipped.T, grad_in.T, *(x.reshape(master.shape) for x in new))


def place_index(owners, slots_dev):
    count = owners.shape[0]
    matches = owners[:, None] == owners[None, :]
    before = jnp.arange(count)[None, :] < jnp.arange(count)[:, None]
    ranks = jnp.sum((matches & before).astype(jnp.int32), axis=1)
    return owners * slots_dev + ranks


def local_plain(
    signal, mel_frames, speaker_ids, owners, master, first_moment, second_moment, res_cot, skip_cot
):
    chans = lax.axis_size("chan")
    slots_dev = master.shape[0]
    tok_count = signal.shape[0]
    hid_local = HIDDEN_SIZE // chans
    col_count = GATES // chans
    seg_count = speaker_ids.shape[0]
    spk_start = 2 * RESID + MELS
    out_start = spk_start + SPEAKERS
    places = place_index(owners, slots_dev)
    table = places[:, None] == jnp.arange(chans * slots_dev)[None, :]
    received = lax.all_to_all(
        master.astype(BF16), "chan", split_axis=2, concat_axis=0, tiled=True
    ).reshape(chans * slots_dev, BLOCK * col_count)
    params = jnp.dot(table.astype(BF16), received, preferred_element_type=F32)
    params = params.astype(BF16).reshape(ROWS, col_count)
    tap_prev, tap_now = params[:RESID], params[RESID : 2 * RESID]
    mel_proj = params[2 * RESID : spk_start]
    speaker_table = params[spk_start:out_start]
    out_cols = params[out_start:].reshape(RESID, hid_local, 2)
    n_tm = lax.axis_size("tm")
    tail_prev = lax.ppermute(signal[-DILATION:], "tm", [(i, i + 1) for i in range(n_tm - 1)])
    inputs = lax.all_gather(signal, "chan", axis=1, tiled=True)
    tail_full = lax.all_gather(tail_prev, "chan", axis=1, tiled=True)
    shifted = jnp.concatenate([tail_full, inputs[:-DILATION]], 0)
    pre_act = jnp.dot(shifted, tap_prev, preferred_element_type=F32)
    pre_act = pre_act + jnp.dot(inputs, tap_now, preferred_element_type=F32)
    pre_act = pre_act + jnp.dot(mel_frames, mel_proj, preferred_element_type=F32)
    one_hot = (speaker_ids[:, None] == jnp.arange(SPEAKERS)[None, :]).astype(BF16)
    embedded = jnp.dot(one_hot, speaker_table, preferred_element_type=F32)
    pre_act = (pre_act.reshape(seg_count, SEG, col_count) + embedded[:, None, :]).reshape(
        tok_count, col_count
    )
    filt = jnp.tanh(pre_act[:, 0::2])
    gates = jax.nn.sigmoid(pre_act[:, 1::2])
    hidden = (filt * gates).astype(BF16)
    summed = lax.psum_scatter(
        jnp.einsum("cuw,tu->cwt", out_cols, hidden, preferred_element_type=F32),
        "chan",
        scatter_dimension=0,
        tiled=True,
    )
    cots = lax.all_gather(
        jnp.stack([res_cot.T, skip_cot.T], axis=1), "chan", axis=0, tiled=True
    )
    grad_hid = jnp.einsum("cwt,cuw->tu", cots, out_cols, preferred_element_type=F32)
    term = jnp.einsum("cwt,tu->cuw", cots, hidden, preferred_element_type=F32)
    grad_filt = grad_hid * gates * (1.0 - filt * filt)
    grad_gate = grad_hid * filt * gates * (1.0 - gates)
    grad_pre = (
        jnp.stack([grad_filt, grad_gate], axis=2).reshape(tok_count, col_count).astype(BF16)
    )
    ahead = lax.ppermute(grad_pre[:DILATION], "tm", [(i + 1, i) for i in range(n_tm - 1)])
    later = jnp.concatenate([grad_pre[DILATION:], ahead], 0)
    input_part = lax.psum_scatter(
        dot(tap_now, grad_pre, NT) + dot(tap_prev, later, NT),
        "chan",
        scatter_dimension=0,
        tiled=True,
    )
    seg_sums = jnp.sum(grad_pre.astype(F32).reshape(seg_count, SEG, col_count), axis=1)
    grad_spk = lax.dot_general(
        one_hot.astype(F32),
        seg_sums,
        TN,
        precision=lax.Precision.HIGHEST,
        preferred_element_type=F32,
    )
    grad_params = jnp.concatenate(
        [
            dot(shifted, grad_pre, TN),
            dot(inputs, grad_pre, TN),
            dot(mel_frames, grad_pre, TN),
            grad_spk,
            term.reshape(RESID, col_count),
        ],
        0,
    )
    grad_params = lax.psum(grad_params, "tm").reshape(NBLK, BLOCK * col_count)
    outgoing = lax.dot_general(
        table.astype(F32), grad_params, TN, precision=lax.Precision.HIGHEST
    ).reshape(chans * slots_dev, BLOCK, col_count)
    grad_slots = lax.all_to_all(outgoing, "chan", split_axis=0, concat_axis=2, tiled=True)
    owned = jnp.sum((owners == lax.axis_index("chan")).astype(jnp.int32))
    keep = (jnp.arange(slots_dev) < owned)[:, None, None]
    first_new = MOMENT_DECAY * first_moment + (1.0 - MOMENT_DECAY) * grad_slots
    second_new = MOMENT_DECAY * second_moment + (1.0 - MOMENT_DECAY) * grad_slots * grad_slots
    first_hat = first_new / (1.0 - MOMENT_DECAY**STEP)
    second_hat = second_new / (1.0 - MOMENT_DECAY**STEP)
    stepped = master - STEP_RATE * (
        first_hat / (jnp.sqrt(second_hat) + EPSILON) + WEIGHT_DECAY * master
    )
    return (
        signal.astype(F32) + summed[:, 0, :].T,
        summed[:, 1, :].T,
        res_cot.astype(F32) + input_part.T,
        jnp.where(keep, first_new, first_moment),
        jnp.where(keep, second_new, second_moment),
        jnp.where(keep, stepped, master),
    )


def solution(mesh):
    wide = P("tm", "chan")
    slots = P("chan", None, None)
    packed_mesh = mesh.shape["tm"] == 2 and mesh.shape["chan"] == 16
    return jax.shard_map(
        local if packed_mesh else local_plain,
        mesh=mesh,
        in_specs=(wide, P("tm", None), P("tm"), P(), slots, slots, slots, wide, wide),
        out_specs=(wide, wide, wide, slots, slots, slots),
        check_vma=False,
    )
```

```python
import functools

import jax
import jax.numpy as jnp
from jax import lax
from jax.experimental import pallas as pl
from jax.experimental.pallas import tpu as pltpu
from jax.sharding import PartitionSpec as P

RESID = 512
HIDDEN_SIZE = 512
MELS = 80
SPEAKERS = 944
DILATION = 8
SEG = 128
BLOCK = 8
STEP = 5
GATES = 1024
ROWS = 2560
NBLK = 320

MOMENT_DECAY = 0.5
STEP_RATE = 0.03
WEIGHT_DECAY = 0.01
EPSILON = 1e-08

F32 = jnp.float32
BF16 = jnp.bfloat16
NN = (((1,), (0,)), ((), ()))
NT = (((1,), (1,)), ((), ()))
TN = (((0,), (0,)), ((), ()))

TAPS = 2 * RESID // BLOCK
MEL_AT = TAPS
MEL_BLOCKS = MELS // BLOCK
SEG_AT = 144
OUT_AT = 160
PACKED = 224
SPK_BLOCK = TAPS + MEL_BLOCKS
OUT_BLOCK = SPK_BLOCK + SPEAKERS // BLOCK
PIECE = 112


def dot(a, b, dims=NN):
    return lax.dot_general(a, b, dims, preferred_element_type=F32)


def iota(shape, dim):
    return lax.broadcasted_iota(jnp.int32, shape, dim)


def onehot(cond):
    return jnp.where(cond, 1.0, 0.0).astype(BF16)


KIB, MIB = 2**10, 2**20
VMEM, SMEM, HBM = pltpu.VMEM, pltpu.SMEM, pltpu.HBM


def call(kernel, out, spaces, gflops=0, scratch=(), out_space=VMEM, pinned=()):
    out_spaces = out_space if isinstance(out_space, tuple) else jax.tree.map(lambda _: out_space, out)
    run = pl.pallas_call(
        kernel,
        out_shape=out,
        in_specs=[pl.BlockSpec(memory_space=space) for space in spaces],
        out_specs=jax.tree.map(lambda _, space: pl.BlockSpec(memory_space=space), out, out_spaces),
        scratch_shapes=list(scratch),
        compiler_params=pltpu.CompilerParams(vmem_limit_bytes=24 * MIB),
        cost_estimate=pl.CostEstimate(
            flops=gflops * 10**9, bytes_accessed=MIB, transcendentals=0
        ),
    )
    pin = pltpu.with_memory_space_constraint
    fixed = [space if space == HBM or n in pinned else None for n, space in enumerate(spaces)]
    return lambda *args: run(*(pin(x, f) if f else x for x, f in zip(args, fixed, strict=True)))


def gate_order(dim):
    natural, split = iota((256, 256), dim), iota((256, 256), 1 - dim)
    return onehot(natural == 2 * (split & 127) + (split >> 7))


def begin(speakers, master, sig, res, skp, mel, sent, acts, edges, strips, packed, spk, sems):
    half = lax.axis_index("tm")
    slots = sent.shape[1]
    cut = pl.ds(pl.multiple_of((1 - half) * 896, 128), 128)
    moves = [(speakers, spk)]
    moves += [(part, acts.at[n]) for n, part in enumerate((sig, res, skp))]
    moves += [(mel.at[:, cut], edges.at[96:176, :])]
    moves += [(master.at[:, 128 * t : 128 * t + 128], strips.at[t]) for t in range(8)]
    copies = [pltpu.make_async_copy(a, b, sems.at[n]) for n, (a, b) in enumerate(moves)]
    for copy in copies:
        copy.start()
    copies[0].wait()
    row, lane = iota((16, 128), 0), iota((16, 128), 1)
    table = jnp.zeros((16, 128), jnp.int32)
    for s in range(8):
        code = jnp.where(row == 0, spk[s] >> 3, spk[s] & 7)
        table = jnp.where((lane == s) & (row < 2), code, table)
    edges[176:192, :] = table.astype(F32).astype(BF16)
    for copy in copies[1:5]:
        copy.wait()
    for n in range(3):
        edges[32 * n : 32 * n + 32, :] = acts[n, :, cut]
    for t in range(8):
        copies[5 + t].wait()
        lanes = slice(128 * (t % 2), 128 * (t % 2) + 128)
        for j in range(4):
            low = strips[t, pl.ds(j, slots, stride=8), :]
            high = strips[t, pl.ds(4 + j, slots, stride=8), :]
            packed[4 * (t // 2) + j, :, lanes] = jnp.where(half == 0, low, high).astype(BF16)
        if t % 2:
            part = slice(2 * t - 2, 2 * t + 2)
            copies.append(pltpu.make_async_copy(packed.at[part], sent.at[part], sems.at[13 + t // 2]))
            copies[-1].start()
    for copy in copies[13:]:
        copy.wait()


def pack_tokens(acts, other, o0, o1, o2, o3):
    sig, res, skp = (acts.at[n] for n in range(3))
    half, j = lax.axis_index("tm"), lax.axis_index("chan") & 3
    outs = (o0, o1, o2, o3)
    parts = (sig, res, skp)
    befores, nexts = [], ([], [], [])
    for k in range(4):
        to = j ^ k
        cut = pl.ds(pl.multiple_of(to * 256, 256), 256)
        for n, part in enumerate(parts):
            outs[k][32 * n : 32 * n + 32, :] = part[:, cut]
        cut = pl.ds(pl.multiple_of(jnp.maximum(to * 256 - 128, 0), 128), 128)
        edge = jnp.where(half == 1, other[0:32, :].astype(F32), 0.0)
        befores.append(jnp.where(to == 0, edge, sig[:, cut].astype(F32)))
        cut = pl.ds(pl.multiple_of(jnp.minimum(to * 256 + 256, 896), 128), 128)
        for n, part in enumerate(parts):
            edge = jnp.where(half == 0, other[32 * n : 32 * n + 32, :].astype(F32), 0.0)
            nexts[n].append(jnp.where(to == 3, edge, part[:, cut].astype(F32)))
    tall = [jnp.concatenate(x, 0).astype(BF16) for x in (befores, *nexts)]
    t, lane = iota((16, 128), 0), iota((16, 128), 1)
    top, low = t < DILATION, t >= DILATION
    head_top = onehot(top & (lane == t))
    head_low = onehot(low & (lane == t - DILATION))
    last_top = onehot(top & (lane == t + 120))
    rows = (
        dot(last_top, tall[0], NT) + dot(head_low, tall[1], NT),
        dot(head_top, tall[2], NT) + dot(head_low, tall[3], NT),
    )
    for k in range(4):
        for n in range(2):
            outs[k][96:112, 128 * n : 128 * n + 128] = jnp.where(
                (lane >> 5) == k, rows[n], 0.0
            ).astype(BF16)


def join(o0, o1, o2, o3, out):
    ends = o0[96:112, :].astype(F32)
    for piece in (o1, o2, o3):
        ends = ends + piece[96:112, :].astype(F32)
    for k, piece in enumerate((o0, o1, o2, o3)):
        out[96 * k : 96 * k + 96, :] = piece[0:96, :]
    out[384:400, :] = ends.astype(BF16)


def place_blocks(spk_ids, owners, other, at_col, put, owned, *, slots_dev):
    half = lax.axis_index("tm")
    own_row = owners[...]
    mine = jnp.where(own_row == lax.axis_index("chan"), 1, 0)
    owned[...] = jnp.broadcast_to(jnp.sum(mine, axis=1, keepdims=True), owned.shape)
    down, across = iota((NBLK, NBLK), 0), iota((NBLK, NBLK), 1)
    row_all = jnp.broadcast_to(own_row, (NBLK, NBLK))
    own_col = jnp.sum(jnp.where(down == across, row_all, 0), axis=1, keepdims=True)
    before = (own_col == row_all) & (down < across)
    rank = jnp.sum(jnp.where(before, 1, 0), axis=0, keepdims=True)
    place = own_row * slots_dev + rank
    n = iota((PACKED, 128), 0)
    far = n - SEG_AT - 8 * (1 - half) == iota((PACKED, 128), 1)
    blocks = jnp.broadcast_to(other[176:192, :].astype(F32)[0:1], (PACKED, 128))
    spk = jnp.sum(jnp.where(far, blocks, 0.0), axis=1, keepdims=True).astype(jnp.int32)
    n = iota((PACKED, 1), 0)
    for s in range(8):
        spk = jnp.where(n == SEG_AT + 8 * half + s, spk_ids[s] >> 3, spk)
    blk = jnp.where(
        n < SPK_BLOCK,
        n,
        jnp.where(n < SEG_AT, -1, jnp.where(n < OUT_AT, SPK_BLOCK + spk, n + (OUT_BLOCK - OUT_AT))),
    )
    match = jnp.broadcast_to(blk, (PACKED, NBLK)) == iota((PACKED, NBLK), 1)
    at = jnp.sum(jnp.where(match, jnp.broadcast_to(place, (PACKED, NBLK)), 0), axis=1, keepdims=True)
    at = jnp.where(blk < 0, -1, at)
    at_col[...] = jnp.broadcast_to(at, (PACKED, 128))
    same = iota((PACKED, PACKED), 0) == iota((PACKED, PACKED), 1)
    row = jnp.sum(jnp.where(same, jnp.broadcast_to(at, (PACKED, PACKED)), 0), axis=0, keepdims=True)
    put[...] = onehot(jnp.broadcast_to(row, put.shape) == iota(put.shape, 0))


def gather_blocks(at_col, slots, out):
    shape = (PACKED, slots.shape[0])
    pick = onehot(jnp.broadcast_to(at_col[:, 0:1], shape) == iota(shape, 1))
    got = dot(pick, slots[...]).astype(BF16)
    out[...] = dot(got, gate_order(0)).astype(BF16)


def sum_cores(kept, got, *outs):
    i = 2 * lax.axis_index("tm") + ((lax.axis_index("chan") >> 1) & 1)
    for k, out in enumerate(outs):
        out[...] = (kept[i ^ k] + got[i ^ k].astype(F32)).astype(out.dtype)


def scatter_blocks(put, p0, p1, p2, p3, out, held, sems):
    total = p0[...].astype(F32)
    for part in (p1, p2, p3):
        total = total + part[...].astype(F32)
    natural = dot(total.astype(BF16), gate_order(1)).astype(BF16)
    copies = []
    rows = held.shape[0] // 2
    for n in range(2):
        part = slice(n * rows, (n + 1) * rows)
        held[part, :] = dot(put[part, :], natural).astype(BF16)
        for m in range(2):
            copy = pltpu.make_async_copy(held.at[part], out.at[m, part], sems.at[2 * n + m])
            copy.start()
            copies.append(copy)
    for copy in copies:
        copy.wait()


def sum_units(z0, z1, z2, z3, o0, o1, o2, o3):
    for i, out in enumerate((o0, o1, o2, o3)):
        out[...] = (
            z0[i].astype(F32) + z1[i].astype(F32) + z2[i].astype(F32) + z3[i].astype(F32)
        ).astype(BF16)


def turn(spk, packed, mel, other, conv, out, extra, start):
    half, j = lax.axis_index("tm"), lax.axis_index("chan") & 3
    tokens, wide = 256, 384
    same = onehot(iota((256, 256), 0) == iota((256, 256), 1))
    conv[...] = dot(same, packed[:, 0:TAPS, :].reshape(8 * TAPS, 256), NT).astype(BF16)
    out[...] = dot(same, packed[:, OUT_AT:PACKED, :].reshape(RESID, 256), NT).astype(BF16)
    m = iota((128, MELS), 0)
    mel_pick = onehot(((m & 15) < MEL_BLOCKS) & (iota((128, MELS), 1) == 8 * (m & 15) + (m >> 4)))
    cut = pl.ds(pl.multiple_of(j * tokens, tokens), tokens)
    far = pl.ds(pl.multiple_of(jnp.minimum(j * tokens + tokens, 896), 128), 128)
    ahead = jnp.where(j == 3, other[96:176, :].astype(F32), mel[:, far].astype(F32)).astype(BF16)
    mels = jnp.concatenate([dot(mel_pick, mel[:, cut]), dot(mel_pick, ahead)], 1).astype(BF16)
    seg = 8 * half + 2 * j
    row, lane = iota((16, wide), 0), iota((16, wide), 1)
    beyond = other[176:192, :].astype(F32)[1:2, 0:1].astype(jnp.int32)
    beyond = jnp.where(j == 3, beyond, spk[jnp.minimum(2 * j + 2, 7)] & 7)
    sub = jnp.where(
        lane < SEG,
        spk[2 * j] & 7,
        jnp.where(lane < 2 * SEG, spk[2 * j + 1] & 7, jnp.broadcast_to(beyond, (16, wide))),
    )
    for r in range(8):
        extra[r, 0:16] = mels[16 * r : 16 * r + 16]
        extra[r, 16:32] = onehot((row == seg + (lane >> 7)) & (sub == r))
    side = 8 * (OUT_AT - TAPS)
    start[...] = dot(packed[:, TAPS:OUT_AT, :].reshape(side, 256), extra[...].reshape(side, wide), TN)


def layer(conv, out, extra, start, o0, o1, o2, o3, p1, p2, p3, kept, given, hidden_out, grad_out, feat, res, skp, natural, p0):
    join(o0, o1, o2, o3, p0)
    ch = lax.axis_index("chan")
    got = (p0, p1, p2, p3)
    tokens, wide = 256, 384
    for k in range(4):
        for i in range(4):
            rows = pl.ds(pl.multiple_of(32 * (ch ^ (4 * k + i)), 32), 32)
            for n in range(3):
                at = 96 * i + 32 * n
                for h in range(2):
                    natural[2 * n + h, rows, :] = got[k][at : at + 32, 128 * h : 128 * h + 128].astype(F32)

    ends = [part[384:400, :].astype(F32) for part in got]
    gap = jnp.zeros((96, 128), F32)
    for k, end in enumerate(ends):
        left, right = end[:, 0:128], end[:, 128:256]
        tile = jnp.concatenate([left[8:16], right, gap, left[0:8]], 0).T
        for i in range(4):
            rows = pl.ds(pl.multiple_of(32 * (ch ^ (4 * k + i)), 32), 32)
            natural[6, rows, :] = tile[32 * i : 32 * i + 32]

    def majors(n):
        return jnp.concatenate([natural[n, pl.ds(r, 64, stride=8), :] for r in range(8)], 0)

    tile = majors(6)
    sig = jnp.concatenate([majors(0), majors(1), tile], 1)
    for n, cot in ((1, res), (2, skp)):
        cot[:, 0:128] = majors(2 * n).astype(BF16)
        cot[:, 128:256] = majors(2 * n + 1).astype(BF16)
        cot[:, 256:384] = pltpu.roll(tile, 128 - 8 * n, 1).astype(BF16)
    shifted = pltpu.roll(sig, DILATION, 1).astype(BF16)
    sig = sig.astype(BF16)
    for r in range(8):
        feat[r, 0:64] = shifted[64 * r : 64 * r + 64]
        feat[r, 64:128] = sig[64 * r : 64 * r + 64]
    features = feat[...].reshape(8 * TAPS, wide)
    pre = start[...] + dot(conv[...], features)
    filt = jnp.tanh(pre[:128])
    gate = jax.nn.sigmoid(pre[128:])
    hidden = (filt[:, :tokens] * gate[:, :tokens]).astype(BF16)
    hidden_out[...] = hidden
    grad_hidden = dot(out[0:128, :], res[...]) + dot(out[128:256, :], skp[...])
    grad_pre = jnp.concatenate(
        [
            grad_hidden * gate * (1.0 - filt * filt),
            grad_hidden * filt * gate * (1.0 - gate),
        ],
        0,
    ).astype(BF16)
    grad_out[...] = grad_pre
    grad_pre = grad_pre[:, :tokens]
    conv_grad = dot(features[:, :tokens], grad_pre, NT)
    side_grad = dot(extra[:, :, :tokens].reshape(8 * (OUT_AT - TAPS), tokens), grad_pre, NT)
    res_grad = dot(res[:, :tokens], hidden, NT)
    skp_grad = dot(skp[:, :tokens], hidden, NT)
    core = ch & 1
    for part, rows, cols in (
        (conv_grad.reshape(8, TAPS, 256), slice(0, TAPS), slice(0, 256)),
        (side_grad.reshape(8, OUT_AT - TAPS, 256), slice(TAPS, OUT_AT), slice(0, 256)),
        (res_grad.reshape(8, 64, 128), slice(OUT_AT, PACKED), slice(0, 128)),
        (skp_grad.reshape(8, 64, 128), slice(OUT_AT, PACKED), slice(128, 256)),
    ):
        for i in range(4):
            even, odd = part[2 * i], part[2 * i + 1]
            kept[i, rows, cols] = jnp.where(core == 0, even, odd)
            given[i, rows, cols] = jnp.where(core == 0, odd, even).astype(BF16)


def outputs(packed, hidden, grad_pre, z0, z1, z2, z3, natural):
    ch = lax.axis_index("chan")
    tokens, wide = 256, 384
    hidden = hidden[...]
    res_part = dot(packed[:, OUT_AT:PACKED, 0:128].reshape(RESID, 128), hidden)
    skp_part = dot(packed[:, OUT_AT:PACKED, 128:256].reshape(RESID, 128), hidden)
    prev = packed[:, 0:64, :].reshape(RESID, 256)
    now = packed[:, 64:128, :].reshape(RESID, 256)
    later = pltpu.roll(dot(prev, grad_pre[...]), wide - DILATION, 1)[:, :tokens]
    in_part = dot(now, grad_pre[:, :tokens]) + later
    for n, part in enumerate((res_part, skp_part, in_part)):
        for h in range(2):
            for r in range(8):
                natural[2 * n + h, pl.ds(r, 64, stride=8), :] = part[
                    64 * r : 64 * r + 64, 128 * h : 128 * h + 128
                ]
    for k, out in enumerate((z0, z1, z2, z3)):
        for i in range(4):
            rows = pl.ds(pl.multiple_of(32 * (ch ^ (4 * k + i)), 32), 32)
            for n in range(3):
                for h in range(2):
                    out[i, 32 * n : 32 * n + 32, 128 * h : 128 * h + 128] = natural[
                        2 * n + h, rows, :
                    ].astype(BF16)


def finish_tokens(o0, o1, o2, o3, sig, res, residual, skipped, grad_in):
    j = lax.axis_index("chan") & 3
    for k, piece in enumerate((o0, o1, o2, o3)):
        cut = pl.ds(pl.multiple_of((j ^ k) * 256, 256), 256)
        residual[:, cut] = sig[:, cut].astype(F32) + piece[0:32, :].astype(F32)
        skipped[:, cut] = piece[32:64, :].astype(F32)
        grad_in[:, cut] = res[:, cut].astype(F32) + piece[64:96, :].astype(F32)


def update(owned, grads, master, first, second, *refs):
    outs, held, old, grad, sems = refs[:3], refs[3:6], (*refs[6:8], first), refs[8], refs[9]
    slots = grads.shape[1]
    rows = 8 * slots
    steps = 10
    parts = [slice(n * rows // steps, (n + 1) * rows // steps) for n in range(steps)]
    fetches = []
    for n, part in enumerate(parts):
        for m, source in enumerate((second, master)):
            fetch = pltpu.make_async_copy(
                source.at[part, :], old[m].at[part, :], sems.at[3 * steps + 2 * n + m]
            )
            fetch.start()
            fetches.append(fetch)
    for r in range(8):
        for z in range(4):
            got = grads[16 * (r // 4) + 4 * z + r % 4].astype(F32)
            for h in range(2):
                grad[2 * z + h, pl.ds(r, slots, stride=8), :] = got[:, 128 * h : 128 * h + 128]
    unbias = 1.0 / (1.0 - MOMENT_DECAY**STEP)
    copies = []
    for n, part in enumerate(parts):
        for m in range(2):
            fetches[2 * n + m].wait()
        old_s, old_m, old_f = (ref[part, :] for ref in old)
        new = jnp.concatenate([grad[t, part, :] for t in range(8)], 1)
        keep = n * (rows // steps) + iota((rows // steps, 1), 0) < 8 * owned[0:1, 0:1]
        first_new = MOMENT_DECAY * old_f + (1.0 - MOMENT_DECAY) * new
        second_new = MOMENT_DECAY * old_s + (1.0 - MOMENT_DECAY) * new * new
        first_hat = first_new * unbias
        second_hat = second_new * unbias
        root = second_hat * lax.rsqrt(second_hat)
        stepped = old_m - STEP_RATE * (
            first_hat * pl.reciprocal(root + EPSILON) + WEIGHT_DECAY * old_m
        )
        held[0][part, :] = jnp.where(keep, first_new, old_f)
        held[1][part, :] = jnp.where(keep, second_new, old_s)
        held[2][part, :] = jnp.where(keep, stepped, old_m)
        for m in range(3):
            copy = pltpu.make_async_copy(
                held[m].at[part, :], outs[m].at[part, :], sems.at[3 * n + m]
            )
            copy.start()
            copies.append(copy)
    for copy in copies:
        copy.wait()


BOTH = ("tm", "chan")


def swap(x, k):
    n = lax.axis_size("chan")
    return lax.ppermute(x, "chan", [(i, i ^ k) for i in range(n)])


def local(
    signal, mel_frames, speaker_ids, owners, master, first_moment, second_moment, res_cot, skip_cot
):
    slots_dev = master.shape[0]
    slots = 16 * slots_dev
    flat = (8 * slots_dev, GATES)
    sig, res, skp, mel = signal.T, res_cot.T, skip_cot.T, mel_frames.T
    own_row = owners.reshape(1, NBLK)
    share = [[16 * y + 4 * z + j for y in range(2) for j in range(4)] for z in range(4)]
    sds = jax.ShapeDtypeStruct
    dma = pltpu.SemaphoreType.DMA

    sent, acts, edges = call(
        begin,
        (sds((16, slots_dev, 256), BF16), sds((3, *sig.shape), BF16), sds((192, 128), BF16)),
        (HBM,) * 6,
        scratch=(
            pltpu.VMEM((8, 8 * slots_dev, 128), F32),
            pltpu.VMEM((16, slots_dev, 256), BF16),
            pltpu.SMEM(speaker_ids.shape, jnp.int32),
            dma((17,)),
        ),
        out_space=(HBM, VMEM, VMEM),
    )(speaker_ids, master.reshape(flat), sig, res, skp, mel)
    other = lax.ppermute(edges, "tm", [(0, 1), (1, 0)])
    piece = sds((PIECE, 256), BF16)
    o = call(pack_tokens, (piece,) * 4, (VMEM,) * 2, gflops=8)(acts, other)
    arrived = lax.all_to_all(sent, "chan", 0, 0, tiled=True)
    o = (o[0], swap(o[1], 1), swap(o[2], 2), swap(o[3], 3))
    mine = call(join, sds((400, 256), BF16), (VMEM,) * 4)(*o)
    p1, p2, p3 = (swap(mine, 4 * k) for k in (1, 2, 3))

    at_col, put, owned = call(
        functools.partial(place_blocks, slots_dev=slots_dev),
        (
            sds((PACKED, 128), jnp.int32),
            sds((slots, PACKED), BF16),
            sds((8, 128), jnp.int32),
        ),
        (SMEM, VMEM, VMEM),
    )(speaker_ids, own_row, other)
    arrived, _ = lax.optimization_barrier((arrived, mine))
    gathered = call(gather_blocks, sds((PACKED, 256), BF16), (VMEM, VMEM), gflops=8)(
        at_col, arrived.reshape(slots, 256)
    )
    packed = lax.all_gather(gathered, BOTH, axis_index_groups=share)
    rows = (4, PACKED, 256)
    turned = call(
        turn,
        (
            sds((256, 8 * TAPS), BF16),
            sds((256, RESID), BF16),
            sds((8, OUT_AT - TAPS, 384), BF16),
            sds((256, 384), F32),
        ),
        (SMEM,) + (VMEM,) * 3,
        gflops=8,
    )(speaker_ids, packed, mel, other)
    kept, given, hidden, grad_pre = call(
        layer,
        (sds(rows, F32), sds(rows, BF16), sds((128, 256), BF16), sds((256, 384), BF16)),
        (VMEM,) * 11,
        gflops=0,
        scratch=(
            pltpu.VMEM((8, TAPS, 384), BF16),
            pltpu.VMEM((RESID, 384), BF16),
            pltpu.VMEM((RESID, 384), BF16),
            pltpu.VMEM((7, RESID, 128), F32),
            pltpu.VMEM((400, 256), BF16),
        ),
    )(*turned, *o, p1, p2, p3)
    z0, z1, z2, z3 = call(
        outputs,
        (sds((4, 96, 256), BF16),) * 4,
        (VMEM,) * 3,
        gflops=0,
        scratch=(pltpu.VMEM((6, RESID, 128), F32),),
    )(packed, hidden, grad_pre)

    kept, _ = lax.optimization_barrier((kept, z0))
    n = lax.axis_size("chan")
    g = call(sum_cores, tuple(sds((PACKED, 256), t) for t in (F32, BF16, BF16, BF16)), (VMEM,) * 2)(kept, swap(given, 1))
    across = [(16 * y + i, 16 * (1 - y) + (i ^ 2)) for y in range(2) for i in range(n)]
    g = (g[0], swap(g[1], 2), lax.ppermute(g[2], "tm", [(0, 1), (1, 0)]), lax.ppermute(g[3], BOTH, across))
    t1, t2, t3 = (swap(z, 4 * k) for k, z in ((1, z1), (2, z2), (3, z3)))
    spread = call(
        scatter_blocks,
        sds((2, slots, 256), BF16),
        (VMEM,) * 5,
        scratch=(pltpu.VMEM((slots, 256), BF16), dma((4,))),
        out_space=HBM,
    )(put, *g)
    returned = lax.all_to_all(spread.reshape(32, slots_dev, 256), BOTH, 0, 0)
    o = call(sum_units, (sds((96, 256), BF16),) * 4, (VMEM,) * 4, gflops=20)(z0, t1, t2, t3)
    o = (o[0], swap(o[1], 1), swap(o[2], 2), swap(o[3], 3))
    narrow = sds(sig.shape, F32)
    residual, skipped, grad_in = call(finish_tokens, (narrow,) * 3, (VMEM,) * 6)(*o, sig, res)
    new = call(
        update,
        (sds(flat, F32),) * 3,
        (VMEM, VMEM, HBM, VMEM, HBM),
        scratch=(pltpu.VMEM(flat, F32),) * 5
        + (pltpu.VMEM((8, flat[0], 128), F32), dma((50,))),
        out_space=HBM,
    )(
        owned,
        returned,
        master.reshape(flat),
        first_moment.reshape(flat),
        second_moment.reshape(flat),
    )
    return (residual.T, skipped.T, grad_in.T, *(x.reshape(master.shape) for x in new))


def place_index(owners, slots_dev):
    count = owners.shape[0]
    matches = owners[:, None] == owners[None, :]
    before = jnp.arange(count)[None, :] < jnp.arange(count)[:, None]
    ranks = jnp.sum((matches & before).astype(jnp.int32), axis=1)
    return owners * slots_dev + ranks


def local_plain(
    signal, mel_frames, speaker_ids, owners, master, first_moment, second_moment, res_cot, skip_cot
):
    chans = lax.axis_size("chan")
    slots_dev = master.shape[0]
    tok_count = signal.shape[0]
    hid_local = HIDDEN_SIZE // chans
    col_count = GATES // chans
    seg_count = speaker_ids.shape[0]
    spk_start = 2 * RESID + MELS
    out_start = spk_start + SPEAKERS
    places = place_index(owners, slots_dev)
    table = places[:, None] == jnp.arange(chans * slots_dev)[None, :]
    received = lax.all_to_all(
        master.astype(BF16), "chan", split_axis=2, concat_axis=0, tiled=True
    ).reshape(chans * slots_dev, BLOCK * col_count)
    params = jnp.dot(table.astype(BF16), received, preferred_element_type=F32)
    params = params.astype(BF16).reshape(ROWS, col_count)
    tap_prev, tap_now = params[:RESID], params[RESID : 2 * RESID]
    mel_proj = params[2 * RESID : spk_start]
    speaker_table = params[spk_start:out_start]
    out_cols = params[out_start:].reshape(RESID, hid_local, 2)
    n_tm = lax.axis_size("tm")
    tail_prev = lax.ppermute(signal[-DILATION:], "tm", [(i, i + 1) for i in range(n_tm - 1)])
    inputs = lax.all_gather(signal, "chan", axis=1, tiled=True)
    tail_full = lax.all_gather(tail_prev, "chan", axis=1, tiled=True)
    shifted = jnp.concatenate([tail_full, inputs[:-DILATION]], 0)
    pre_act = jnp.dot(shifted, tap_prev, preferred_element_type=F32)
    pre_act = pre_act + jnp.dot(inputs, tap_now, preferred_element_type=F32)
    pre_act = pre_act + jnp.dot(mel_frames, mel_proj, preferred_element_type=F32)
    one_hot = (speaker_ids[:, None] == jnp.arange(SPEAKERS)[None, :]).astype(BF16)
    embedded = jnp.dot(one_hot, speaker_table, preferred_element_type=F32)
    pre_act = (pre_act.reshape(seg_count, SEG, col_count) + embedded[:, None, :]).reshape(
        tok_count, col_count
    )
    filt = jnp.tanh(pre_act[:, 0::2])
    gates = jax.nn.sigmoid(pre_act[:, 1::2])
    hidden = (filt * gates).astype(BF16)
    summed = lax.psum_scatter(
        jnp.einsum("cuw,tu->cwt", out_cols, hidden, preferred_element_type=F32),
        "chan",
        scatter_dimension=0,
        tiled=True,
    )
    cots = lax.all_gather(
        jnp.stack([res_cot.T, skip_cot.T], axis=1), "chan", axis=0, tiled=True
    )
    grad_hid = jnp.einsum("cwt,cuw->tu", cots, out_cols, preferred_element_type=F32)
    term = jnp.einsum("cwt,tu->cuw", cots, hidden, preferred_element_type=F32)
    grad_filt = grad_hid * gates * (1.0 - filt * filt)
    grad_gate = grad_hid * filt * gates * (1.0 - gates)
    grad_pre = (
        jnp.stack([grad_filt, grad_gate], axis=2).reshape(tok_count, col_count).astype(BF16)
    )
    ahead = lax.ppermute(grad_pre[:DILATION], "tm", [(i + 1, i) for i in range(n_tm - 1)])
    later = jnp.concatenate([grad_pre[DILATION:], ahead], 0)
    input_part = lax.psum_scatter(
        dot(tap_now, grad_pre, NT) + dot(tap_prev, later, NT),
        "chan",
        scatter_dimension=0,
        tiled=True,
    )
    seg_sums = jnp.sum(grad_pre.astype(F32).reshape(seg_count, SEG, col_count), axis=1)
    grad_spk = lax.dot_general(
        one_hot.astype(F32),
        seg_sums,
        TN,
        precision=lax.Precision.HIGHEST,
        preferred_element_type=F32,
    )
    grad_params = jnp.concatenate(
        [
            dot(shifted, grad_pre, TN),
            dot(inputs, grad_pre, TN),
            dot(mel_frames, grad_pre, TN),
            grad_spk,
            term.reshape(RESID, col_count),
        ],
        0,
    )
    grad_params = lax.psum(grad_params, "tm").reshape(NBLK, BLOCK * col_count)
    outgoing = lax.dot_general(
        table.astype(F32), grad_params, TN, precision=lax.Precision.HIGHEST
    ).reshape(chans * slots_dev, BLOCK, col_count)
    grad_slots = lax.all_to_all(outgoing, "chan", split_axis=0, concat_axis=2, tiled=True)
    owned = jnp.sum((owners == lax.axis_index("chan")).astype(jnp.int32))
    keep = (jnp.arange(slots_dev) < owned)[:, None, None]
    first_new = MOMENT_DECAY * first_moment + (1.0 - MOMENT_DECAY) * grad_slots
    second_new = MOMENT_DECAY * second_moment + (1.0 - MOMENT_DECAY) * grad_slots * grad_slots
    first_hat = first_new / (1.0 - MOMENT_DECAY**STEP)
    second_hat = second_new / (1.0 - MOMENT_DECAY**STEP)
    stepped = master - STEP_RATE * (
        first_hat / (jnp.sqrt(second_hat) + EPSILON) + WEIGHT_DECAY * master
    )
    return (
        signal.astype(F32) + summed[:, 0, :].T,
        summed[:, 1, :].T,
        res_cot.astype(F32) + input_part.T,
        jnp.where(keep, first_new, first_moment),
        jnp.where(keep, second_new, second_moment),
        jnp.where(keep, stepped, master),
    )


def solution(mesh):
    wide = P("tm", "chan")
    slots = P("chan", None, None)
    packed_mesh = mesh.shape["tm"] == 2 and mesh.shape["chan"] == 16
    return jax.shard_map(
        local if packed_mesh else local_plain,
        mesh=mesh,
        in_specs=(wide, P("tm", None), P("tm"), P(), slots, slots, slots, wide, wide),
        out_specs=(wide, wide, wide, slots, slots, slots),
        check_vma=False,
    )
```
